32 devices in a mesh: dp: 8 (over z, x), blk: 4 (over y, core).
Axes of the slice: x: 2, y: 2, z: 4, core: 2. Of those that a mesh axis runs over, the one named last changes fastest.
Arguments:
- tokens: bfloat16 [8, 2048, 768], P('dp', 'blk'), may hold values from -6 to 6
- cotangent: bfloat16 [8, 2048, 768], P('dp', 'blk'), may hold values from -6 to 6
- lengths: int32 [8, 4], P('dp'), may hold values from 64 to 1856, as said below
- ln1_gain: bfloat16 [768], replicated, may hold values from 0.5 to 1.5
- ln1_bias: bfloat16 [768], replicated, may hold values from -1 to 1
- ln2_gain: bfloat16 [768], replicated, may hold values from 0.5 to 1.5
- ln2_bias: bfloat16 [768], replicated, may hold values from -1 to 1
- w_qkv: bfloat16 [768, 2304], replicated, may hold values from -0.21875 to 0.21875
- b_qkv: bfloat16 [2304], replicated, may hold values from -1 to 1
- w_out_attn: bfloat16 [768, 768], replicated, may hold values from -3 to 3
- b_out_attn: bfloat16 [768], replicated, may hold values from -1 to 1
- w_in: bfloat16 [768, 3072], replicated, may hold values from -0.21875 to 0.21875
- b_in: bfloat16 [3072], replicated, may hold values from -1 to 1
- w_out: bfloat16 [3072, 768], replicated, may hold values from -0.109375 to 0.109375
- b_out: bfloat16 [768], replicated, may hold values from -1 to 1
Outputs:
- layer_out: bfloat16 [8, 2048, 768], P('dp', 'blk')
- tokens_grad: bfloat16 [8, 2048, 768], P('dp', 'blk')
- ln1_gain_grad: float32 [768], P(('dp', 'blk'))
- ln1_bias_grad: float32 [768], P(('dp', 'blk'))
- ln2_gain_grad: float32 [768], P(('dp', 'blk'))
- ln2_bias_grad: float32 [768], P(('dp', 'blk'))
- w_qkv_grad: float32 [768, 2304], P(('dp', 'blk'))
- b_qkv_grad: float32 [2304], P(('dp', 'blk'))
- w_out_attn_grad: float32 [768, 768], P(('dp', 'blk'))
- b_out_attn_grad: float32 [768], P(('dp', 'blk'))
- w_in_grad: float32 [768, 3072], P(('dp', 'blk'))
- b_in_grad: float32 [3072], P(('dp', 'blk'))
- w_out_grad: float32 [3072, 768], P(('dp', 'blk'))
- b_out_grad: float32 [768], P(('dp', 'blk'))
- doc_norms: float32 [8, 4], P('dp')
The draws below stay inside these ranges and needn't reach their ends.
Inputs may be any that keep to these rules, and one draw needn't show every extreme that they name: Each row has 4 documents in order; one of them, chosen by the seed, begins within the first 512 tokens of the row and ends within the last 512; every other document has max(1, 64) to max(1, 128) tokens, and the one right after the long document (the first one if the long one is last) has exactly max(1, 64); the lengths of a row sum to 2048.
All inputs are finite; a program needn't handle non-finite values.
Results may differ from the reference program's by a relative error of at most 0.0095.
Values may be sent and summed in bfloat16 or wider, within the bound.
No kernel may reach another device: no remote copies, remote signals or barrier semaphores. Data moves between devices by JAX's collectives and lax.ppermute only.
A program may use at most 512 MiB of HBM per device.

```python
import math
import jax
import jax.numpy as jnp
from jax import lax

D = 768
HEADS = 12
HEAD = 64
FF = 3072
ROT = 16
DOCS = 4
TOK_DEV = 512
ROW_LEN = 2048
ROWS = 8


def draw_lengths(key, part):
    key = jax.random.fold_in(key, 11)
    pick_key, size_key = jax.random.split(key)
    least = max(1, TOK_DEV // 8)
    longest = jax.random.randint(pick_key, (ROWS, 1), 0, DOCS)
    shorts = jax.random.randint(size_key, (ROWS, DOCS), least, max(least, TOK_DEV // 4) + 1)
    doc_index = jnp.arange(DOCS)[None, :]
    is_long = doc_index == longest
    is_least = doc_index == (longest + 1) % DOCS
    shorts = jnp.where(is_least, least, shorts)
    others = jnp.sum(jnp.where(is_long, 0, shorts), axis=1, keepdims=True)
    return jnp.where(is_long, ROW_LEN - others, shorts).astype(jnp.int32)


def block_levels(own_key, extent, shards, smallest, top_value):
    def one(dim, blocks):
        draws = jax.random.uniform(jax.random.fold_in(jax.random.fold_in(own_key, 6), dim), (blocks,), jnp.float32, smallest / len(shards), top_value / len(shards))
        return jnp.repeat(jnp.exp(draws), extent[dim] // blocks).reshape((-1,) + (1,) * (len(extent) - dim - 1))

    level = one(*shards[0])
    for cut in shards[1:]:
        level = level * one(*cut)
    return level


def noise(stream_key, dims, spread, reach, pieces=(), held_as=jnp.bfloat16):
    loudness = block_levels(stream_key, dims, pieces, -0.22, 0.18) if pieces else 1.0
    drawn = jax.random.normal(stream_key, dims, jnp.float32) * spread * loudness
    return jnp.minimum(jnp.maximum(drawn, -reach), reach).astype(held_as)


def setup_inputs(seed: int = 0) -> dict:
    seeds = jax.random.split(jax.random.key(seed), 16)
    tokens = noise(seeds[0], (ROWS, ROW_LEN, D), 1.0, 6.0, ((0, 8), (1, 4)))
    cotangent = noise(seeds[1], (ROWS, ROW_LEN, D), 1.0, 6.0, ((0, 8), (1, 4)))
    lengths = draw_lengths(jax.random.fold_in(seeds[15], 71), 0)
    ln1_gain = jnp.clip(1.0 + 0.1 * jax.random.normal(seeds[3], (D,), jnp.float32), 0.5, 1.5).astype(jnp.bfloat16)
    ln1_bias = noise(seeds[4], (D,), 0.2, 1.0)
    ln2_gain = jnp.clip(1.0 + 0.1 * jax.random.normal(seeds[5], (D,), jnp.float32), 0.5, 1.5).astype(jnp.bfloat16)
    ln2_bias = noise(seeds[6], (D,), 0.2, 1.0)
    w_qkv = noise(seeds[7], (D, 3 * D), D ** -0.5, 0.21875)
    b_qkv = noise(seeds[8], (3 * D,), 0.2, 1.0)
    w_out_attn = noise(seeds[9], (D, D), 4 ** -0.5, 3.0)
    b_out_attn = noise(seeds[10], (D,), 0.2, 1.0)
    w_in = noise(seeds[11], (D, FF), D ** -0.5, 0.21875)
    b_in = noise(seeds[12], (FF,), 0.2, 1.0)
    w_out = noise(seeds[13], (FF, D), FF ** -0.5, 0.109375)
    b_out = noise(seeds[14], (D,), 0.2, 1.0)
    return {"tokens": tokens, "cotangent": cotangent, "lengths": lengths, "ln1_gain": ln1_gain, "ln1_bias": ln1_bias, "ln2_gain": ln2_gain, "ln2_bias": ln2_bias, "w_qkv": w_qkv, "b_qkv": b_qkv, "w_out_attn": w_out_attn, "b_out_attn": b_out_attn, "w_in": w_in, "b_in": b_in, "w_out": w_out, "b_out": b_out}


@jax.custom_vjp
def low(v):
    return lax.optimization_barrier(v.astype(jnp.bfloat16)).astype(jnp.float32)

@jax.custom_vjp
def low_back(v):
    return v

def low_keep(v):
    return (low(v), None)

def low_pass(kept, grad):
    return (grad,)

def back_keep(v):
    return (v, None)

def back_low(kept, grad):
    return (low(grad),)
low.defvjp(low_keep, low_pass)
low_back.defvjp(back_keep, back_low)
epsilon = 1e-05

def layer_norm(value, gain, shift):
    mean = lax.optimization_barrier(jnp.mean(value, axis=-1, keepdims=True))
    centered = value - mean
    variance = lax.optimization_barrier(jnp.mean(centered * centered, axis=-1, keepdims=True))
    return centered * lax.rsqrt(variance + epsilon) * gain + shift

def rotate(value, cosine, sine):
    half = ROT // 2
    rotary_part = value[..., :ROT]
    first = rotary_part[..., :half]
    second = rotary_part[..., half:]
    turned = jnp.concatenate([-second, first], axis=-1)
    return jnp.concatenate([rotary_part * cosine + turned * sine, value[..., ROT:]], axis=-1)

def forward(row_tokens, parameters, document, cosine, sine):
    highest = lax.Precision.HIGHEST
    ln1_gain, ln1_bias, ln2_gain, ln2_bias, w_qkv, b_qkv, w_out_attn, b_out_attn, w_in, b_in, w_out, b_out = parameters
    length = row_tokens.shape[0]
    normed_one = low(layer_norm(row_tokens, ln1_gain, ln1_bias))
    projected = low_back(jnp.dot(normed_one, w_qkv, precision=highest) + b_qkv)
    queries = projected[:, :D].reshape(length, HEADS, HEAD)
    keys = projected[:, D:2 * D].reshape(length, HEADS, HEAD)
    values = low(projected[:, 2 * D:].reshape(length, HEADS, HEAD))
    queries = low(rotate(queries, cosine, sine))
    keys = low(rotate(keys, cosine, sine))
    block_rows = math.gcd(length, 512)
    block_count = length // block_rows
    key_positions = jnp.arange(length, dtype=jnp.int32)

    def attend(block_index):
        first_row = block_index * block_rows
        query_block = lax.dynamic_slice_in_dim(queries, first_row, block_rows, 0)
        query_docs = lax.dynamic_slice_in_dim(document, first_row, block_rows, 0)
        query_positions = first_row + jnp.arange(block_rows, dtype=jnp.int32)
        scores = jnp.einsum('qhd,khd->hqk', query_block, keys, precision=highest) * HEAD ** (-0.5)
        allowed = (query_docs[:, None] == document[None, :]) & (key_positions[None, :] <= query_positions[:, None])
        scores = low_back(jnp.where(allowed[None], scores, -1e+30))
        weights = jax.nn.softmax(scores, axis=-1)
        return jnp.einsum('hqk,khd->qhd', low(weights), values, precision=highest)
    attended = lax.map(jax.checkpoint(attend), jnp.arange(block_count, dtype=jnp.int32))
    attended = low(low_back(attended.reshape(length, D)))
    attn_branch = jnp.dot(attended, w_out_attn, precision=highest) + b_out_attn
    normed_two = low(layer_norm(row_tokens, ln2_gain, ln2_bias))
    hidden = low_back(jnp.dot(normed_two, w_in, precision=highest) + b_in)
    activated = low(jax.nn.gelu(hidden, approximate=False))
    mlp_branch = jnp.dot(activated, w_out, precision=highest) + b_out
    return row_tokens + low_back(attn_branch + mlp_branch)

def reference(tokens, cotangent, lengths, ln1_gain, ln1_bias, ln2_gain, ln2_bias, w_qkv, b_qkv, w_out_attn, b_out_attn, w_in, b_in, w_out, b_out):
    parameters = tuple((value.astype(jnp.float32) for value in (ln1_gain, ln1_bias, ln2_gain, ln2_bias, w_qkv, b_qkv, w_out_attn, b_out_attn, w_in, b_in, w_out, b_out)))
    positions = jnp.arange(ROW_LEN, dtype=jnp.int32)
    half = ROT // 2
    frequency = 10000.0 ** (-(jnp.arange(half, dtype=jnp.float32) * 2.0) / ROT)
    angle = positions.astype(jnp.float32)[:, None] * frequency[None, :]
    cosine = jnp.concatenate([jnp.cos(angle), jnp.cos(angle)], axis=-1)[:, None, :]
    sine = jnp.concatenate([jnp.sin(angle), jnp.sin(angle)], axis=-1)[:, None, :]

    def one_row(running, row):
        row_tokens, row_cotangent, row_lengths = row
        ends = jnp.cumsum(row_lengths).astype(jnp.int32)
        document = lax.optimization_barrier(jnp.sum((positions[:, None] >= ends[None, :]).astype(jnp.int32), axis=1))
        member = (document[:, None] == jnp.arange(DOCS, dtype=jnp.int32)[None, :]).astype(jnp.float32)
        token_length = lax.optimization_barrier(jnp.sum(member * row_lengths.astype(jnp.float32)[None, :], axis=1))
        weight = jnp.sqrt(TOK_DEV / token_length)
        row_input = row_tokens.astype(jnp.float32)
        result, pullback = jax.vjp(lambda inputs, params_in: forward(inputs, params_in, document, cosine, sine), row_input, parameters)
        input_grad, param_grads = pullback(row_cotangent.astype(jnp.float32) * weight[:, None])
        squares = lax.optimization_barrier(jnp.sum(input_grad * input_grad, axis=1))
        norms = lax.optimization_barrier(jnp.sum(member * squares[:, None], axis=0)) * (row_lengths.astype(jnp.float32) / TOK_DEV)
        running = tuple((left + right for left, right in zip(running, param_grads)))
        return (running, (result.astype(jnp.bfloat16), input_grad.astype(jnp.bfloat16), norms))
    zeros = tuple((jnp.zeros_like(value) for value in parameters))
    summed, (results, input_grads, norms) = lax.scan(one_row, zeros, (tokens, cotangent, lengths))
    return (results, input_grads, summed[0], summed[1], summed[2], summed[3], summed[4], summed[5], summed[6], summed[7], summed[8], summed[9], summed[10], summed[11], norms)
```

```python
import jax
import jax.numpy as jnp
from jax import lax
from jax.experimental import pallas as pl
from jax.experimental.pallas import tpu as pltpu
from jax.sharding import PartitionSpec as P

HEADS = 12
HEAD = 64
ROT = 16
DOCS = 4
TOK_DEV = 512


epsilon = 1e-05


def layer_norm(value, gain, shift):
    mean = jnp.mean(value, axis=-1, keepdims=True)
    centered = value - mean
    variance = jnp.mean(centered * centered, axis=-1, keepdims=True)
    return centered * lax.rsqrt(variance + epsilon) * gain + shift


def rotate(value, cosine, sine):
    half = ROT // 2
    rotary_part = value[..., :ROT]
    first = rotary_part[..., :half]
    second = rotary_part[..., half:]
    turned = jnp.concatenate([-second, first], axis=-1)
    return jnp.concatenate([rotary_part * cosine + turned * sine, value[..., ROT:]], axis=-1)


def document_of(positions, ends):
    return jnp.sum((positions[:, None] >= ends[None, :]).astype(jnp.int32), axis=1)


def inner(left, right):
    return lax.dot_general(
        left, right, (((0,), (0,)), ((), ())), preferred_element_type=jnp.float32
    )


def back_through(grad, weight_matrix):
    return lax.dot_general(
        grad, weight_matrix, (((1,), (1,)), ((), ())), preferred_element_type=jnp.float32
    )


def general_plan(
    tokens,
    cotangent,
    lengths,
    ln1_gain,
    ln1_bias,
    ln2_gain,
    ln2_bias,
    w_qkv,
    b_qkv,
    w_out_attn,
    b_out_attn,
    w_in,
    b_in,
    w_out,
    b_out,
):
    blocks = lax.axis_size("blk")
    block_here = lax.axis_index("blk")
    inputs = tokens[0].astype(jnp.float32)
    rows_here = inputs.shape[0]
    width = inputs.shape[1]
    scale = HEAD ** (-0.5)
    query_positions = block_here * rows_here + jnp.arange(rows_here, dtype=jnp.int32)
    row_lengths = lengths[0]
    ends = jnp.cumsum(row_lengths)
    doc_starts = ends - row_lengths
    query_docs = document_of(query_positions, ends)
    doc_numbers = jnp.arange(DOCS, dtype=jnp.int32)
    member = (query_docs[:, None] == doc_numbers[None, :]).astype(jnp.float32)
    earliest = jnp.sum(jnp.where(doc_numbers == query_docs[0], doc_starts, 0))
    last_query = query_positions[rows_here - 1]
    token_length = jnp.sum(member * row_lengths.astype(jnp.float32)[None, :], axis=1)
    weight = jnp.sqrt(TOK_DEV / token_length)
    half = ROT // 2
    frequency = 10000.0 ** (-(jnp.arange(half, dtype=jnp.float32) * 2.0) / ROT)
    angle = query_positions.astype(jnp.float32)[:, None] * frequency[None, :]
    cosine = jnp.concatenate([jnp.cos(angle), jnp.cos(angle)], axis=-1)[:, None, :]
    sine = jnp.concatenate([jnp.sin(angle), jnp.sin(angle)], axis=-1)[:, None, :]
    gain_one = ln1_gain.astype(jnp.float32)
    shift_one = ln1_bias.astype(jnp.float32)
    gain_two = ln2_gain.astype(jnp.float32)
    shift_two = ln2_bias.astype(jnp.float32)
    normed_one = layer_norm(inputs, gain_one, shift_one).astype(jnp.bfloat16)
    projected = jnp.dot(normed_one, w_qkv, preferred_element_type=jnp.float32) + b_qkv.astype(
        jnp.float32
    )
    query_raw = projected[:, :width].reshape(rows_here, HEADS, HEAD)
    key_raw = projected[:, width : 2 * width].reshape(rows_here, HEADS, HEAD)
    queries = rotate(query_raw, cosine, sine).astype(jnp.bfloat16)
    keys_rotated = rotate(key_raw, cosine, sine).reshape(rows_here, width)
    keys_values = jnp.concatenate([keys_rotated, projected[:, 2 * width :]], axis=1).astype(
        jnp.bfloat16
    )

    def useful(first_row, count):
        return (first_row <= last_query) & (first_row + count > earliest)

    def masked_scores(kv_piece, first_row):
        count = kv_piece.shape[0]
        key_block = kv_piece[:, :width].reshape(count, HEADS, HEAD)
        value_block = kv_piece[:, width:].reshape(count, HEADS, HEAD)
        key_positions = first_row + jnp.arange(count, dtype=jnp.int32)
        key_docs = document_of(key_positions, ends)
        allowed = (query_docs[:, None] == key_docs[None, :]) & (
            key_positions[None, :] <= query_positions[:, None]
        )
        scores = (
            jnp.einsum("qhd,khd->qhk", queries, key_block, preferred_element_type=jnp.float32)
            * scale
        )
        return (jnp.where(allowed[:, None, :], scores, -jnp.inf), key_block, value_block)

    initial = (
        jnp.full((rows_here, HEADS), -1e30, jnp.float32),
        jnp.zeros((rows_here, HEADS), jnp.float32),
        jnp.zeros((rows_here, HEADS, HEAD), jnp.float32),
    )
    kv_piece = lax.all_gather(keys_values, "blk", axis=0, tiled=True)
    first_row = jnp.int32(0)

    def fold_work(state):
        row_max, denominator, accum = state
        scores, key_block, value_block = masked_scores(kv_piece, first_row)
        new_max = jnp.maximum(row_max, jnp.max(scores, axis=-1))
        expo = jnp.exp(scores - new_max[..., None])
        denominator = jnp.sum(expo, axis=-1)
        accum = jnp.einsum(
            "qhk,khd->qhd",
            expo.astype(jnp.bfloat16),
            value_block,
            preferred_element_type=jnp.float32,
        )
        return (new_max, denominator, accum)

    row_max, denominator, accum = lax.cond(
        useful(first_row, kv_piece.shape[0]), fold_work, lambda state: state, initial
    )
    log_total = row_max + jnp.log(denominator)
    attended_full = accum / denominator[..., None]
    attended = attended_full.reshape(rows_here, width).astype(jnp.bfloat16)
    attn_branch = jnp.dot(
        attended, w_out_attn, preferred_element_type=jnp.float32
    ) + b_out_attn.astype(jnp.float32)
    normed_two = layer_norm(inputs, gain_two, shift_two).astype(jnp.bfloat16)
    hidden = jnp.dot(normed_two, w_in, preferred_element_type=jnp.float32) + b_in.astype(
        jnp.float32
    )
    activated = jax.nn.gelu(hidden, approximate=False).astype(jnp.bfloat16)
    mlp_branch = jnp.dot(activated, w_out, preferred_element_type=jnp.float32) + b_out.astype(
        jnp.float32
    )
    layer_out = (inputs + attn_branch + mlp_branch).astype(jnp.bfloat16)
    out_grad = cotangent[0].astype(jnp.float32) * weight[:, None]
    branch_grad = out_grad.astype(jnp.bfloat16)
    branch_bias_grad = jnp.sum(branch_grad.astype(jnp.float32), axis=0)
    w_out_grad = inner(activated, branch_grad)
    activated_grad = back_through(branch_grad, w_out)
    unused, gelu_back = jax.vjp(lambda value: jax.nn.gelu(value, approximate=False), hidden)
    hidden_grad = gelu_back(activated_grad)[0].astype(jnp.bfloat16)
    w_in_grad = inner(normed_two, hidden_grad)
    b_in_grad = jnp.sum(hidden_grad.astype(jnp.float32), axis=0)
    normed_two_grad = back_through(hidden_grad, w_in)
    unused, norm_two_back = jax.vjp(layer_norm, inputs, gain_two, shift_two)
    input_two, gain_two_grad, shift_two_grad = norm_two_back(normed_two_grad)
    w_out_attn_grad = inner(attended, branch_grad)
    attended_grad = (
        back_through(branch_grad, w_out_attn).astype(jnp.bfloat16).reshape(rows_here, HEADS, HEAD)
    )
    delta = jnp.sum(attended_grad.astype(jnp.float32) * attended_full, axis=-1)
    gathered = lax.all_gather(keys_values, "blk", axis=0, tiled=True)

    def pair_terms_of(scores, value_block, grad_side, lse_side, delta_side):
        weights = jnp.exp(scores - lse_side[..., None])
        weight_grad = jnp.einsum(
            "qhd,khd->qhk", grad_side, value_block, preferred_element_type=jnp.float32
        )
        score_grad = (weights * (weight_grad - delta_side[..., None])).astype(jnp.bfloat16)
        return (weights, score_grad)

    def block_back(query_grad, block_index):
        first_row = block_index * rows_here
        kv_piece = lax.dynamic_slice_in_dim(gathered, first_row, rows_here, 0)

        def block_work(query_grad):
            scores, key_block, value_block = masked_scores(kv_piece, first_row)
            weights, score_grad = pair_terms_of(
                scores, value_block, attended_grad, log_total, delta
            )
            query_grad = (
                query_grad
                + jnp.einsum(
                    "qhk,khd->qhd", score_grad, key_block, preferred_element_type=jnp.float32
                )
                * scale
            )
            key_grad = (
                jnp.einsum("qhk,qhd->khd", score_grad, queries, preferred_element_type=jnp.float32)
                * scale
            )
            value_grad = jnp.einsum(
                "qhk,qhd->khd",
                weights.astype(jnp.bfloat16),
                attended_grad,
                preferred_element_type=jnp.float32,
            )
            pair_grad = jnp.concatenate(
                [key_grad.reshape(rows_here, width), value_grad.reshape(rows_here, width)], axis=1
            )
            return (query_grad, pair_grad)

        def skipped(query_grad):
            return (query_grad, jnp.zeros((rows_here, 2 * width), jnp.float32))

        return lax.cond(useful(first_row, rows_here), block_work, skipped, query_grad)

    query_grad, pair_terms = lax.scan(
        block_back,
        jnp.zeros((rows_here, HEADS, HEAD), jnp.float32),
        jnp.arange(blocks, dtype=jnp.int32),
    )
    pair_grads = lax.psum_scatter(
        pair_terms.reshape(blocks * rows_here, 2 * width).astype(jnp.bfloat16),
        "blk",
        scatter_dimension=0,
        tiled=True,
    ).astype(jnp.float32)
    unused, rotate_back = jax.vjp(lambda value: rotate(value, cosine, sine), query_raw)
    query_raw_grad = rotate_back(query_grad)[0].reshape(rows_here, width)
    key_raw_grad = rotate_back(pair_grads[:, :width].reshape(rows_here, HEADS, HEAD))[0].reshape(
        rows_here, width
    )
    projected_grad = jnp.concatenate(
        [query_raw_grad, key_raw_grad, pair_grads[:, width:]], axis=1
    ).astype(jnp.bfloat16)
    w_qkv_grad = inner(normed_one, projected_grad)
    b_qkv_grad = jnp.sum(projected_grad.astype(jnp.float32), axis=0)
    normed_one_grad = back_through(projected_grad, w_qkv)
    unused, norm_one_back = jax.vjp(layer_norm, inputs, gain_one, shift_one)
    input_one, gain_one_grad, shift_one_grad = norm_one_back(normed_one_grad)
    input_grad = out_grad + input_one + input_two
    squares = jnp.sum(input_grad * input_grad, axis=1)
    doc_local = jnp.sum(member * squares[:, None], axis=0)
    doc_norms = lax.psum(doc_local, "blk") * (row_lengths.astype(jnp.float32) / TOK_DEV)
    summed = (
        lax.psum_scatter(gain_one_grad, ("dp", "blk"), scatter_dimension=0, tiled=True),
        lax.psum_scatter(shift_one_grad, ("dp", "blk"), scatter_dimension=0, tiled=True),
        lax.psum_scatter(gain_two_grad, ("dp", "blk"), scatter_dimension=0, tiled=True),
        lax.psum_scatter(shift_two_grad, ("dp", "blk"), scatter_dimension=0, tiled=True),
        lax.psum_scatter(w_qkv_grad, ("dp", "blk"), scatter_dimension=0, tiled=True),
        lax.psum_scatter(b_qkv_grad, ("dp", "blk"), scatter_dimension=0, tiled=True),
        lax.psum_scatter(w_out_attn_grad, ("dp", "blk"), scatter_dimension=0, tiled=True),
        lax.psum_scatter(branch_bias_grad, ("dp", "blk"), scatter_dimension=0, tiled=True),
        lax.psum_scatter(w_in_grad, ("dp", "blk"), scatter_dimension=0, tiled=True),
        lax.psum_scatter(b_in_grad, ("dp", "blk"), scatter_dimension=0, tiled=True),
        lax.psum_scatter(w_out_grad, ("dp", "blk"), scatter_dimension=0, tiled=True),
        lax.psum_scatter(branch_bias_grad, ("dp", "blk"), scatter_dimension=0, tiled=True),
    )
    return (
        layer_out[None],
        input_grad.astype(jnp.bfloat16)[None],
        summed[0],
        summed[1],
        summed[2],
        summed[3],
        summed[4],
        summed[5],
        summed[6],
        summed[7],
        summed[8],
        summed[9],
        summed[10],
        summed[11],
        doc_norms[None],
    )


NT = (((1,), (1,)), ((), ()))
TN = (((0,), (0,)), ((), ()))
NN = (((1,), (0,)), ((), ()))
F32 = jnp.float32
BF16 = jnp.bfloat16
MASKED = -1e30


def mxu(left, right, dims=NN):
    return lax.dot_general(left, right, dims, preferred_element_type=F32)


def project_kernel(place, x_ref, gain, shift, wt_ref, bias, cos_ref, sin_ref, qkv_ref, normed_ref):
    x = x_ref[...].astype(F32)
    normed = layer_norm(x, gain[...], shift[...]).astype(BF16)
    normed_ref[...] = normed.T
    out = mxu(wt_ref[...], normed, NT) + bias[...]
    cosine, sine = cos_ref[...], sin_ref[...]
    half = ROT // 2
    heads = qkv_ref.shape[0] // (3 * HEAD)
    rotated = [2 * HEAD * h for h in range(heads)]
    rotated += [2 * HEAD * heads + HEAD * h for h in range(heads)]
    qkv_ref[...] = out.astype(BF16)
    for row in rotated:
        first, second = out[row : row + half], out[row + half : row + ROT]
        turned = jnp.concatenate(
            [first * cosine - second * sine, second * cosine + first * sine], axis=0
        )
        qkv_ref[row : row + ROT, :] = turned.astype(BF16)


def project(place, x, gain, shift, wt, bias, cosine, sine, earlier):
    count, rows, width = x.shape
    features = wt.shape[0]
    total = cosine.shape[1]
    whole = lambda j, place: (0, 0)
    moved = lambda j, place: (0, place[j])
    in_specs = [
        pl.BlockSpec((None, rows, width), lambda j, place: (j, 0, 0)),
        pl.BlockSpec((1, width), whole),
        pl.BlockSpec((1, width), whole),
        pl.BlockSpec((features, width), whole),
        pl.BlockSpec((features, 1), whole),
        pl.BlockSpec((ROT // 2, rows), moved),
        pl.BlockSpec((ROT // 2, rows), moved),
    ]
    operands = [place, x, gain, shift, wt, bias, cosine, sine]
    aliases = {}
    kernel = project_kernel
    if earlier is not None:
        in_specs += [pl.BlockSpec(memory_space=pl.ANY)] * 2
        operands += list(earlier)
        aliases = {8: 0, 9: 1}

        def kernel(*refs):
            project_kernel(*refs[:8], *refs[10:])

    return pl.pallas_call(
        kernel,
        grid_spec=pltpu.PrefetchScalarGridSpec(
            num_scalar_prefetch=1,
            grid=(count,),
            in_specs=in_specs,
            out_specs=[
                pl.BlockSpec((features, rows), moved),
                pl.BlockSpec((width, rows), moved),
            ],
        ),
        out_shape=[
            jax.ShapeDtypeStruct((features, total), BF16),
            jax.ShapeDtypeStruct((width, total), BF16),
        ],
        input_output_aliases=aliases,
        compiler_params=pltpu.CompilerParams(vmem_limit_bytes=40 << 20),
        cost_estimate=pl.CostEstimate(
            flops=2 * count * rows * width * features,
            bytes_accessed=2 * count * rows * (2 * width + features) + 2 * features * width,
            transcendentals=0,
        ),
        name="project",
    )(*operands)


def mlp_kernel(
    core,
    x_ref,
    ct_ref,
    weight_ref,
    gain,
    shift,
    win_ref,
    bin_ref,
    wout_ref,
    branch_ref,
    term_ref,
    gin_ref,
    gout_ref,
    small_ref,
    bin_grad_ref,
    gin_acc,
    gout_acc,
    act_ref,
    hid_ref,
):
    step = pl.program_id(0)
    last = pl.num_programs(0) - 1
    hidden_size = win_ref.shape[1]
    chunk = min(256, hidden_size)

    @pl.when(step == 0)
    def _():
        small_ref[...] = jnp.zeros_like(small_ref)
        bin_grad_ref[...] = jnp.zeros_like(bin_grad_ref)

    x = x_ref[...].astype(F32)
    mean = jnp.mean(x, axis=-1, keepdims=True)
    centered = x - mean
    variance = jnp.mean(centered * centered, axis=-1, keepdims=True)
    scaled = centered * lax.rsqrt(variance + epsilon)
    normed = (scaled * gain[...] + shift[...]).astype(BF16)
    normed_t = normed.T
    branch_grad = (ct_ref[...].astype(F32) * weight_ref[...]).astype(BF16)
    for j in range(0, hidden_size, chunk):
        cols = slice(j, j + chunk)
        hidden = mxu(normed, win_ref[:, cols]) + bin_ref[:, cols]
        back = mxu(branch_grad, wout_ref[cols, :], NT)
        below = 0.5 + 0.5 * lax.erf(hidden * (0.5**0.5))
        bell = jnp.exp(hidden * hidden * -0.5) * 0.3989422804014327
        act_ref[:, cols] = (hidden * below).astype(BF16)
        hidden_grad = back * (below + hidden * bell)
        rounded = hidden_grad.astype(BF16)
        hid_ref[:, cols] = rounded
        bin_grad_ref[:, cols] += jnp.sum(rounded.astype(F32), axis=0, keepdims=True)
    activated = act_ref[...]
    hidden_grads = hid_ref[...]
    branch_ref[...] = mxu(activated, wout_ref[...]).astype(BF16)
    normed_grad = mxu(hidden_grads, win_ref[...], NT)
    term_ref[...] = (normed_grad * gain[...]).astype(BF16)
    small_ref[0:1, :] += jnp.sum(normed_grad * scaled, axis=0, keepdims=True)
    small_ref[1:2, :] += jnp.sum(normed_grad, axis=0, keepdims=True)
    out_term = mxu(activated, branch_grad, TN)
    in_term = mxu(normed_t, hidden_grads)

    @pl.when(step == 0)
    def _():
        gout_acc[...] = out_term
        gin_acc[...] = in_term

    @pl.when((step > 0) & (step < last))
    def _():
        gout_acc[...] += out_term
        gin_acc[...] += in_term

    @pl.when(step == last)
    def _():
        gout_ref[...] = (gout_acc[...] + out_term).astype(BF16)
        gin_ref[...] = (gin_acc[...] + in_term).astype(BF16)


def mlp(core, x, ct, weight, gain, shift, w_in, b_in, w_out, parts):
    tokens, width = x.shape
    hidden_size = w_in.shape[1] // parts
    tile = min(256, tokens)
    whole = lambda i, core: (0, 0)
    row = lambda i, core: (i, 0)
    return pl.pallas_call(
        mlp_kernel,
        grid_spec=pltpu.PrefetchScalarGridSpec(
            num_scalar_prefetch=1,
            grid=(tokens // tile,),
            in_specs=[
                pl.BlockSpec((tile, width), row),
                pl.BlockSpec((tile, width), row),
                pl.BlockSpec((tile, 1), row),
                pl.BlockSpec((1, width), whole),
                pl.BlockSpec((1, width), whole),
                pl.BlockSpec((width, hidden_size), lambda i, core: (0, core[0])),
                pl.BlockSpec((1, hidden_size), lambda i, core: (0, core[0])),
                pl.BlockSpec((hidden_size, width), lambda i, core: (core[0], 0)),
            ],
            out_specs=[
                pl.BlockSpec((tile, width), row),
                pl.BlockSpec((tile, width), row),
                pl.BlockSpec((width, hidden_size), whole),
                pl.BlockSpec((hidden_size, width), whole),
                pl.BlockSpec((8, width), whole),
                pl.BlockSpec((1, hidden_size), whole),
            ],
            scratch_shapes=[
                pltpu.VMEM((width, hidden_size), F32),
                pltpu.VMEM((hidden_size, width), F32),
                pltpu.VMEM((tile, hidden_size), BF16),
                pltpu.VMEM((tile, hidden_size), BF16),
            ],
        ),
        out_shape=[
            jax.ShapeDtypeStruct((tokens, width), BF16),
            jax.ShapeDtypeStruct((tokens, width), BF16),
            jax.ShapeDtypeStruct((width, hidden_size), BF16),
            jax.ShapeDtypeStruct((hidden_size, width), BF16),
            jax.ShapeDtypeStruct((8, width), F32),
            jax.ShapeDtypeStruct((1, hidden_size), F32),
        ],
        compiler_params=pltpu.CompilerParams(vmem_limit_bytes=56 << 20),
        cost_estimate=pl.CostEstimate(
            flops=12 * tokens * width * hidden_size,
            bytes_accessed=8 * tokens * width + 8 * width * hidden_size,
            transcendentals=2 * tokens * hidden_size,
        ),
        name="feed_forward",
    )(core, x, ct, weight, gain, shift, w_in, b_in, w_out)


def attend_kernel(
    kv_t_ref,
    q_t_ref,
    do_t_ref,
    start_ref,
    cos_ref,
    sin_ref,
    out_t_ref,
    dqo_ref,
    dkv_ref,
    kv_ref,
    s_ref,
    pd_ref,
    acc_ref,
    cos_row,
    sin_row,
):
    head, tile_index = pl.program_id(0), pl.program_id(1)
    tile = q_t_ref.shape[1]
    length = kv_t_ref.shape[1]
    half = ROT // 2
    scale = HEAD ** (-0.5)

    @pl.when((head == 0) & (tile_index == 0))
    def _():
        cosine, sine = cos_ref[...], sin_ref[...]
        ones = jnp.ones((2 * HEAD - ROT, length), F32)
        zeros = jnp.zeros((2 * HEAD - ROT, length), F32)
        cos_row[...] = jnp.concatenate([cosine, cosine, ones], axis=0).T
        sin_row[...] = jnp.concatenate([sine, -sine, zeros], axis=0).T

    @pl.when(tile_index == 0)
    def _():
        kv_ref[...] = kv_t_ref[...].T
        acc_ref[...] = jnp.zeros_like(acc_ref)

    q_t = q_t_ref[...] * jnp.asarray(scale, BF16)
    do_t = do_t_ref[...]
    blank = jnp.zeros((HEAD, tile), BF16)
    q_pad = jnp.concatenate([q_t, blank], axis=0)
    start = start_ref[...]
    first_query = tile_index * tile
    query = first_query + lax.broadcasted_iota(jnp.int32, (tile, tile), 1)
    key0 = lax.broadcasted_iota(jnp.int32, (tile, tile), 0)

    def run(width):
        chunks = width // tile
        top = jnp.full((1, tile), MASKED, F32)
        for k in range(chunks):
            rows = slice(k * tile, (k + 1) * tile)
            scores = mxu(kv_ref[rows, :], q_pad)
            key = key0 + k * tile
            allowed = key >= start
            if k >= chunks - 2:
                allowed = allowed & (key <= query)
            scores = jnp.where(allowed, scores, MASKED)
            s_ref[rows, :] = scores
            top = jnp.maximum(top, jnp.max(scores, axis=0, keepdims=True))
        total = jnp.zeros((1, tile), F32)
        for k in range(chunks):
            rows = slice(k * tile, (k + 1) * tile)
            expo = jnp.exp(s_ref[rows, :] - top)
            total = total + jnp.sum(expo, axis=0, keepdims=True)
            pd_ref[rows, :tile] = expo.astype(BF16)
        inverse = 1.0 / total
        out_t = mxu(kv_t_ref[HEAD:, :width], pd_ref[:width, :tile]) * inverse
        do_scaled = (do_t.astype(F32) * inverse).astype(BF16)
        delta = jnp.sum(do_scaled.astype(F32) * out_t, axis=0, keepdims=True)
        do_pad = jnp.concatenate([blank, do_scaled], axis=0)
        sides = jnp.concatenate([do_pad, jnp.concatenate([q_t, blank], axis=0)], axis=1).T
        for k in range(chunks):
            rows = slice(k * tile, (k + 1) * tile)
            weight_grad = mxu(kv_ref[rows, :], do_pad)
            score_grad = pd_ref[rows, :tile].astype(F32) * (weight_grad - delta)
            pd_ref[rows, tile:] = score_grad.astype(BF16)
            acc_ref[rows, :] += mxu(pd_ref[rows, :], sides)
        dq_t = mxu(kv_t_ref[:HEAD, :width], pd_ref[:width, tile:]) * scale
        cosine = cos_ref[:, pl.ds(first_query, tile)]
        sine = sin_ref[:, pl.ds(first_query, tile)]
        first, second = dq_t[:half], dq_t[half:ROT]
        joined = jnp.concatenate(
            [
                first * cosine + second * sine,
                second * cosine - first * sine,
                dq_t[ROT:],
                out_t,
            ],
            axis=0,
        )
        out_t_ref[...] = out_t.astype(BF16)
        dqo_ref[...] = joined.T.astype(BF16)

    tiles = length // tile
    for v in range(0, tiles, 2):

        @pl.when(tile_index // 2 == v // 2)
        def _(v=v):
            run((v + 2) * tile)

    @pl.when(tile_index == tiles - 1)
    def _():
        grads = acc_ref[...]
        lane = lax.broadcasted_iota(jnp.int32, grads.shape, 1)
        partner = jnp.where(
            lane < half,
            pltpu.roll(grads, 2 * HEAD - half, 1),
            pltpu.roll(grads, half, 1),
        )
        dkv_ref[...] = (grads * cos_row[...] + partner * sin_row[...]).astype(BF16)


def attend(qkv_t, do_t, start, cosine, sine):
    heads = do_t.shape[0] // HEAD
    length = qkv_t.shape[1]
    tile = min(256, length // 2)
    pairs = heads * length * length // 2
    whole = lambda h, i: (0, 0)
    return pl.pallas_call(
        attend_kernel,
        grid=(heads, length // tile),
        in_specs=[
            pl.BlockSpec((2 * HEAD, length), lambda h, i: (h, 0)),
            pl.BlockSpec((HEAD, tile), lambda h, i: (2 * heads + h, i)),
            pl.BlockSpec((HEAD, tile), lambda h, i: (h, i)),
            pl.BlockSpec((1, tile), lambda h, i: (0, i)),
            pl.BlockSpec((ROT // 2, length), whole),
            pl.BlockSpec((ROT // 2, length), whole),
        ],
        out_specs=[
            pl.BlockSpec((HEAD, tile), lambda h, i: (h, i)),
            pl.BlockSpec((tile, 2 * HEAD), lambda h, i: (i, h)),
            pl.BlockSpec((length, 2 * HEAD), lambda h, i: (0, h)),
        ],
        out_shape=[
            jax.ShapeDtypeStruct((heads * HEAD, length), BF16),
            jax.ShapeDtypeStruct((length, 2 * heads * HEAD), BF16),
            jax.ShapeDtypeStruct((length, 2 * heads * HEAD), BF16),
        ],
        scratch_shapes=[
            pltpu.VMEM((length, 2 * HEAD), BF16),
            pltpu.VMEM((length, tile), F32),
            pltpu.VMEM((length, 2 * tile), BF16),
            pltpu.VMEM((length, 2 * HEAD), F32),
            pltpu.VMEM((length, 2 * HEAD), F32),
            pltpu.VMEM((length, 2 * HEAD), F32),
        ],
        compiler_params=pltpu.CompilerParams(vmem_limit_bytes=48 << 20),
        cost_estimate=pl.CostEstimate(
            flops=12 * pairs * HEAD,
            bytes_accessed=2 * length * heads * HEAD * 9,
            transcendentals=pairs,
        ),
        name="attend",
    )(qkv_t, qkv_t, do_t, start, cosine, sine)


def flip(value, axis, bit):
    size = lax.axis_size(axis)
    return lax.ppermute(value, axis, [(i, i ^ (1 << bit)) for i in range(size)])


def pick(value, index, dim):
    return lax.dynamic_index_in_dim(value, index, dim, keepdims=False)


def halve(value, dim, axis, bit, mine, out=BF16):
    arrived = flip(pick(value, 1 - mine, dim), axis, bit)
    return (pick(value, mine, dim).astype(F32) + arrived.astype(F32)).astype(out)


def in_order(mine, index, other):
    return jnp.where(index == 0, jnp.stack([mine, other]), jnp.stack([other, mine]))


def head_plan(
    tokens,
    cotangent,
    lengths,
    ln1_gain,
    ln1_bias,
    ln2_gain,
    ln2_bias,
    w_qkv,
    b_qkv,
    w_out_attn,
    b_out_attn,
    w_in,
    b_in,
    w_out,
    b_out,
):
    dp_size = lax.axis_size("dp")
    dp_bits = dp_size.bit_length() - 1
    here = lax.axis_index("blk")
    pair, core = here // 2, here % 2
    group = 2 * core + pair
    row = lax.axis_index("dp")
    row_bit = [(row >> b) & 1 for b in range(dp_bits)]
    own = tokens[0]
    own_ct = cotangent[0]
    rows, width = own.shape
    length = 4 * rows
    near = 2 * rows
    heads = HEADS // 4
    span = heads * HEAD
    hidden_size = w_in.shape[1]

    own_x = own
    core_x = flip(own, "blk", 0)
    core_ct = flip(own_ct, "blk", 0)
    pair_x = flip(own, "blk", 1)
    far_x = flip(pair_x, "blk", 0)

    row_lengths = lengths[0]
    ends = jnp.cumsum(row_lengths)
    doc_starts = ends - row_lengths
    positions = jnp.arange(length, dtype=jnp.int32)
    docs = document_of(positions, ends)
    doc_numbers = jnp.arange(DOCS, dtype=jnp.int32)
    all_member = docs[:, None] == doc_numbers[None, :]
    start = jnp.sum(jnp.where(all_member, doc_starts[None, :], 0), axis=1)[None, :]
    token_length = jnp.sum(jnp.where(all_member, row_lengths[None, :], 0), axis=1).astype(F32)
    weight = jnp.sqrt(TOK_DEV / token_length)
    near_weight = lax.dynamic_slice_in_dim(weight, pair * near, near, 0)[:, None]
    own_weight = lax.dynamic_slice_in_dim(weight, here * rows, rows, 0)[:, None]
    member = (
        lax.dynamic_slice_in_dim(docs, here * rows, rows, 0)[:, None] == doc_numbers[None, :]
    ).astype(F32)
    half = ROT // 2
    frequency = 10000.0 ** (-(jnp.arange(half, dtype=F32) * 2.0) / ROT)
    angle = frequency[:, None] * positions.astype(F32)[None, :]
    cosine, sine = jnp.cos(angle), jnp.sin(angle)

    parts = lax.dynamic_slice(
        w_qkv.reshape(width, 3, 4, span), (0, 0, group, 0), (width, 3, 1, span)
    ).reshape(width, 3, span)
    bias_parts = lax.dynamic_slice(
        b_qkv.reshape(3, 4, span), (0, group, 0), (3, 1, span)
    ).reshape(3, heads, HEAD)
    by_head = parts.transpose(1, 2, 0).reshape(3, heads, HEAD, width)
    w_kv_t = jnp.stack([by_head[1], by_head[2]], axis=1).reshape(2 * span, width)
    wt = jnp.concatenate([w_kv_t, by_head[0].reshape(span, width)], axis=0)
    bias = jnp.concatenate(
        [
            jnp.stack([bias_parts[1], bias_parts[2]], axis=1).reshape(2 * span),
            bias_parts[0].reshape(span),
        ]
    ).astype(F32)[:, None]
    w_q_pad = jnp.pad(by_head[0], ((0, 0), (0, HEAD), (0, 0))).reshape(2 * span, width)
    gain_one, shift_one = ln1_gain.astype(F32)[None, :], ln1_bias.astype(F32)[None, :]
    gain_two, shift_two = ln2_gain.astype(F32)[None, :], ln2_bias.astype(F32)[None, :]

    near_x = in_order(own_x, core, core_x).reshape(near, width)
    near_ct = in_order(own_ct, core, core_ct).reshape(near, width)
    branch_grad = (near_ct.astype(F32) * near_weight).astype(BF16)

    w_rows = lax.dynamic_slice_in_dim(w_out_attn, core * 2 * span, 2 * span, 0)
    do_rows = mxu(w_rows, branch_grad, NT).astype(BF16).reshape(2, span, near)
    do_arrived = flip(pick(do_rows, 1 - pair, 0), "blk", 1)

    near_place = 2 * pair + jnp.arange(2, dtype=jnp.int32)
    first_half = project(
        near_place, near_x.reshape(2, rows, width), gain_one, shift_one, wt, bias, cosine, sine, None
    )

    core_index = core.astype(jnp.int32).reshape(1)
    branch, term_two, gin, gout, small_two, b_in_grad = mlp(
        core_index,
        near_x,
        near_ct,
        near_weight,
        gain_two,
        shift_two,
        w_in,
        b_in.astype(F32)[None, :],
        w_out,
        2,
    )

    far_pair = in_order(pair_x, core, far_x)
    far_place = 2 * (1 - pair) + jnp.arange(2, dtype=jnp.int32)
    qkv_t, normed_t = project(
        far_place, far_pair, gain_one, shift_one, wt, bias, cosine, sine, first_half
    )
    do_mine = pick(do_rows, pair, 0)
    do_t = jnp.where(
        pair == 0,
        jnp.concatenate([do_mine, do_arrived], axis=1),
        jnp.concatenate([do_arrived, do_mine], axis=1),
    )
    out_t, dqo, dkv = attend(qkv_t, do_t, start, cosine, sine)

    def rows_over_chips(value, fine):
        shape = (2,) * (dp_bits + 1) + (fine,) + value.shape[1:]
        return value.reshape(shape)

    def scatter(value, order, slot=None):
        names = ["dp%d" % b for b in reversed(range(dp_bits))] + ["pair"]
        for name in order:
            dim = names.index(name)
            names.pop(dim)
            if name == "pair":
                value = halve(value, dim, "blk", 1, pair)
            else:
                bit = int(name[2:])
                mine = row_bit[bit]
                if bit == dp_bits - 1 and slot is not None:
                    mine = mine ^ slot
                value = halve(value, dim, "dp", bit, mine)
        return value

    chunk = width // (4 * dp_size)
    gin_rows = scatter(
        gin.reshape((2,) * (dp_bits + 1) + (2 * chunk, hidden_size // 2)),
        ["dp%d" % b for b in range(dp_bits)] + ["pair"],
    )
    gin_rows = gin_rows.reshape(2, chunk, hidden_size // 2)
    w_in_grad = (
        in_order(pick(gin_rows, core, 0), core, flip(pick(gin_rows, 1 - core, 0), "blk", 0))
        .transpose(1, 0, 2)
        .reshape(chunk, hidden_size)
        .astype(F32)
    )

    def scatter_half_rows(value, fine, order):
        value = value.reshape((2,) * dp_bits + (2, fine, width))
        kept = pick(value, core, dp_bits)
        arrived = flip(pick(value, 1 - core, dp_bits), "blk", 0)
        both = jnp.stack([kept, arrived])
        return scatter(both, order, slot=core).astype(F32)

    w_out_grad = scatter_half_rows(
        gout, 4 * chunk, ["dp%d" % b for b in range(dp_bits)] + ["pair"]
    )

    halves = out_t.reshape(span, 2, near)
    out_arrived = flip(pick(halves, 1 - pair, 1), "blk", 1)
    attended = in_order(pick(halves, pair, 1), pair, out_arrived).reshape(2 * span, near)
    partial_out = mxu(attended, w_rows, TN) + branch.astype(F32)
    partial_out = partial_out.reshape(2, rows, width)
    out_other = flip(pick(partial_out, 1 - core, 0).astype(BF16), "blk", 0)
    layer_out = (
        own.astype(F32)
        + pick(partial_out, core, 0)
        + out_other.astype(F32)
        + (b_out_attn.astype(F32) + b_out.astype(F32))[None, :]
    ).astype(BF16)
    goa = mxu(attended, branch_grad).astype(BF16)
    w_out_attn_grad = scatter_half_rows(
        goa, chunk, ["dp%d" % b for b in range(dp_bits)] + ["pair"]
    )

    normed_grad = mxu(dkv, w_kv_t) + mxu(dqo, w_q_pad)
    term_one = (normed_grad * gain_one).reshape(2, 2, rows, width)
    far_term = pick(term_one, 1 - pair, 0)
    near_term = pick(term_one, pair, 0) + term_two.astype(F32).reshape(2, rows, width)
    far_sum = halve(far_term.astype(BF16), 0, "blk", 0, core)
    far_arrived = flip(far_sum, "blk", 1)
    near_sum = halve(near_term.astype(BF16), 0, "blk", 0, core, F32)
    term = near_sum + far_arrived.astype(F32)
    x = own.astype(F32)
    mean = jnp.mean(x, axis=-1, keepdims=True)
    centered = x - mean
    scale = lax.rsqrt(jnp.mean(centered * centered, axis=-1, keepdims=True) + epsilon)
    scaled = centered * scale
    back = scale * (
        term
        - jnp.mean(term, axis=-1, keepdims=True)
        - scaled * jnp.mean(term * scaled, axis=-1, keepdims=True)
    )
    out_grad = own_ct.astype(F32) * own_weight
    input_grad = out_grad + back
    squares = jnp.sum(input_grad * input_grad, axis=1)
    doc_local = jnp.sum(member * squares[:, None], axis=0)
    doc_norms = lax.psum(doc_local, "blk") * (row_lengths.astype(F32) / TOK_DEV)

    g_kv = mxu(normed_t, dkv).reshape(width, heads, 2, HEAD)
    g_q = mxu(normed_t, dqo).reshape(width, heads, 2, HEAD)[:, :, 0]
    g_qkv = jnp.stack([g_q, g_kv[:, :, 0], g_kv[:, :, 1]], axis=1).reshape(width, 3 * span)
    value = g_qkv.astype(BF16).reshape((2,) * dp_bits + (4 * chunk, 3 * span))
    names = list(reversed(range(dp_bits)))
    for bit in range(dp_bits):
        dim = names.index(bit)
        names.pop(dim)
        value = halve(value, dim, "dp", bit, row_bit[bit])
    value = value.reshape(2, 2, chunk, 3 * span)
    value = in_order(pick(value, pair, 0), pair, flip(pick(value, 1 - pair, 0), "blk", 1))
    value = in_order(
        pick(value, core, 1), core, flip(pick(value, 1 - core, 1), "blk", 0)
    )
    w_qkv_grad = (
        value.reshape(4, chunk, 3, span).transpose(1, 2, 0, 3).reshape(chunk, 3 * width).astype(F32)
    )

    kv_sum = jnp.sum(dkv.astype(F32), axis=0).reshape(heads, 2, HEAD)
    q_sum = jnp.sum(dqo.astype(F32), axis=0).reshape(heads, 2, HEAD)[:, 0]
    b_parts = jnp.stack([q_sum, kv_sum[:, 0], kv_sum[:, 1]]).reshape(3, span)
    w_flat = parts.astype(F32).reshape(width, 3 * span)
    shift_one_grad = jnp.sum(w_flat * b_parts.reshape(1, 3 * span), axis=1)
    gain_one_grad = (
        jnp.sum(w_flat * g_qkv, axis=1) - shift_one[0] * shift_one_grad
    ) / gain_one[0]
    b_qkv_full = lax.dynamic_update_slice(
        jnp.zeros((3, 4, span), F32), b_parts[:, None], (0, group, 0)
    )
    b_in_full = lax.dynamic_update_slice(
        jnp.zeros((2, hidden_size // 2), F32), b_in_grad, (core, 0)
    )
    own_branch_grad = pick(branch_grad.reshape(2, rows, width), core, 0)
    branch_bias = jnp.sum(own_branch_grad.astype(F32), axis=0)
    vectors = [
        gain_one_grad,
        shift_one_grad,
        small_two[0],
        small_two[1],
        b_qkv_full.reshape(-1),
        branch_bias,
        b_in_full.reshape(-1),
    ]
    devices = 4 * dp_size
    sizes = [v.shape[0] // devices for v in vectors]
    packed = jnp.concatenate([v.reshape(devices, -1) for v in vectors], axis=1)
    summed = jnp.sum(
        lax.all_to_all(packed, ("dp", "blk"), 0, 0, tiled=True), axis=0
    )
    pieces = []
    at = 0
    for size in sizes:
        pieces.append(summed[at : at + size])
        at += size
    return (
        layer_out[None],
        input_grad.astype(BF16)[None],
        pieces[0],
        pieces[1],
        pieces[2],
        pieces[3],
        w_qkv_grad,
        pieces[4],
        w_out_attn_grad,
        pieces[5],
        w_in_grad,
        pieces[6],
        w_out_grad,
        pieces[5],
        doc_norms[None],
    )


def solution(mesh):
    in_specs = (
        P("dp", "blk", None),
        P("dp", "blk", None),
        P("dp", None),
        P(),
        P(),
        P(),
        P(),
        P(),
        P(),
        P(),
        P(),
        P(),
        P(),
        P(),
        P(),
    )
    out_specs = (
        P("dp", "blk", None),
        P("dp", "blk", None),
        P(("dp", "blk")),
        P(("dp", "blk")),
        P(("dp", "blk")),
        P(("dp", "blk")),
        P(("dp", "blk"), None),
        P(("dp", "blk")),
        P(("dp", "blk"), None),
        P(("dp", "blk")),
        P(("dp", "blk"), None),
        P(("dp", "blk")),
        P(("dp", "blk"), None),
        P(("dp", "blk")),
        P("dp", None),
    )
    dp_size = mesh.shape["dp"]
    suits = mesh.shape["blk"] == 4 and HEADS % 4 == 0 and dp_size & (dp_size - 1) == 0
    plan = head_plan if suits else general_plan
    return jax.shard_map(
        plan, mesh=mesh, in_specs=in_specs, out_specs=out_specs, check_vma=False
    )
```

```python
import functools

import jax
import jax.numpy as jnp
import numpy as np
from jax import lax
from jax.experimental import pallas as pl
from jax.experimental.pallas import tpu as pltpu
from jax.sharding import PartitionSpec as P

HEADS = 12
HEAD = 64
ROT = 16
DOCS = 4
TOK_DEV = 512


epsilon = 1e-05


def layer_norm(value, gain, shift):
    mean = jnp.mean(value, axis=-1, keepdims=True)
    centered = value - mean
    variance = jnp.mean(centered * centered, axis=-1, keepdims=True)
    return centered * lax.rsqrt(variance + epsilon) * gain + shift


def rotate(value, cosine, sine):
    half = ROT // 2
    rotary_part = value[..., :ROT]
    first = rotary_part[..., :half]
    second = rotary_part[..., half:]
    turned = jnp.concatenate([-second, first], axis=-1)
    return jnp.concatenate([rotary_part * cosine + turned * sine, value[..., ROT:]], axis=-1)


def document_of(positions, ends):
    return jnp.sum((positions[:, None] >= ends[None, :]).astype(jnp.int32), axis=1)


def inner(left, right):
    return lax.dot_general(
        left, right, (((0,), (0,)), ((), ())), preferred_element_type=jnp.float32
    )


def back_through(grad, weight_matrix):
    return lax.dot_general(
        grad, weight_matrix, (((1,), (1,)), ((), ())), preferred_element_type=jnp.float32
    )


def general_plan(
    tokens,
    cotangent,
    lengths,
    ln1_gain,
    ln1_bias,
    ln2_gain,
    ln2_bias,
    w_qkv,
    b_qkv,
    w_out_attn,
    b_out_attn,
    w_in,
    b_in,
    w_out,
    b_out,
):
    blocks = lax.axis_size("blk")
    block_here = lax.axis_index("blk")
    inputs = tokens[0].astype(jnp.float32)
    rows_here = inputs.shape[0]
    width = inputs.shape[1]
    scale = HEAD ** (-0.5)
    query_positions = block_here * rows_here + jnp.arange(rows_here, dtype=jnp.int32)
    row_lengths = lengths[0]
    ends = jnp.cumsum(row_lengths)
    doc_starts = ends - row_lengths
    query_docs = document_of(query_positions, ends)
    doc_numbers = jnp.arange(DOCS, dtype=jnp.int32)
    member = (query_docs[:, None] == doc_numbers[None, :]).astype(jnp.float32)
    earliest = jnp.sum(jnp.where(doc_numbers == query_docs[0], doc_starts, 0))
    last_query = query_positions[rows_here - 1]
    token_length = jnp.sum(member * row_lengths.astype(jnp.float32)[None, :], axis=1)
    weight = jnp.sqrt(TOK_DEV / token_length)
    half = ROT // 2
    frequency = 10000.0 ** (-(jnp.arange(half, dtype=jnp.float32) * 2.0) / ROT)
    angle = query_positions.astype(jnp.float32)[:, None] * frequency[None, :]
    cosine = jnp.concatenate([jnp.cos(angle), jnp.cos(angle)], axis=-1)[:, None, :]
    sine = jnp.concatenate([jnp.sin(angle), jnp.sin(angle)], axis=-1)[:, None, :]
    gain_one = ln1_gain.astype(jnp.float32)
    shift_one = ln1_bias.astype(jnp.float32)
    gain_two = ln2_gain.astype(jnp.float32)
    shift_two = ln2_bias.astype(jnp.float32)
    normed_one = layer_norm(inputs, gain_one, shift_one).astype(jnp.bfloat16)
    projected = jnp.dot(normed_one, w_qkv, preferred_element_type=jnp.float32) + b_qkv.astype(
        jnp.float32
    )
    query_raw = projected[:, :width].reshape(rows_here, HEADS, HEAD)
    key_raw = projected[:, width : 2 * width].reshape(rows_here, HEADS, HEAD)
    queries = rotate(query_raw, cosine, sine).astype(jnp.bfloat16)
    keys_rotated = rotate(key_raw, cosine, sine).reshape(rows_here, width)
    keys_values = jnp.concatenate([keys_rotated, projected[:, 2 * width :]], axis=1).astype(
        jnp.bfloat16
    )

    def useful(first_row, count):
        return (first_row <= last_query) & (first_row + count > earliest)

    def masked_scores(kv_piece, first_row):
        count = kv_piece.shape[0]
        key_block = kv_piece[:, :width].reshape(count, HEADS, HEAD)
        value_block = kv_piece[:, width:].reshape(count, HEADS, HEAD)
        key_positions = first_row + jnp.arange(count, dtype=jnp.int32)
        key_docs = document_of(key_positions, ends)
        allowed = (query_docs[:, None] == key_docs[None, :]) & (
            key_positions[None, :] <= query_positions[:, None]
        )
        scores = (
            jnp.einsum("qhd,khd->qhk", queries, key_block, preferred_element_type=jnp.float32)
            * scale
        )
        return (jnp.where(allowed[:, None, :], scores, -jnp.inf), key_block, value_block)

    initial = (
        jnp.full((rows_here, HEADS), -1e30, jnp.float32),
        jnp.zeros((rows_here, HEADS), jnp.float32),
        jnp.zeros((rows_here, HEADS, HEAD), jnp.float32),
    )
    kv_piece = lax.all_gather(keys_values, "blk", axis=0, tiled=True)
    first_row = jnp.int32(0)

    def fold_work(state):
        row_max, denominator, accum = state
        scores, key_block, value_block = masked_scores(kv_piece, first_row)
        new_max = jnp.maximum(row_max, jnp.max(scores, axis=-1))
        expo = jnp.exp(scores - new_max[..., None])
        denominator = jnp.sum(expo, axis=-1)
        accum = jnp.einsum(
            "qhk,khd->qhd",
            expo.astype(jnp.bfloat16),
            value_block,
            preferred_element_type=jnp.float32,
        )
        return (new_max, denominator, accum)

    row_max, denominator, accum = lax.cond(
        useful(first_row, kv_piece.shape[0]), fold_work, lambda state: state, initial
    )
    log_total = row_max + jnp.log(denominator)
    attended_full = accum / denominator[..., None]
    attended = attended_full.reshape(rows_here, width).astype(jnp.bfloat16)
    attn_branch = jnp.dot(
        attended, w_out_attn, preferred_element_type=jnp.float32
    ) + b_out_attn.astype(jnp.float32)
    normed_two = layer_norm(inputs, gain_two, shift_two).astype(jnp.bfloat16)
    hidden = jnp.dot(normed_two, w_in, preferred_element_type=jnp.float32) + b_in.astype(
        jnp.float32
    )
    activated = jax.nn.gelu(hidden, approximate=False).astype(jnp.bfloat16)
    mlp_branch = jnp.dot(activated, w_out, preferred_element_type=jnp.float32) + b_out.astype(
        jnp.float32
    )
    layer_out = (inputs + attn_branch + mlp_branch).astype(jnp.bfloat16)
    out_grad = cotangent[0].astype(jnp.float32) * weight[:, None]
    branch_grad = out_grad.astype(jnp.bfloat16)
    branch_bias_grad = jnp.sum(branch_grad.astype(jnp.float32), axis=0)
    w_out_grad = inner(activated, branch_grad)
    activated_grad = back_through(branch_grad, w_out)
    unused, gelu_back = jax.vjp(lambda value: jax.nn.gelu(value, approximate=False), hidden)
    hidden_grad = gelu_back(activated_grad)[0].astype(jnp.bfloat16)
    w_in_grad = inner(normed_two, hidden_grad)
    b_in_grad = jnp.sum(hidden_grad.astype(jnp.float32), axis=0)
    normed_two_grad = back_through(hidden_grad, w_in)
    unused, norm_two_back = jax.vjp(layer_norm, inputs, gain_two, shift_two)
    input_two, gain_two_grad, shift_two_grad = norm_two_back(normed_two_grad)
    w_out_attn_grad = inner(attended, branch_grad)
    attended_grad = (
        back_through(branch_grad, w_out_attn).astype(jnp.bfloat16).reshape(rows_here, HEADS, HEAD)
    )
    delta = jnp.sum(attended_grad.astype(jnp.float32) * attended_full, axis=-1)
    gathered = lax.all_gather(keys_values, "blk", axis=0, tiled=True)

    def pair_terms_of(scores, value_block, grad_side, lse_side, delta_side):
        weights = jnp.exp(scores - lse_side[..., None])
        weight_grad = jnp.einsum(
            "qhd,khd->qhk", grad_side, value_block, preferred_element_type=jnp.float32
        )
        score_grad = (weights * (weight_grad - delta_side[..., None])).astype(jnp.bfloat16)
        return (weights, score_grad)

    def block_back(query_grad, block_index):
        first_row = block_index * rows_here
        kv_piece = lax.dynamic_slice_in_dim(gathered, first_row, rows_here, 0)

        def block_work(query_grad):
            scores, key_block, value_block = masked_scores(kv_piece, first_row)
            weights, score_grad = pair_terms_of(
                scores, value_block, attended_grad, log_total, delta
            )
            query_grad = (
                query_grad
                + jnp.einsum(
                    "qhk,khd->qhd", score_grad, key_block, preferred_element_type=jnp.float32
                )
                * scale
            )
            key_grad = (
                jnp.einsum("qhk,qhd->khd", score_grad, queries, preferred_element_type=jnp.float32)
                * scale
            )
            value_grad = jnp.einsum(
                "qhk,qhd->khd",
                weights.astype(jnp.bfloat16),
                attended_grad,
                preferred_element_type=jnp.float32,
            )
            pair_grad = jnp.concatenate(
                [key_grad.reshape(rows_here, width), value_grad.reshape(rows_here, width)], axis=1
            )
            return (query_grad, pair_grad)

        def skipped(query_grad):
            return (query_grad, jnp.zeros((rows_here, 2 * width), jnp.float32))

        return lax.cond(useful(first_row, rows_here), block_work, skipped, query_grad)

    query_grad, pair_terms = lax.scan(
        block_back,
        jnp.zeros((rows_here, HEADS, HEAD), jnp.float32),
        jnp.arange(blocks, dtype=jnp.int32),
    )
    pair_grads = lax.psum_scatter(
        pair_terms.reshape(blocks * rows_here, 2 * width).astype(jnp.bfloat16),
        "blk",
        scatter_dimension=0,
        tiled=True,
    ).astype(jnp.float32)
    unused, rotate_back = jax.vjp(lambda value: rotate(value, cosine, sine), query_raw)
    query_raw_grad = rotate_back(query_grad)[0].reshape(rows_here, width)
    key_raw_grad = rotate_back(pair_grads[:, :width].reshape(rows_here, HEADS, HEAD))[0].reshape(
        rows_here, width
    )
    projected_grad = jnp.concatenate(
        [query_raw_grad, key_raw_grad, pair_grads[:, width:]], axis=1
    ).astype(jnp.bfloat16)
    w_qkv_grad = inner(normed_one, projected_grad)
    b_qkv_grad = jnp.sum(projected_grad.astype(jnp.float32), axis=0)
    normed_one_grad = back_through(projected_grad, w_qkv)
    unused, norm_one_back = jax.vjp(layer_norm, inputs, gain_one, shift_one)
    input_one, gain_one_grad, shift_one_grad = norm_one_back(normed_one_grad)
    input_grad = out_grad + input_one + input_two
    squares = jnp.sum(input_grad * input_grad, axis=1)
    doc_local = jnp.sum(member * squares[:, None], axis=0)
    doc_norms = lax.psum(doc_local, "blk") * (row_lengths.astype(jnp.float32) / TOK_DEV)
    summed = (
        lax.psum_scatter(gain_one_grad, ("dp", "blk"), scatter_dimension=0, tiled=True),
        lax.psum_scatter(shift_one_grad, ("dp", "blk"), scatter_dimension=0, tiled=True),
        lax.psum_scatter(gain_two_grad, ("dp", "blk"), scatter_dimension=0, tiled=True),
        lax.psum_scatter(shift_two_grad, ("dp", "blk"), scatter_dimension=0, tiled=True),
        lax.psum_scatter(w_qkv_grad, ("dp", "blk"), scatter_dimension=0, tiled=True),
        lax.psum_scatter(b_qkv_grad, ("dp", "blk"), scatter_dimension=0, tiled=True),
        lax.psum_scatter(w_out_attn_grad, ("dp", "blk"), scatter_dimension=0, tiled=True),
        lax.psum_scatter(branch_bias_grad, ("dp", "blk"), scatter_dimension=0, tiled=True),
        lax.psum_scatter(w_in_grad, ("dp", "blk"), scatter_dimension=0, tiled=True),
        lax.psum_scatter(b_in_grad, ("dp", "blk"), scatter_dimension=0, tiled=True),
        lax.psum_scatter(w_out_grad, ("dp", "blk"), scatter_dimension=0, tiled=True),
        lax.psum_scatter(branch_bias_grad, ("dp", "blk"), scatter_dimension=0, tiled=True),
    )
    return (
        layer_out[None],
        input_grad.astype(jnp.bfloat16)[None],
        summed[0],
        summed[1],
        summed[2],
        summed[3],
        summed[4],
        summed[5],
        summed[6],
        summed[7],
        summed[8],
        summed[9],
        summed[10],
        summed[11],
        doc_norms[None],
    )


NT = (((1,), (1,)), ((), ()))
TN = (((0,), (0,)), ((), ()))
NN = (((1,), (0,)), ((), ()))
F32 = jnp.float32
BF16 = jnp.bfloat16
MASKED = -1e30
PEAK = 1.15e9
HALF = ROT // 2
EXTRA = 16
HERE, PAIR, CORE, GROUP, XBIT, ZLOW, ZHIGH, LENS = 0, 1, 2, 3, 4, 5, 6, 7


def mxu(left, right, dims=NN):
    return lax.dot_general(left, right, dims, preferred_element_type=F32)


def exact(left, right):
    return lax.dot_general(
        left, right, NN, precision=lax.Precision.HIGHEST, preferred_element_type=F32
    )


def row_of(ref):
    return ref[...].astype(F32).reshape(1, -1)


def token_weight(meta, pos):
    lens = [meta[LENS + d] for d in range(DOCS)]
    length = jnp.full(pos.shape, lens[DOCS - 1], jnp.int32)
    end = lens[0]
    ends = [end]
    for d in range(1, DOCS - 1):
        end = end + lens[d]
        ends.append(end)
    for d in reversed(range(DOCS - 1)):
        length = jnp.where(pos < ends[d], lens[d], length)
    return jnp.sqrt(TOK_DEV / length.astype(F32))


def doc_bounds(meta, length):
    ends = [meta[LENS]]
    for d in range(1, DOCS - 1):
        ends.append(ends[-1] + meta[LENS + d])
    return [0] + ends, ends + [length]


def column(first, count):
    return first + lax.broadcasted_iota(jnp.int32, (count, 1), 0)


def standard(x):
    mean = jnp.mean(x, axis=-1, keepdims=True)
    centered = x - mean
    variance = jnp.mean(centered * centered, axis=-1, keepdims=True)
    rate = lax.rsqrt(variance + epsilon)
    return centered * rate, rate


def call(kernel, name, meta, operands, outs, cost_us, scratch=(), vmem=6, after=(), hold=(), far=()):
    inside = pl.BlockSpec(memory_space=pltpu.VMEM)
    scalars = pl.BlockSpec(memory_space=pltpu.SMEM)
    used = 1 + len(operands)
    idle = len(after) + len(hold)

    def body(*refs):
        kernel(*refs[:used], *refs[used + idle :])

    return pl.pallas_call(
        body,
        in_specs=[scalars]
        + [pl.BlockSpec(memory_space=pl.ANY) if k in far else inside for k in range(len(operands))]
        + [inside] * len(hold)
        + [pl.BlockSpec(memory_space=pl.ANY)] * len(after),
        out_specs=[scalars if o.shape == (1,) else inside for o in outs],
        out_shape=outs,
        scratch_shapes=list(scratch),
        compiler_params=pltpu.CompilerParams(vmem_limit_bytes=vmem << 20),
        cost_estimate=cost(cost_us),
        name=name,
    )(meta, *operands, *hold, *after)


def cost(us):
    return pl.CostEstimate(flops=int(us * PEAK), bytes_accessed=0, transcendentals=0)


def shape(dims, dtype=BF16):
    return jax.ShapeDtypeStruct(tuple(dims), dtype)


def all_of(array):
    rank = array.ndim
    return pl.BlockSpec(array.shape, lambda *_: (0,) * rank)


def weights_kernel(meta, w_ref, b_ref, wt_ref, bias_ref, columns, row_ref, sems):
    span = wt_ref.shape[0] // 3
    width = wt_ref.shape[1]
    first = meta[GROUP] * span
    odd = (meta[GROUP] % 2) == 1

    def place(part):
        return pl.ds(pl.multiple_of(part * width + (first // 128) * 128, 128), 256)

    copies = [
        pltpu.make_async_copy(w_ref.at[:, place(part)], columns.at[part], sems.at[part]) for part in range(3)
    ]
    for copy in copies:
        copy.start()
    row_ref[...] = row_of(b_ref)
    for copy in copies:
        copy.wait()

    def rows(part, bias):
        both = (jnp.broadcast_to(row_ref[:, place(part)], (8, 256)) if bias else columns[part]).T
        return jnp.where(odd, both[HEAD : HEAD + span], both[:span])

    for out, bias in ((wt_ref, False), (bias_ref, True)):
        queries, keys, values = (rows(part, bias) for part in range(3))
        pieces = []
        for h in range(span // HEAD):
            head = slice(h * HEAD, (h + 1) * HEAD)
            pieces += [keys[head], values[head]]
        whole = jnp.concatenate(pieces + [queries], axis=0)
        out[...] = whole[:, 0:1] if bias else whole


def prepare_weights(meta, w_qkv, b_qkv):
    width, total = w_qkv.shape
    features = total // 4
    return call(
        weights_kernel,
        "weights",
        meta,
        [w_qkv, b_qkv],
        [shape((features, width)), shape((features, 1), F32)],
        2,
        scratch=[
            pltpu.VMEM((3, width, 256), BF16),
            pltpu.VMEM((1, total), F32),
            pltpu.SemaphoreType.DMA((3,)),
        ],
        far=(0,),
    )


def queries_keys_values(place, cols, normed, wt_ref, bias, cos_ref, sin_ref, out_ref):
    count = normed.shape[0]
    out = mxu(wt_ref[...], normed, NT) + bias[...]
    at = pl.ds(pl.multiple_of(place, count), count)
    cosine, sine = cos_ref[:, at], sin_ref[:, at]
    heads = out_ref.shape[0] // (3 * HEAD)
    out_ref[:, cols] = out.astype(BF16)
    starts = [2 * HEAD * h for h in range(heads)] + [2 * HEAD * heads + HEAD * h for h in range(heads)]
    for row in starts:
        first, second = out[row : row + HALF], out[row + HALF : row + ROT]
        turned = jnp.concatenate([first * cosine - second * sine, second * cosine + first * sine], axis=0)
        out_ref[row : row + ROT, cols] = turned.astype(BF16)


def project_kernel(meta, pair_x, far_x, gain, shift, wt_ref, bias, cos_ref, sin_ref, qkv_pair, qkv_far, normed_pair, normed_far):
    rows = pair_x.shape[0]
    for j, (x_ref, qkv_ref, normed_ref) in enumerate(((pair_x, qkv_pair, normed_pair), (far_x, qkv_far, normed_far))):
        scaled, _ = standard(x_ref[...].astype(F32))
        normed = (scaled * row_of(gain) + row_of(shift)).astype(BF16)
        normed_ref[...] = normed.T
        place = (meta[HERE] ^ (2 + j)) * rows
        queries_keys_values(place, slice(None), normed, wt_ref, bias, cos_ref, sin_ref, qkv_ref)


def project(meta, pair_x, far_x, projection, hold):
    rows, width = pair_x.shape
    features = projection[2].shape[0]
    return call(
        project_kernel,
        "project",
        meta,
        [pair_x, far_x, *projection],
        [shape((features, rows))] * 2 + [shape((width, rows))] * 2,
        4,
        hold=hold,
    )


def attended_grad_kernel(meta, own_ct, core_ct, w_ref, mine_ref, send_ref, rows_ref, sem):
    rows = own_ct.shape[0]
    span = mine_ref.shape[0]
    core, pair = meta[CORE], meta[PAIR]
    half = pl.ds(pl.multiple_of(core * 2 * span, 2 * span), 2 * span)
    copy = pltpu.make_async_copy(w_ref.at[half, :], rows_ref, sem)
    copy.start()
    copy.wait()
    for b in range(2):
        ct = jnp.where(core == b, own_ct[...], core_ct[...]).astype(F32)
        grad = (ct * token_weight(meta, column((2 * pair + b) * rows, rows))).astype(BF16)
        both = mxu(rows_ref[...], grad, NT).astype(BF16)
        cols = slice(b * rows, (b + 1) * rows)
        mine_ref[:, cols] = jnp.where(pair == 0, both[:span], both[span:])
        send_ref[:, cols] = jnp.where(pair == 0, both[span:], both[:span])


def attended_grad(meta, own_ct, core_ct, w_out_attn, hold):
    rows, width = own_ct.shape
    span = width // 4
    return call(
        attended_grad_kernel,
        "attended_grad",
        meta,
        [own_ct, core_ct, w_out_attn],
        [shape((span, 2 * rows)), shape((span, 2 * rows)), shape((2 * span, width))],
        2,
        scratch=[pltpu.SemaphoreType.DMA],
        hold=hold,
        far=(2,),
    )


def hidden_kernel(
    meta,
    own_x,
    core_x,
    own_ct,
    core_ct,
    gain,
    shift,
    win_ref,
    bin_ref,
    wout_ref,
    gain_one,
    shift_one,
    wt_ref,
    bias,
    cos_ref,
    sin_ref,
    act_ref,
    hid_ref,
    grad_ref,
    turned_ref,
    scaled_ref,
    bin_grad_ref,
    branch_sum_ref,
    qkv_own,
    qkv_core,
    normed_own,
    normed_core,
    win_half,
    wout_half,
    bin_row,
    sems,
):
    rows, width = own_x.shape
    hidden_size = win_ref.shape[1] // 2
    chunk = 256
    base = pl.multiple_of(meta[CORE] * hidden_size, hidden_size)
    copies = [
        pltpu.make_async_copy(win_ref.at[:, pl.ds(base, hidden_size)], win_half, sems.at[0]),
        pltpu.make_async_copy(wout_ref.at[pl.ds(base, hidden_size), :], wout_half, sems.at[1]),
    ]
    for copy in copies:
        copy.start()
    bin_row[...] = row_of(bin_ref)
    branch_sum_ref[...] = jnp.zeros_like(branch_sum_ref)
    inputs = ((own_x, own_ct, qkv_own, normed_own), (core_x, core_ct, qkv_core, normed_core))
    totals = []
    for block, (x_ref, ct_ref, qkv_ref, normed_ref) in enumerate(inputs):
        at = slice(block * rows, (block + 1) * rows)
        place = (meta[HERE] ^ block) * rows
        scaled, _ = standard(x_ref[...].astype(F32))
        scaled_ref[at, :] = scaled
        normed = (scaled * row_of(gain_one) + row_of(shift_one)).astype(BF16)
        normed_ref[...] = normed.T
        queries_keys_values(place, slice(None), normed, wt_ref, bias, cos_ref, sin_ref, qkv_ref)
        normed = (scaled * row_of(gain) + row_of(shift)).astype(BF16)
        turned_ref[:, at] = normed.T
        grad = (ct_ref[...].astype(F32) * token_weight(meta, column(place, rows))).astype(BF16)
        grad_ref[at, :] = grad
        if block == 0:
            branch_sum_ref[0:1, :] = jnp.sum(grad.astype(F32), axis=0, keepdims=True)
        if block == 0:
            for copy in copies:
                copy.wait()
        sums = []
        for j in range(0, hidden_size, chunk):
            cols = slice(j, j + chunk)
            there = pl.ds(pl.multiple_of(base + j, 128), chunk)
            hidden = mxu(normed, win_half[:, cols]) + bin_row[:, there]
            back = mxu(grad, wout_half[cols, :], NT)
            below = 0.5 + 0.5 * lax.erf(hidden * (0.5**0.5))
            bell = jnp.exp(hidden * hidden * -0.5) * 0.3989422804014327
            act_ref[at, cols] = (hidden * below).astype(BF16)
            rounded = (back * (below + hidden * bell)).astype(BF16)
            hid_ref[at, cols] = rounded
            sums.append(jnp.sum(rounded.astype(F32), axis=0, keepdims=True))
        totals.append(jnp.concatenate(sums, axis=1))
    bin_grad_ref[...] = totals[0] + totals[1]


def hidden_part(meta, own_x, core_x, own_ct, core_ct, gain, shift, w_in, b_in, w_out, projection, hold):
    rows, width = own_x.shape
    hidden_size = w_in.shape[1] // 2
    features = projection[2].shape[0]
    outs = [
        shape((2 * rows, hidden_size)),
        shape((2 * rows, hidden_size)),
        shape((2 * rows, width)),
        shape((width, 2 * rows)),
        shape((2 * rows, width), F32),
        shape((1, hidden_size), F32),
        shape((8, width), F32),
        shape((features, rows)),
        shape((features, rows)),
        shape((width, rows)),
        shape((width, rows)),
        shape((width, hidden_size)),
        shape((hidden_size, width)),
    ]
    operands = [own_x, core_x, own_ct, core_ct, gain, shift, w_in, b_in, w_out, *projection]
    return call(
        hidden_kernel,
        "hidden",
        meta,
        operands,
        outs,
        13,
        scratch=[pltpu.VMEM((1, 2 * hidden_size), F32), pltpu.SemaphoreType.DMA((2,))],
        vmem=8,
        hold=hold,
        far=(6, 8),
    )


def out_grad_kernel(meta, act_ref, grad_ref, x_ref, send_ref, keep_ref, again_ref):
    again_ref[...] = x_ref[...]
    quarter = send_ref.shape[0] // 2
    grad = grad_ref[...]
    for ref, bit in ((send_ref, 1 - meta[XBIT]), (keep_ref, meta[XBIT])):
        for z in range(2):
            there = pl.ds(pl.multiple_of((2 * z + bit) * quarter, quarter), quarter)
            ref[z * quarter : (z + 1) * quarter, :] = mxu(act_ref[:, there], grad, TN).astype(BF16)


def out_grad(meta, act, grad, x, hold):
    half = shape((act.shape[1] // 2, grad.shape[1]))
    return call(out_grad_kernel, "w_out_grad", meta, [act, grad, x], [half, half, shape(x.shape)], 3, hold=hold)


def in_grad_kernel(
    meta, act_ref, hid_ref, turned_ref, scaled_ref, gain, win_ref, wout_ref, branch_ref, term_ref, send_ref, keep_ref, small_ref
):
    width = win_ref.shape[0]
    fine = width // 16
    for ref, bit in ((send_ref, 1 - meta[PAIR]), (keep_ref, meta[PAIR])):
        pieces = []
        for xb in range(2):
            for zl in range(2):
                for zh in range(2):
                    source = (4 * zh + 2 * zl + xb) * 2 * fine + bit * fine
                    pieces.append(turned_ref[pl.ds(pl.multiple_of(source, fine), fine), :])
        ref[...] = mxu(jnp.concatenate(pieces, axis=0), hid_ref[...]).astype(BF16)
    rows = act_ref.shape[0] // 2
    small_ref[...] = jnp.zeros_like(small_ref)
    for block in range(2):
        at = slice(block * rows, (block + 1) * rows)
        branch_ref[at, :] = mxu(act_ref[at, :], wout_ref[...]).astype(BF16)
        normed_grad = mxu(hid_ref[at, :], win_ref[...], NT)
        term_ref[at, :] = (normed_grad * row_of(gain)).astype(BF16)
        small_ref[0:1, :] += jnp.sum(normed_grad * scaled_ref[at, :], axis=0, keepdims=True)
        small_ref[1:2, :] += jnp.sum(normed_grad, axis=0, keepdims=True)


def in_grad(meta, act, hid, turned, scaled, gain, w_in, w_out, hold):
    tokens, hidden_size = act.shape
    width = w_in.shape[0]
    outs = [
        shape((tokens, width)),
        shape((tokens, width)),
        shape((width // 2, hidden_size)),
        shape((width // 2, hidden_size)),
        shape((8, width), F32),
    ]
    return call(
        in_grad_kernel,
        "w_in_grad",
        meta,
        [act, hid, turned, scaled, gain, w_in, w_out],
        outs,
        9,
        hold=hold,
    )


def three(value):
    a = value.astype(BF16).astype(F32)
    rest = value - a
    b = rest.astype(BF16).astype(F32)
    return a, b, rest - b


def attend_kernel(
    head,
    meta,
    b0,
    b1,
    b2,
    b3,
    do_near,
    do_far,
    cos_ref,
    sin_ref,
    near_ref,
    far_ref,
    dqo_ref,
    dkv_ref,
    stamp_ref,
    out_ref,
    kt_ref,
    ka_ref,
    va_ref,
    vt_ref,
    s_ref,
    p_ref,
    d_ref,
    acc_ref,
):
    tile = b0.shape[1]
    heads = do_near.shape[0] // HEAD
    of_head = slice(head * HEAD, (head + 1) * HEAD)
    kv_rows = slice(2 * HEAD * head, 2 * HEAD * (head + 1))
    q_rows = slice(HEAD * (2 * heads + head), HEAD * (2 * heads + head + 1))
    length = 4 * tile
    step = tile // 2
    scale = HEAD ** (-0.5)
    here, pair = meta[HERE], meta[PAIR]
    lows, highs = doc_bounds(meta, length)

    def placed(rows, b):
        low = here % 2 == b % 2
        near = jnp.where(low, b0[rows, :], b1[rows, :])
        far = jnp.where(low, b2[rows, :], b3[rows, :])
        return jnp.where(pair == b // 2, near, far)

    pos = lax.broadcasted_iota(jnp.int32, (EXTRA, length), 1)
    row = lax.broadcasted_iota(jnp.int32, (EXTRA, length), 0)
    inside = jnp.zeros(pos.shape, jnp.bool_)
    for d in range(DOCS):
        inside = inside | ((row == d) & (pos >= lows[d]) & (pos < highs[d]))
    key_rows = jnp.where(inside, 1.0, 0.0).astype(BF16)
    one_rows = jnp.where(row < 3, 1.0, 0.0).astype(BF16)
    query_rows = jnp.where((row < DOCS) & jnp.logical_not(inside), MASKED, 0.0).astype(BF16)
    fill = jnp.zeros((HEAD - EXTRA, tile), BF16)
    for b in range(4):
        cols = slice(b * tile, (b + 1) * tile)
        kv = placed(kv_rows, b)
        kt_ref[:, cols] = kv[:HEAD]
        ka_ref[cols, :] = jnp.concatenate([kv[:HEAD], key_rows[:, cols], fill], axis=0).T
        va = jnp.concatenate([kv[HEAD:], one_rows[:, cols], fill], axis=0)
        vt_ref[:, cols] = va[: HEAD + EXTRA]
        va_ref[cols, :] = va.T
    extra_row = lax.broadcasted_iota(jnp.int32, (EXTRA, tile), 0)
    offset = lax.broadcasted_iota(jnp.int32, (step, tile), 0) - lax.broadcasted_iota(jnp.int32, (step, tile), 1)
    per_half = 2 * tile

    def run(v, buf, widest):
        width = (v + 1) * tile
        chunks = width // step
        cols = slice(v * tile, (v + 1) * tile)
        low = lambda k: max(0, k * step - v * tile)
        cosine, sine = cos_ref[:, cols], sin_ref[:, cols]
        q_t = placed(q_rows, v) * jnp.asarray(scale, BF16)
        half = slice((v % 2) * tile, (v % 2 + 1) * tile)
        do_t = jnp.where(pair == v // 2, do_near[of_head, half], do_far[of_head, half])
        q_aug = jnp.concatenate([q_t, query_rows[:, cols], fill], axis=0)
        top = jnp.full((1, tile), MASKED, F32)
        for k in range(chunks):
            rows, l = slice(k * step, (k + 1) * step), low(k)
            scores = mxu(ka_ref[rows, :], q_aug[:, l:])
            if (k + 1) * step > v * tile:
                scores = jnp.where(offset[:, l:] <= v * tile - k * step, scores, MASKED)
            s_ref[buf, rows, l:] = scores
            peak = jnp.max(scores, axis=0, keepdims=True)
            if l:
                top = jnp.concatenate([top[:, :l], jnp.maximum(top[:, l:], peak)], axis=1)
            else:
                top = jnp.maximum(top, peak)
            yield
        for k in range(chunks):
            rows, l = slice(k * step, (k + 1) * step), low(k)
            p_ref[buf, rows, l:] = jnp.exp(s_ref[buf, rows, l:] - top[:, l:]).astype(BF16)
            yield
        lanes = [(g * step, v * tile + (g + 1) * step) for g in range(tile // step)]
        out_all = jnp.concatenate(
            [mxu(vt_ref[:, :w], p_ref[buf, :w, l : l + step]) for l, w in lanes], axis=1
        )
        yield
        inverse = 1.0 / out_all[HEAD : HEAD + 1]
        out_t = out_all[:HEAD] * inverse
        do_scaled = (do_t.astype(F32) * inverse).astype(BF16)
        delta = jnp.sum(do_scaled.astype(F32) * out_t, axis=0, keepdims=True)
        a, b, c = three(-delta)
        terms = jnp.where(extra_row == 0, a, jnp.where(extra_row == 1, b, jnp.where(extra_row == 2, c, 0.0)))
        do_aug = jnp.concatenate([do_scaled, terms.astype(BF16), fill], axis=0)
        for k in range(chunks):
            rows, l = slice(k * step, (k + 1) * step), low(k)
            weight_grad = mxu(va_ref[rows, :], do_aug[:, l:])
            d_ref[buf, rows, l:] = (p_ref[buf, rows, l:].astype(F32) * weight_grad).astype(BF16)
            yield
        groups = [(0, v * tile, 0)] if v else []
        groups += [(v * tile + g * step, v * tile + (g + 1) * step, g * step) for g in range(tile // step)]
        for first, side, ref in ((HEAD, do_scaled, p_ref), (0, q_t, d_ref)):
            for r, s, l in groups:
                value = mxu(side[:, l:], ref[buf, r:s, l:], NT)
                if widest:
                    acc_ref[first : first + HEAD, r:s] = value
                else:
                    acc_ref[first : first + HEAD, r:s] += value
            yield
        dq_t = (
            jnp.concatenate([mxu(kt_ref[:, :w], d_ref[buf, :w, l : l + step]) for l, w in lanes], axis=1) * scale
        )
        first, second = dq_t[:HALF], dq_t[HALF:ROT]
        joined = jnp.concatenate(
            [first * cosine + second * sine, second * cosine - first * sine, dq_t[ROT:], out_t], axis=0
        )
        out_ref[(v // 2) ^ pair, :, half] = out_t.astype(BF16)
        dqo_ref[(v // 2) ^ pair, half, :] = joined.T.astype(BF16)
        yield

    tiles = length // tile
    order = list(range(tiles))[::-1]
    runs = [(run(v, n % 2, n == 0), (v + 1) * tile // step) for n, v in enumerate(order)]
    current, count = runs[0]
    for _ in range(2 * count):
        next(current)
    for n in range(tiles):
        current, count = runs[n]
        following, total = (runs[n + 1][0], 2 * runs[n + 1][1]) if n + 1 < tiles else (None, 0)
        done = 0
        for i in range(count + 4):
            next(current, None)
            while done < (i + 1) * total // (count + 4):
                next(following)
                done += 1
        for _ in current:
            pass
    grads = acc_ref[...]
    cosine, sine = cos_ref[...], sin_ref[...]
    first, second = grads[:HALF], grads[HALF:ROT]
    grads = jnp.concatenate(
        [first * cosine + second * sine, second * cosine - first * sine, grads[ROT:]], axis=0
    )
    stamp_ref[0] = 0
    near_ref[...] = out_ref[0]
    far_ref[...] = out_ref[1]
    for h in range(2):
        dkv_ref[h ^ pair] = grads[:, h * per_half : (h + 1) * per_half].T.astype(BF16)


def attend(meta, head, blocks, do_near, do_far, cosine, sine, hold):
    rows = blocks[0].shape[1]
    length = 4 * rows
    return call(
        functools.partial(attend_kernel, head),
        "attend%d" % head,
        meta,
        [*blocks, do_near, do_far, cosine, sine],
        [shape((HEAD, 2 * rows))] * 2 + [shape((2, 2 * rows, 2 * HEAD))] * 2 + [shape((1,), jnp.int32)],
        9,
        hold=hold,
        scratch=[
            pltpu.VMEM((2, HEAD, 2 * rows), BF16),
            pltpu.VMEM((HEAD, length), BF16),
            pltpu.VMEM((length, 2 * HEAD), BF16),
            pltpu.VMEM((length, 2 * HEAD), BF16),
            pltpu.VMEM((HEAD + EXTRA, length), BF16),
            pltpu.VMEM((2, length, rows), F32),
            pltpu.VMEM((2, length, rows), BF16),
            pltpu.VMEM((2, length, rows), BF16),
            pltpu.VMEM((2 * HEAD, length), F32),
        ],
        vmem=21,
    )


def branch_kernel(meta, m0, m1, m2, a0, a1, a2, w_ref, branch, own_ct, core_ct, own_ref, send_ref, goa_send, goa_keep):
    pair, core = meta[PAIR], meta[CORE]
    rows = own_ref.shape[0]
    heads = (m0, m1, m2, a0, a1, a2)
    mine = jnp.concatenate([r[...] for r in heads[:3]], axis=0)
    theirs = jnp.concatenate([r[...] for r in heads[3:]], axis=0)
    six = jnp.concatenate([jnp.where(pair == 0, mine, theirs), jnp.where(pair == 0, theirs, mine)], axis=0)
    own_cols = jnp.where(core == 0, six[:, :rows], six[:, rows:])
    other_cols = jnp.where(core == 0, six[:, rows:], six[:, :rows])
    half = w_ref.shape[0]
    weight = w_ref[...]
    send_ref[...] = (mxu(other_cols, weight, TN) + branch[rows:, :].astype(F32)).astype(BF16)
    own_ref[...] = mxu(own_cols, weight, TN) + branch[:rows, :].astype(F32)
    grads = []
    for j, ct in enumerate((own_ct, core_ct)):
        place = (meta[HERE] ^ j) * rows
        grads.append((ct[...].astype(F32) * token_weight(meta, column(place, rows))).astype(BF16))
    total = mxu(own_cols, grads[0]) + mxu(other_cols, grads[1])
    part = half // 4
    for z in range(2):
        both = total[2 * z * part : (2 * z + 1) * part], total[(2 * z + 1) * part : (2 * z + 2) * part]
        to = slice(z * part, (z + 1) * part)
        goa_keep[to, :] = jnp.where(meta[XBIT] == 0, both[0], both[1]).astype(BF16)
        goa_send[to, :] = jnp.where(meta[XBIT] == 0, both[1], both[0]).astype(BF16)


def branch_part(meta, mine, arrived, w_rows, branch, own_ct, core_ct, after):
    rows, width = own_ct.shape
    return call(
        branch_kernel,
        "branch",
        meta,
        [*mine, *arrived, w_rows, branch, own_ct, core_ct],
        [shape((rows, width), F32), shape((rows, width))] + [shape((width // 4, width))] * 2,
        0,
        after=after,
    )


def with_queries(wt_ref):
    span = wt_ref.shape[0] // 3
    pieces = [wt_ref[: 2 * span, :]]
    for h in range(span // HEAD):
        head = wt_ref[2 * span + h * HEAD : 2 * span + (h + 1) * HEAD, :]
        pieces += [head, jnp.zeros_like(head)]
    return jnp.concatenate(pieces, axis=0)


def far_kernel(meta, *refs):
    kv, qo = refs[0:3], refs[3:6]
    wt_ref, gain, send_ref, keep_ref = refs[6:]
    core = meta[CORE]
    rows = send_ref.shape[0]
    right = with_queries(wt_ref)
    for out, b in ((send_ref, 1 - core), (keep_ref, core)):
        at = pl.ds(pl.multiple_of(b * rows, rows), rows)
        left = jnp.concatenate([r[1, at, :] for r in kv] + [r[1, at, :] for r in qo], axis=1)
        out[...] = (mxu(left, right) * row_of(gain)).astype(BF16)


def far_terms(meta, dkv, dqo, wt, gain, hold):
    rows, width = dkv[0].shape[1] // 2, wt.shape[1]
    return call(
        far_kernel,
        "far_terms",
        meta,
        [*dkv, *dqo, wt, gain],
        [shape((rows, width)), shape((rows, width))],
        0,
        hold=hold,
    )


PIECES = 24


def near_kernel(meta, *refs):
    kv, qo = refs[0:3], refs[3:6]
    wt_ref, gain, shift, term_two, n0, n1, n2, n3, two_ref, branch_sum, bin_ref = refs[6:17]
    send_ref, own_ref, out_ref, vector_ref = refs[17:]
    core = meta[CORE]
    rows, width = own_ref.shape
    features = wt_ref.shape[0]
    span = features // 3
    devices = out_ref.shape[0]
    gain_row, shift_row = row_of(gain), row_of(shift)
    right = with_queries(wt_ref)

    def both(half, b):
        at = pl.ds(pl.multiple_of(b * rows, rows), rows)
        return jnp.concatenate([r[half, at, :] for r in kv] + [r[half, at, :] for r in qo], axis=1)

    near_own, near_core = both(0, core), both(0, 1 - core)
    far_own, far_core = both(1, core), both(1, 1 - core)
    grad = mxu(n0[...], near_own) + mxu(n1[...], near_core) + mxu(n2[...], far_own) + mxu(n3[...], far_core)
    sums = sum(
        jnp.sum(a.astype(F32), axis=0, keepdims=True) for a in (near_own, near_core, far_own, far_core)
    )

    def tight(value):
        queries = [value[:, 2 * span + 2 * HEAD * h : 2 * span + 2 * HEAD * h + HEAD] for h in range(3)]
        return jnp.concatenate([value[:, : 2 * span]] + queries, axis=1)

    grad, sums = tight(grad), tight(sums)
    weights = wt_ref[...].T.astype(F32)
    by_weight = jnp.sum(weights * grad, axis=1, keepdims=True)
    shift_grad = jnp.sum(weights * sums, axis=1, keepdims=True)
    lane = lax.broadcasted_iota(jnp.int32, (width, 128), 1)
    turned = jnp.where(lane == 0, by_weight, jnp.where(lane == 1, shift_grad, 0.0)).T
    shift_grad = turned[1:2, :]
    gain_grad = (turned[0:1, :] - shift_row * shift_grad) / gain_row

    offset = features % 128

    def spread(vectors, place_row, place_col, pieces):
        count = vectors.shape[0]
        index = lambda place: jnp.floor((place.astype(F32) + 0.5) * (1.0 / PIECES)).astype(jnp.int32)
        device = lax.broadcasted_iota(jnp.int32, (devices, vectors.shape[1]), 0)
        owner = index(place_row)
        parts = []
        for p in range(pieces):
            chosen = owner == device * pieces + p
            for c in range(count):
                value = vectors[c : c + 1, :]
                high = value.astype(BF16)
                low = (value - high.astype(F32)).astype(BF16)
                for part in (high, low):
                    parts.append(jnp.where(chosen, part.astype(F32), 0.0))
        within = place_col - PIECES * index(place_col) + offset
        lane = lax.broadcasted_iota(jnp.int32, (vectors.shape[1], 128), 1)
        table = jnp.where(within == lane, 1.0, 0.0).astype(BF16)
        return mxu(jnp.concatenate(parts, axis=0).astype(BF16), table)

    def counted(size):
        return (
            lax.broadcasted_iota(jnp.int32, (1, size), 1),
            lax.broadcasted_iota(jnp.int32, (size, 1), 0),
        )

    def qkv_place(index):
        rest = index - 2 * span
        keys = (1 + (index // HEAD) % 2) * width + (index // (2 * HEAD)) * HEAD
        return meta[GROUP] * span + index % HEAD + jnp.where(rest < 0, keys, (rest // HEAD) * HEAD)

    lanes, sub = counted(width)
    norms = jnp.concatenate(
        [gain_grad, shift_grad, two_ref[0:1, :], two_ref[1:2, :], branch_sum[0:1, :]], axis=0
    )
    lanes_kv, sub_kv = counted(features)
    hidden_size = bin_ref.shape[1]
    lanes_in, sub_in = counted(hidden_size)
    base = core * hidden_size
    row = 0
    for found in (
        spread(norms, lanes, sub, 1),
        spread(sums, qkv_place(lanes_kv), qkv_place(sub_kv), 3),
        spread(bin_ref[...], base + lanes_in, base + sub_in, 4),
    ):
        for k in range(found.shape[0] // devices):
            vector_ref[:, row, :] = found[k * devices : (k + 1) * devices]
            row += 1
    chunk = width // devices
    whole = (features // 128) * 128
    tail = jnp.concatenate([grad[:, whole:], jnp.zeros((width, 128 - offset), F32)], axis=1)
    for d in range(devices):
        at = slice(d * chunk, (d + 1) * chunk)
        out_ref[d, :, :whole] = grad[at, :whole].astype(BF16)
        out_ref[d, :, whole:] = (tail[at] + vector_ref[d]).astype(BF16)
    send_ref[...] = (mxu(near_core, right) * gain_row + term_two[rows:, :].astype(F32)).astype(BF16)
    own_ref[...] = mxu(near_own, right) * gain_row + term_two[:rows, :].astype(F32)


def near_terms(meta, dkv, dqo, wt, gain, shift, term_two, normed, vectors, devices, after):
    rows, width = dkv[0].shape[1] // 2, wt.shape[1]
    lanes = -(-wt.shape[0] // 128) * 128
    chunk = width // devices
    outs = [shape((rows, width)), shape((rows, width), F32), shape((devices, chunk, lanes))]
    return call(
        near_kernel,
        "near_terms",
        meta,
        [*dkv, *dqo, wt, gain, shift, term_two, *normed, *vectors],
        outs,
        0,
        scratch=[pltpu.VMEM((devices, chunk, 128), F32)],
        vmem=9,
        after=after,
    )


def gather_kernel(meta, in_ref, out_ref, vectors_ref):
    heads = HEADS // 4
    span = heads * HEAD
    width = out_ref.shape[1] // 3
    whole = ((3 * span) // 128) * 128
    vectors = 0.0
    for s in range(4):
        value = sum(in_ref[4 * r + s].astype(F32) for r in range(in_ref.shape[0] // 4))
        vectors = vectors + value[:, whole:]
        group = 2 * (s % 2) + s // 2
        for h in range(heads):
            at = group * span + h * HEAD
            out_ref[:, at : at + HEAD] = value[:, 2 * span + h * HEAD : 2 * span + (h + 1) * HEAD]
            out_ref[:, width + at : width + at + HEAD] = value[:, 2 * HEAD * h : 2 * HEAD * h + HEAD]
            out_ref[:, 2 * width + at : 2 * width + at + HEAD] = value[:, 2 * HEAD * h + HEAD : 2 * HEAD * (h + 1)]
    vectors = pltpu.roll(vectors, 128 - (3 * span) % 128, 1)
    vectors_ref[...] = jnp.zeros_like(vectors_ref)
    for k in range(vectors.shape[0] // 2):
        vectors_ref[k : k + 1, :] = vectors[2 * k : 2 * k + 1, :] + vectors[2 * k + 1 : 2 * k + 2, :]


def gather_qkv(meta, arrived):
    rows = arrived.shape[1]
    outs = [shape((rows, 3 * HEADS * HEAD), F32), shape((16, 128), F32)]
    return call(gather_kernel, "gather", meta, [arrived], outs, 0)


def last_kernel(meta, x_ref, ct_ref, near_ref, core_ref, pair_ref, tokens_ref, docs_ref):
    rows = x_ref.shape[0]
    scaled, rate = standard(x_ref[...].astype(F32))
    term = near_ref[...] + core_ref[...].astype(F32) + pair_ref[...].astype(F32)
    back = rate * (
        term
        - jnp.mean(term, axis=-1, keepdims=True)
        - scaled * jnp.mean(term * scaled, axis=-1, keepdims=True)
    )
    pos = column(meta[HERE] * rows, rows)
    grad = ct_ref[...].astype(F32) * token_weight(meta, pos) + back
    tokens_ref[...] = grad.astype(BF16)
    squares = jnp.sum(grad * grad, axis=1, keepdims=True)
    lows, highs = doc_bounds(meta, 4 * rows)
    lane = lax.broadcasted_iota(jnp.int32, (8, 128), 1)
    docs = jnp.zeros((8, 128), F32)
    for d in range(DOCS):
        total = jnp.sum(jnp.where((pos >= lows[d]) & (pos < highs[d]), squares, 0.0), axis=0, keepdims=True)
        docs = jnp.where(lane == d, total, docs)
    docs_ref[...] = docs


def last(meta, x, ct, near, core, pair, after=()):
    operands = [x, ct, near, core, pair]
    outs = [shape(x.shape), shape((8, 128), F32)]
    return call(last_kernel, "input_grad", meta, operands, outs, 0, after=after)


def flip(value, axis, bit):
    size = lax.axis_size(axis)
    return lax.ppermute(value, axis, [(i, i ^ (1 << bit)) for i in range(size)])


def relay_kernel(places, finals, meta, *refs):
    count = len(places)
    ins, outs = refs[: 2 * count], refs[2 * count :]
    for k, (place, final) in enumerate(zip(places, finals)):
        keep, arrived = ins[2 * k], ins[2 * k + 1]
        first, second = outs[2 * k], outs[2 * k + 1]
        if final:
            total = keep[...].astype(F32) + arrived[...].astype(F32)
            first[...] = total.astype(first.dtype)
            second[...] = total
        else:
            half = first.shape[0]
            for out, bit in ((first, 1 - meta[place]), (second, meta[place])):
                at = pl.ds(pl.multiple_of(bit * half, half), half)
                out[...] = (keep[at, :].astype(F32) + arrived[at, :].astype(F32)).astype(out.dtype)


def relay(meta, name, steps, after=(), hold=()):
    outs, operands = [], []
    for keep, arrived, place in steps:
        rows, width = keep.shape
        rows = rows if place is None else rows // 2
        outs += [shape((rows, width)), shape((rows, width), F32)]
        operands += [keep, arrived]
    places = [place for _, _, place in steps]
    found = call(
        functools.partial(relay_kernel, places, [p is None for p in places]),
        name,
        meta,
        operands,
        outs,
        0,
        after=after,
        hold=hold,
    )
    return [(found[2 * k], found[2 * k + 1]) for k in range(len(steps))]


def add_kernel(meta, a_ref, b_ref, out_ref):
    out_ref[...] = (a_ref[...].astype(F32) + b_ref[...].astype(F32)).astype(out_ref.dtype)


def add(meta, name, a, b, after=()):
    return call(add_kernel, name, meta, [a, b], [shape(a.shape)], 0, after=after)[0]


def head_plan(
    tokens,
    cotangent,
    lengths,
    ln1_gain,
    ln1_bias,
    ln2_gain,
    ln2_bias,
    w_qkv,
    b_qkv,
    w_out_attn,
    b_out_attn,
    w_in,
    b_in,
    w_out,
    b_out,
):
    dp_size = lax.axis_size("dp")
    here = lax.axis_index("blk").astype(jnp.int32)
    row = lax.axis_index("dp").astype(jnp.int32)
    pair, core = here // 2, here % 2
    xbit, z_low, z_high = row & 1, (row >> 1) & 1, row >> 2
    meta = jnp.concatenate([jnp.stack([here, pair, core, 2 * core + pair, xbit, z_low, z_high]), lengths[0]])
    own_x, own_ct = tokens[0], cotangent[0]
    rows, width = own_x.shape
    length = 4 * rows
    heads = HEADS // 4
    assert width == PIECES * 4 * dp_size
    positions = np.arange(length, dtype=np.float32)
    frequency = (10000.0 ** (-(np.arange(HALF, dtype=np.float32) * 2.0) / ROT)).astype(np.float32)
    angle = frequency[:, None] * positions[None, :]
    cosine, sine = jnp.asarray(np.cos(angle)), jnp.asarray(np.sin(angle))

    core_x = flip(own_x, "blk", 0)
    core_ct = flip(own_ct, "blk", 0)
    pair_x = flip(own_x, "blk", 1)

    devices = 4 * dp_size
    axes = ("dp", "blk")
    wt, bias = prepare_weights(meta, w_qkv, b_qkv)
    projection = (ln1_gain, ln1_bias, wt, bias, cosine, sine)
    do_near, do_send, w_rows = attended_grad(meta, own_ct, core_ct, w_out_attn, (wt, bias))
    do_far = flip(do_send, "blk", 1)
    (
        act,
        hid,
        grad,
        turned,
        scaled,
        b_in_grad,
        branch_sum,
        qkv_own,
        qkv_core,
        normed_own,
        normed_core,
        win_half,
        wout_half,
    ) = hidden_part(
        meta, own_x, core_x, own_ct, core_ct, ln2_gain, ln2_bias, w_in, b_in, w_out, projection, (do_near, do_send)
    )
    early = (do_near, wt, bias, qkv_own, qkv_core, normed_own, normed_core, b_in_grad, branch_sum)
    gout_send, gout_keep, pair_again = out_grad(
        meta, act, grad, pair_x, early + (hid, turned, scaled, win_half, wout_half)
    )
    gout_x = flip(gout_send, "dp", 0)
    far_x = flip(pair_again, "blk", 0)
    branch, term_two, gin_send, gin_keep, small_two = in_grad(
        meta, act, hid, turned, scaled, ln2_gain, win_half, wout_half, early + (gout_keep,)
    )
    gin_y = flip(gin_send, "blk", 1)
    early = (do_near, normed_own, normed_core, b_in_grad, branch_sum, branch, term_two, small_two, gout_keep, gin_keep)
    qkv_pair, qkv_far, normed_pair, normed_far = project(
        meta, pair_x, far_x, projection, early + (qkv_own, qkv_core)
    )
    blocks = (qkv_own, qkv_core, qkv_pair, qkv_far)
    early = early[1:] + (wt, normed_pair, normed_far)
    nears, arrived, dqo, dkv = [], [], [], []
    for h in range(heads):
        near, far, dqo_h, dkv_h, _ = attend(
            meta, h, blocks, do_near, do_far, cosine, sine, early + tuple(nears + dqo + dkv)
        )
        nears.append(near)
        dqo.append(dqo_h)
        dkv.append(dkv_h)
        arrived.append(flip(far, "blk", 1))
        if h == heads - 2:
            ((gout_send, gout_keep),) = relay(
                meta, "gout_z_low", [(gout_keep, gout_x, ZLOW)], (near,), early[:7] + early[8:] + tuple(nears + dqo + dkv)
            )
            gout_z = flip(gout_send, "dp", 1)
            early = early[:7] + early[8:] + (gout_keep, gout_send)
    held = early + tuple(nears)
    ((gin_send, gin_keep),) = relay(meta, "gin_x", [(gin_keep, gin_y, XBIT)], (), held + tuple(dqo + dkv))
    gin_x = flip(gin_send, "dp", 0)
    far_send, far_keep = far_terms(meta, dkv, dqo, wt, ln1_gain, held + (gin_keep, gin_send))
    far_arrived = flip(far_send, "blk", 0)
    near_send, near_own, g_qkv = near_terms(
        meta,
        dkv,
        dqo,
        wt,
        ln1_gain,
        ln1_bias,
        term_two,
        (normed_own, normed_core, normed_pair, normed_far),
        (small_two, branch_sum, b_in_grad),
        devices,
        (far_send,),
    )
    from_core = flip(near_send, "blk", 0)
    far_sum = add(meta, "far_sum", far_keep, far_arrived, (near_send,))
    from_pair = flip(far_sum, "blk", 1)
    ((gout_send, gout_keep),) = relay(meta, "gout_y", [(gout_keep, gout_z, PAIR)], (far_sum,))
    gout_y = flip(gout_send, "blk", 1)
    arrived_qkv = lax.all_to_all(g_qkv, axes, 0, 0, tiled=True)
    own_part, send_part, goa_send, goa_keep = branch_part(
        meta, nears, arrived, w_rows, branch, own_ct, core_ct, (gout_send,)
    )
    goa_x = flip(goa_send, "dp", 0)
    layer_out = (
        own_x.astype(F32)
        + own_part
        + flip(send_part, "blk", 0).astype(F32)
        + (b_out_attn.astype(F32) + b_out.astype(F32))[None, :]
    ).astype(BF16)
    top = devices // 2
    to_owner = [(i, i ^ top) for i in range(devices) if i // top != i % 2]
    (gin_send, gin_keep), (gout_send, gout_keep) = relay(
        meta, "gin_z_low", [(gin_keep, gin_x, ZLOW), (gout_keep, gout_y, None)], (goa_send,)
    )
    gin_z = flip(gin_send, "dp", 1)
    gout_o = lax.ppermute(gout_send, axes, to_owner)
    ((goa_send, goa_keep),) = relay(meta, "goa_z_low", [(goa_keep, goa_x, ZLOW)], (gin_send,))
    goa_z = flip(goa_send, "dp", 1)
    (gin_send, gin_keep), (_, gout) = relay(
        meta, "gin_z_high", [(gin_keep, gin_z, ZHIGH), (gout_keep, gout_o, None)], (goa_send,)
    )
    gin_h = flip(gin_send, "dp", 2)
    tokens_grad, docs = last(meta, own_x, own_ct, near_own, from_core, from_pair, (gin_send,))
    ((goa_send, goa_keep),) = relay(meta, "goa_y", [(goa_keep, goa_z, PAIR)], (gin_send,))
    goa_y = flip(goa_send, "blk", 1)
    (_, gin), (goa_send, goa_keep) = relay(meta, "goa_z_high", [(gin_keep, gin_h, None), (goa_keep, goa_y, None)], (docs,))
    goa_o = lax.ppermute(goa_send, axes, to_owner)

    def swap(value):
        fine = value.shape[0] // 2
        kept = lax.dynamic_slice_in_dim(value, core * fine, fine, 0)
        return kept, flip(lax.dynamic_slice_in_dim(value, (1 - core) * fine, fine, 0), "blk", 0)

    kept, given = swap(gin)
    w_in_grad = jnp.where(
        core == 0, jnp.concatenate([kept, given], axis=1), jnp.concatenate([given, kept], axis=1)
    )
    kept, given = swap(gout)
    w_out_grad = jnp.where(z_high == core, kept, given)
    kept, given = swap(goa_keep + goa_o.astype(F32))
    w_out_attn_grad = jnp.where(z_high == core, kept, given)

    docs = docs + flip(docs, "blk", 0)
    docs = docs + flip(docs, "blk", 1)
    doc_norms = docs[0, :DOCS] * (lengths[0].astype(F32) / TOK_DEV)
    w_qkv_grad, vectors = gather_qkv(meta, arrived_qkv)
    ln_grads = [vectors[k, :PIECES] for k in range(4)]
    b_branch = vectors[4, :PIECES]
    return (
        layer_out[None],
        tokens_grad[None],
        *ln_grads,
        w_qkv_grad,
        vectors[5:8, :PIECES].reshape(3 * PIECES),
        w_out_attn_grad,
        b_branch,
        w_in_grad,
        vectors[8:12, :PIECES].reshape(4 * PIECES),
        w_out_grad,
        b_branch,
        doc_norms[None],
    )


def solution(mesh):
    in_specs = (
        P("dp", "blk", None),
        P("dp", "blk", None),
        P("dp", None),
        P(),
        P(),
        P(),
        P(),
        P(),
        P(),
        P(),
        P(),
        P(),
        P(),
        P(),
        P(),
    )
    out_specs = (
        P("dp", "blk", None),
        P("dp", "blk", None),
        P(("dp", "blk")),
        P(("dp", "blk")),
        P(("dp", "blk")),
        P(("dp", "blk")),
        P(("dp", "blk"), None),
        P(("dp", "blk")),
        P(("dp", "blk"), None),
        P(("dp", "blk")),
        P(("dp", "blk"), None),
        P(("dp", "blk")),
        P(("dp", "blk"), None),
        P(("dp", "blk")),
        P("dp", None),
    )
    suits = mesh.shape["blk"] == 4 and HEADS % 4 == 0 and mesh.shape["dp"] == 8
    plan = head_plan if suits else general_plan
    return jax.shard_map(
        plan, mesh=mesh, in_specs=in_specs, out_specs=out_specs, check_vma=False
    )
```

```python
import functools

import jax
import jax.numpy as jnp
import numpy as np
from jax import lax
from jax.experimental import pallas as pl
from jax.experimental.pallas import tpu as pltpu
from jax.sharding import PartitionSpec as P

HEADS = 12
HEAD = 64
ROT = 16
DOCS = 4
TOK_DEV = 512


epsilon = 1e-05


def layer_norm(value, gain, shift):
    mean = jnp.mean(value, axis=-1, keepdims=True)
    centered = value - mean
    variance = jnp.mean(centered * centered, axis=-1, keepdims=True)
    return centered * lax.rsqrt(variance + epsilon) * gain + shift


def rotate(value, cosine, sine):
    half = ROT // 2
    rotary_part = value[..., :ROT]
    first = rotary_part[..., :half]
    second = rotary_part[..., half:]
    turned = jnp.concatenate([-second, first], axis=-1)
    return jnp.concatenate([rotary_part * cosine + turned * sine, value[..., ROT:]], axis=-1)


def document_of(positions, ends):
    return jnp.sum((positions[:, None] >= ends[None, :]).astype(jnp.int32), axis=1)


def inner(left, right):
    return lax.dot_general(
        left, right, (((0,), (0,)), ((), ())), preferred_element_type=jnp.float32
    )


def back_through(grad, weight_matrix):
    return lax.dot_general(
        grad, weight_matrix, (((1,), (1,)), ((), ())), preferred_element_type=jnp.float32
    )


def general_plan(
    tokens,
    cotangent,
    lengths,
    ln1_gain,
    ln1_bias,
    ln2_gain,
    ln2_bias,
    w_qkv,
    b_qkv,
    w_out_attn,
    b_out_attn,
    w_in,
    b_in,
    w_out,
    b_out,
):
    blocks = lax.axis_size("blk")
    block_here = lax.axis_index("blk")
    inputs = tokens[0].astype(jnp.float32)
    rows_here = inputs.shape[0]
    width = inputs.shape[1]
    scale = HEAD ** (-0.5)
    query_positions = block_here * rows_here + jnp.arange(rows_here, dtype=jnp.int32)
    row_lengths = lengths[0]
    ends = jnp.cumsum(row_lengths)
    doc_starts = ends - row_lengths
    query_docs = document_of(query_positions, ends)
    doc_numbers = jnp.arange(DOCS, dtype=jnp.int32)
    member = (query_docs[:, None] == doc_numbers[None, :]).astype(jnp.float32)
    earliest = jnp.sum(jnp.where(doc_numbers == query_docs[0], doc_starts, 0))
    last_query = query_positions[rows_here - 1]
    token_length = jnp.sum(member * row_lengths.astype(jnp.float32)[None, :], axis=1)
    weight = jnp.sqrt(TOK_DEV / token_length)
    half = ROT // 2
    frequency = 10000.0 ** (-(jnp.arange(half, dtype=jnp.float32) * 2.0) / ROT)
    angle = query_positions.astype(jnp.float32)[:, None] * frequency[None, :]
    cosine = jnp.concatenate([jnp.cos(angle), jnp.cos(angle)], axis=-1)[:, None, :]
    sine = jnp.concatenate([jnp.sin(angle), jnp.sin(angle)], axis=-1)[:, None, :]
    gain_one = ln1_gain.astype(jnp.float32)
    shift_one = ln1_bias.astype(jnp.float32)
    gain_two = ln2_gain.astype(jnp.float32)
    shift_two = ln2_bias.astype(jnp.float32)
    normed_one = layer_norm(inputs, gain_one, shift_one).astype(jnp.bfloat16)
    projected = jnp.dot(normed_one, w_qkv, preferred_element_type=jnp.float32) + b_qkv.astype(
        jnp.float32
    )
    query_raw = projected[:, :width].reshape(rows_here, HEADS, HEAD)
    key_raw = projected[:, width : 2 * width].reshape(rows_here, HEADS, HEAD)
    queries = rotate(query_raw, cosine, sine).astype(jnp.bfloat16)
    keys_rotated = rotate(key_raw, cosine, sine).reshape(rows_here, width)
    keys_values = jnp.concatenate([keys_rotated, projected[:, 2 * width :]], axis=1).astype(
        jnp.bfloat16
    )

    def useful(first_row, count):
        return (first_row <= last_query) & (first_row + count > earliest)

    def masked_scores(kv_piece, first_row):
        count = kv_piece.shape[0]
        key_block = kv_piece[:, :width].reshape(count, HEADS, HEAD)
        value_block = kv_piece[:, width:].reshape(count, HEADS, HEAD)
        key_positions = first_row + jnp.arange(count, dtype=jnp.int32)
        key_docs = document_of(key_positions, ends)
        allowed = (query_docs[:, None] == key_docs[None, :]) & (
            key_positions[None, :] <= query_positions[:, None]
        )
        scores = (
            jnp.einsum("qhd,khd->qhk", queries, key_block, preferred_element_type=jnp.float32)
            * scale
        )
        return (jnp.where(allowed[:, None, :], scores, -jnp.inf), key_block, value_block)

    initial = (
        jnp.full((rows_here, HEADS), -1e30, jnp.float32),
        jnp.zeros((rows_here, HEADS), jnp.float32),
        jnp.zeros((rows_here, HEADS, HEAD), jnp.float32),
    )
    kv_piece = lax.all_gather(keys_values, "blk", axis=0, tiled=True)
    first_row = jnp.int32(0)

    def fold_work(state):
        row_max, denominator, accum = state
        scores, key_block, value_block = masked_scores(kv_piece, first_row)
        new_max = jnp.maximum(row_max, jnp.max(scores, axis=-1))
        expo = jnp.exp(scores - new_max[..., None])
        denominator = jnp.sum(expo, axis=-1)
        accum = jnp.einsum(
            "qhk,khd->qhd",
            expo.astype(jnp.bfloat16),
            value_block,
            preferred_element_type=jnp.float32,
        )
        return (new_max, denominator, accum)

    row_max, denominator, accum = lax.cond(
        useful(first_row, kv_piece.shape[0]), fold_work, lambda state: state, initial
    )
    log_total = row_max + jnp.log(denominator)
    attended_full = accum / denominator[..., None]
    attended = attended_full.reshape(rows_here, width).astype(jnp.bfloat16)
    attn_branch = jnp.dot(
        attended, w_out_attn, preferred_element_type=jnp.float32
    ) + b_out_attn.astype(jnp.float32)
    normed_two = layer_norm(inputs, gain_two, shift_two).astype(jnp.bfloat16)
    hidden = jnp.dot(normed_two, w_in, preferred_element_type=jnp.float32) + b_in.astype(
        jnp.float32
    )
    activated = jax.nn.gelu(hidden, approximate=False).astype(jnp.bfloat16)
    mlp_branch = jnp.dot(activated, w_out, preferred_element_type=jnp.float32) + b_out.astype(
        jnp.float32
    )
    layer_out = (inputs + attn_branch + mlp_branch).astype(jnp.bfloat16)
    out_grad = cotangent[0].astype(jnp.float32) * weight[:, None]
    branch_grad = out_grad.astype(jnp.bfloat16)
    branch_bias_grad = jnp.sum(branch_grad.astype(jnp.float32), axis=0)
    w_out_grad = inner(activated, branch_grad)
    activated_grad = back_through(branch_grad, w_out)
    unused, gelu_back = jax.vjp(lambda value: jax.nn.gelu(value, approximate=False), hidden)
    hidden_grad = gelu_back(activated_grad)[0].astype(jnp.bfloat16)
    w_in_grad = inner(normed_two, hidden_grad)
    b_in_grad = jnp.sum(hidden_grad.astype(jnp.float32), axis=0)
    normed_two_grad = back_through(hidden_grad, w_in)
    unused, norm_two_back = jax.vjp(layer_norm, inputs, gain_two, shift_two)
    input_two, gain_two_grad, shift_two_grad = norm_two_back(normed_two_grad)
    w_out_attn_grad = inner(attended, branch_grad)
    attended_grad = (
        back_through(branch_grad, w_out_attn).astype(jnp.bfloat16).reshape(rows_here, HEADS, HEAD)
    )
    delta = jnp.sum(attended_grad.astype(jnp.float32) * attended_full, axis=-1)
    gathered = lax.all_gather(keys_values, "blk", axis=0, tiled=True)

    def pair_terms_of(scores, value_block, grad_side, lse_side, delta_side):
        weights = jnp.exp(scores - lse_side[..., None])
        weight_grad = jnp.einsum(
            "qhd,khd->qhk", grad_side, value_block, preferred_element_type=jnp.float32
        )
        score_grad = (weights * (weight_grad - delta_side[..., None])).astype(jnp.bfloat16)
        return (weights, score_grad)

    def block_back(query_grad, block_index):
        first_row = block_index * rows_here
        kv_piece = lax.dynamic_slice_in_dim(gathered, first_row, rows_here, 0)

        def block_work(query_grad):
            scores, key_block, value_block = masked_scores(kv_piece, first_row)
            weights, score_grad = pair_terms_of(
                scores, value_block, attended_grad, log_total, delta
            )
            query_grad = (
                query_grad
                + jnp.einsum(
                    "qhk,khd->qhd", score_grad, key_block, preferred_element_type=jnp.float32
                )
                * scale
            )
            key_grad = (
                jnp.einsum("qhk,qhd->khd", score_grad, queries, preferred_element_type=jnp.float32)
                * scale
            )
            value_grad = jnp.einsum(
                "qhk,qhd->khd",
                weights.astype(jnp.bfloat16),
                attended_grad,
                preferred_element_type=jnp.float32,
            )
            pair_grad = jnp.concatenate(
                [key_grad.reshape(rows_here, width), value_grad.reshape(rows_here, width)], axis=1
            )
            return (query_grad, pair_grad)

        def skipped(query_grad):
            return (query_grad, jnp.zeros((rows_here, 2 * width), jnp.float32))

        return lax.cond(useful(first_row, rows_here), block_work, skipped, query_grad)

    query_grad, pair_terms = lax.scan(
        block_back,
        jnp.zeros((rows_here, HEADS, HEAD), jnp.float32),
        jnp.arange(blocks, dtype=jnp.int32),
    )
    pair_grads = lax.psum_scatter(
        pair_terms.reshape(blocks * rows_here, 2 * width).astype(jnp.bfloat16),
        "blk",
        scatter_dimension=0,
        tiled=True,
    ).astype(jnp.float32)
    unused, rotate_back = jax.vjp(lambda value: rotate(value, cosine, sine), query_raw)
    query_raw_grad = rotate_back(query_grad)[0].reshape(rows_here, width)
    key_raw_grad = rotate_back(pair_grads[:, :width].reshape(rows_here, HEADS, HEAD))[0].reshape(
        rows_here, width
    )
    projected_grad = jnp.concatenate(
        [query_raw_grad, key_raw_grad, pair_grads[:, width:]], axis=1
    ).astype(jnp.bfloat16)
    w_qkv_grad = inner(normed_one, projected_grad)
    b_qkv_grad = jnp.sum(projected_grad.astype(jnp.float32), axis=0)
    normed_one_grad = back_through(projected_grad, w_qkv)
    unused, norm_one_back = jax.vjp(layer_norm, inputs, gain_one, shift_one)
    input_one, gain_one_grad, shift_one_grad = norm_one_back(normed_one_grad)
    input_grad = out_grad + input_one + input_two
    squares = jnp.sum(input_grad * input_grad, axis=1)
    doc_local = jnp.sum(member * squares[:, None], axis=0)
    doc_norms = lax.psum(doc_local, "blk") * (row_lengths.astype(jnp.float32) / TOK_DEV)
    summed = (
        lax.psum_scatter(gain_one_grad, ("dp", "blk"), scatter_dimension=0, tiled=True),
        lax.psum_scatter(shift_one_grad, ("dp", "blk"), scatter_dimension=0, tiled=True),
        lax.psum_scatter(gain_two_grad, ("dp", "blk"), scatter_dimension=0, tiled=True),
        lax.psum_scatter(shift_two_grad, ("dp", "blk"), scatter_dimension=0, tiled=True),
        lax.psum_scatter(w_qkv_grad, ("dp", "blk"), scatter_dimension=0, tiled=True),
        lax.psum_scatter(b_qkv_grad, ("dp", "blk"), scatter_dimension=0, tiled=True),
        lax.psum_scatter(w_out_attn_grad, ("dp", "blk"), scatter_dimension=0, tiled=True),
        lax.psum_scatter(branch_bias_grad, ("dp", "blk"), scatter_dimension=0, tiled=True),
        lax.psum_scatter(w_in_grad, ("dp", "blk"), scatter_dimension=0, tiled=True),
        lax.psum_scatter(b_in_grad, ("dp", "blk"), scatter_dimension=0, tiled=True),
        lax.psum_scatter(w_out_grad, ("dp", "blk"), scatter_dimension=0, tiled=True),
        lax.psum_scatter(branch_bias_grad, ("dp", "blk"), scatter_dimension=0, tiled=True),
    )
    return (
        layer_out[None],
        input_grad.astype(jnp.bfloat16)[None],
        summed[0],
        summed[1],
        summed[2],
        summed[3],
        summed[4],
        summed[5],
        summed[6],
        summed[7],
        summed[8],
        summed[9],
        summed[10],
        summed[11],
        doc_norms[None],
    )


NT = (((1,), (1,)), ((), ()))
TN = (((0,), (0,)), ((), ()))
NN = (((1,), (0,)), ((), ()))
F32 = jnp.float32
BF16 = jnp.bfloat16
MASKED = -1e30
PEAK = 1.15e9
HALF = ROT // 2
EXTRA = 16
HERE, PAIR, CORE, GROUP, XBIT, ZLOW, ZHIGH, LENS = 0, 1, 2, 3, 4, 5, 6, 7


def mxu(left, right, dims=NN):
    return lax.dot_general(left, right, dims, preferred_element_type=F32)


def exact(left, right):
    return lax.dot_general(
        left, right, NN, precision=lax.Precision.HIGHEST, preferred_element_type=F32
    )


def row_of(ref):
    return ref[...].astype(F32).reshape(1, -1)


def token_weight(meta, pos):
    lens = [meta[LENS + d] for d in range(DOCS)]
    length = jnp.full(pos.shape, lens[DOCS - 1], jnp.int32)
    end = lens[0]
    ends = [end]
    for d in range(1, DOCS - 1):
        end = end + lens[d]
        ends.append(end)
    for d in reversed(range(DOCS - 1)):
        length = jnp.where(pos < ends[d], lens[d], length)
    return jnp.sqrt(TOK_DEV / length.astype(F32))


def doc_bounds(meta, length):
    ends = [meta[LENS]]
    for d in range(1, DOCS - 1):
        ends.append(ends[-1] + meta[LENS + d])
    return [0] + ends, ends + [length]


def column(first, count):
    return first + lax.broadcasted_iota(jnp.int32, (count, 1), 0)


def standard(x):
    mean = jnp.mean(x, axis=-1, keepdims=True)
    centered = x - mean
    variance = jnp.mean(centered * centered, axis=-1, keepdims=True)
    rate = lax.rsqrt(variance + epsilon)
    return centered * rate, rate


def call(kernel, name, meta, operands, outs, cost_us, scratch=(), vmem=6, after=(), hold=(), far=(), aliases={}):
    inside = pl.BlockSpec(memory_space=pltpu.VMEM)
    scalars = pl.BlockSpec(memory_space=pltpu.SMEM)
    used = 1 + len(operands)
    idle = len(after) + len(hold)

    def body(*refs):
        kernel(*refs[:used], *refs[used + idle :])

    return pl.pallas_call(
        body,
        in_specs=[scalars]
        + [pl.BlockSpec(memory_space=pltpu.HBM) if k in far else inside for k in range(len(operands))]
        + [inside] * len(hold)
        + [pl.BlockSpec(memory_space=pl.ANY)] * len(after),
        out_specs=[scalars if o.shape == (1,) else inside for o in outs],
        out_shape=outs,
        scratch_shapes=list(scratch),
        input_output_aliases=aliases,
        compiler_params=pltpu.CompilerParams(vmem_limit_bytes=vmem << 20),
        cost_estimate=cost(cost_us),
        name=name,
    )(meta, *operands, *hold, *after)


def cost(us):
    return pl.CostEstimate(flops=int(us * PEAK), bytes_accessed=0, transcendentals=0)


def shape(dims, dtype=BF16):
    return jax.ShapeDtypeStruct(tuple(dims), dtype)


def all_of(array):
    rank = array.ndim
    return pl.BlockSpec(array.shape, lambda *_: (0,) * rank)


def weights_kernel(meta, w_ref, b_ref, wt_ref, bias_ref, columns, flat_ref, row_ref, sems):
    span = wt_ref.shape[0] // 3
    width = wt_ref.shape[1]
    first = meta[GROUP] * span
    odd = (meta[GROUP] % 2) == 1

    def place(part):
        return pl.ds(pl.multiple_of(part * width + (first // 128) * 128, 128), 256)

    copies = [
        pltpu.make_async_copy(w_ref.at[:, place(part)], columns.at[part], sems.at[part]) for part in range(3)
    ]
    copies.append(pltpu.make_async_copy(b_ref, flat_ref, sems.at[3]))
    for copy in copies:
        copy.start()
    for copy in copies:
        copy.wait()
    row_ref[...] = row_of(flat_ref)

    def rows(part, bias):
        both = (jnp.broadcast_to(row_ref[:, place(part)], (8, 256)) if bias else columns[part]).T
        return jnp.where(odd, both[HEAD : HEAD + span], both[:span])

    for out, bias in ((wt_ref, False), (bias_ref, True)):
        queries, keys, values = (rows(part, bias) for part in range(3))
        pieces = []
        for h in range(span // HEAD):
            head = slice(h * HEAD, (h + 1) * HEAD)
            pieces += [keys[head], values[head]]
        whole = jnp.concatenate(pieces + [queries], axis=0)
        out[...] = whole[:, 0:1] if bias else whole


def prepare_weights(meta, w_qkv, b_qkv):
    width, total = w_qkv.shape
    features = total // 4
    return call(
        weights_kernel,
        "weights",
        meta,
        [w_qkv, b_qkv],
        [shape((features, width)), shape((features, 1), F32)],
        2,
        scratch=[
            pltpu.VMEM((3, width, 256), BF16),
            pltpu.VMEM((total,), BF16),
            pltpu.VMEM((1, total), F32),
            pltpu.SemaphoreType.DMA((4,)),
        ],
        far=(0, 1),
    )


def queries_keys_values(place, cols, normed, wt_ref, bias, cos_ref, sin_ref, out_ref):
    count = normed.shape[0]
    out = mxu(wt_ref[...], normed, NT) + bias[...]
    at = pl.ds(pl.multiple_of(place, count), count)
    cosine, sine = cos_ref[:, at], sin_ref[:, at]
    heads = out_ref.shape[0] // (3 * HEAD)
    out_ref[:, cols] = out.astype(BF16)
    starts = [2 * HEAD * h for h in range(heads)] + [2 * HEAD * heads + HEAD * h for h in range(heads)]
    for row in starts:
        first, second = out[row : row + HALF], out[row + HALF : row + ROT]
        turned = jnp.concatenate([first * cosine - second * sine, second * cosine + first * sine], axis=0)
        out_ref[row : row + ROT, cols] = turned.astype(BF16)


def project_kernel(meta, pair_x, far_x, gain, shift, wt_ref, bias, cos_ref, sin_ref, qkv_pair, qkv_far, normed_pair, normed_far):
    rows = pair_x.shape[0]
    for j, (x_ref, qkv_ref, normed_ref) in enumerate(((pair_x, qkv_pair, normed_pair), (far_x, qkv_far, normed_far))):
        scaled, _ = standard(x_ref[...].astype(F32))
        normed = (scaled * row_of(gain) + row_of(shift)).astype(BF16)
        normed_ref[...] = normed.T
        place = (meta[HERE] ^ (2 + j)) * rows
        queries_keys_values(place, slice(None), normed, wt_ref, bias, cos_ref, sin_ref, qkv_ref)


def project(meta, pair_x, far_x, projection, hold):
    rows, width = pair_x.shape
    features = projection[2].shape[0]
    return call(
        project_kernel,
        "project",
        meta,
        [pair_x, far_x, *projection],
        [shape((features, rows))] * 2 + [shape((width, rows))] * 2,
        4,
        hold=hold,
    )


def attended_grad_kernel(meta, own_ct, core_ct, w_ref, mine_ref, send_ref, rows_ref, sem):
    rows = own_ct.shape[0]
    span = mine_ref.shape[0]
    core, pair = meta[CORE], meta[PAIR]
    half = pl.ds(pl.multiple_of(core * 2 * span, 2 * span), 2 * span)
    copy = pltpu.make_async_copy(w_ref.at[half, :], rows_ref, sem)
    copy.start()
    copy.wait()
    for b in range(2):
        ct = jnp.where(core == b, own_ct[...], core_ct[...]).astype(F32)
        grad = (ct * token_weight(meta, column((2 * pair + b) * rows, rows))).astype(BF16)
        both = mxu(rows_ref[...], grad, NT).astype(BF16)
        cols = slice(b * rows, (b + 1) * rows)
        mine_ref[:, cols] = jnp.where(pair == 0, both[:span], both[span:])
        send_ref[:, cols] = jnp.where(pair == 0, both[span:], both[:span])


def attended_grad(meta, own_ct, core_ct, w_out_attn, hold):
    rows, width = own_ct.shape
    span = width // 4
    return call(
        attended_grad_kernel,
        "attended_grad",
        meta,
        [own_ct, core_ct, w_out_attn],
        [shape((span, 2 * rows)), shape((span, 2 * rows)), shape((2 * span, width))],
        2,
        scratch=[pltpu.SemaphoreType.DMA],
        hold=hold,
        far=(2,),
    )


def hidden_kernel(
    meta,
    own_x,
    core_x,
    own_ct,
    core_ct,
    gain,
    shift,
    win_ref,
    bin_ref,
    wout_ref,
    gain_one,
    shift_one,
    wt_ref,
    bias,
    cos_ref,
    sin_ref,
    act_ref,
    hid_ref,
    grad_ref,
    turned_ref,
    scaled_ref,
    bin_grad_ref,
    branch_sum_ref,
    qkv_own,
    qkv_core,
    normed_own,
    normed_core,
    win_half,
    wout_half,
    bin_row,
    sems,
):
    rows, width = own_x.shape
    hidden_size = win_ref.shape[1] // 2
    chunk = 256
    base = pl.multiple_of(meta[CORE] * hidden_size, hidden_size)
    copies = [
        pltpu.make_async_copy(win_ref.at[:, pl.ds(base, hidden_size)], win_half, sems.at[0]),
        pltpu.make_async_copy(wout_ref.at[pl.ds(base, hidden_size), :], wout_half, sems.at[1]),
    ]
    for copy in copies:
        copy.start()
    bin_row[...] = row_of(bin_ref)
    branch_sum_ref[...] = jnp.zeros_like(branch_sum_ref)
    inputs = ((own_x, own_ct, qkv_own, normed_own), (core_x, core_ct, qkv_core, normed_core))
    totals = []
    for block, (x_ref, ct_ref, qkv_ref, normed_ref) in enumerate(inputs):
        at = slice(block * rows, (block + 1) * rows)
        place = (meta[HERE] ^ block) * rows
        scaled, _ = standard(x_ref[...].astype(F32))
        scaled_ref[at, :] = scaled
        normed = (scaled * row_of(gain_one) + row_of(shift_one)).astype(BF16)
        normed_ref[...] = normed.T
        queries_keys_values(place, slice(None), normed, wt_ref, bias, cos_ref, sin_ref, qkv_ref)
        normed = (scaled * row_of(gain) + row_of(shift)).astype(BF16)
        turned_ref[:, at] = normed.T
        grad = (ct_ref[...].astype(F32) * token_weight(meta, column(place, rows))).astype(BF16)
        grad_ref[at, :] = grad
        if block == 0:
            branch_sum_ref[0:1, :] = jnp.sum(grad.astype(F32), axis=0, keepdims=True)
        if block == 0:
            for copy in copies:
                copy.wait()
        sums = []
        for j in range(0, hidden_size, chunk):
            cols = slice(j, j + chunk)
            there = pl.ds(pl.multiple_of(base + j, 128), chunk)
            hidden = mxu(normed, win_half[:, cols]) + bin_row[:, there]
            back = mxu(grad, wout_half[cols, :], NT)
            below = 0.5 + 0.5 * lax.erf(hidden * (0.5**0.5))
            bell = jnp.exp(hidden * hidden * -0.5) * 0.3989422804014327
            act_ref[at, cols] = (hidden * below).astype(BF16)
            rounded = (back * (below + hidden * bell)).astype(BF16)
            hid_ref[at, cols] = rounded
            sums.append(jnp.sum(rounded.astype(F32), axis=0, keepdims=True))
        totals.append(jnp.concatenate(sums, axis=1))
    bin_grad_ref[...] = totals[0] + totals[1]


def hidden_part(meta, own_x, core_x, own_ct, core_ct, gain, shift, w_in, b_in, w_out, projection, hold):
    rows, width = own_x.shape
    hidden_size = w_in.shape[1] // 2
    features = projection[2].shape[0]
    outs = [
        shape((2 * rows, hidden_size)),
        shape((2 * rows, hidden_size)),
        shape((2 * rows, width)),
        shape((width, 2 * rows)),
        shape((2 * rows, width), F32),
        shape((1, hidden_size), F32),
        shape((8, width), F32),
        shape((features, rows)),
        shape((features, rows)),
        shape((width, rows)),
        shape((width, rows)),
        shape((width, hidden_size)),
        shape((hidden_size, width)),
    ]
    operands = [own_x, core_x, own_ct, core_ct, gain, shift, w_in, b_in, w_out, *projection]
    return call(
        hidden_kernel,
        "hidden",
        meta,
        operands,
        outs,
        13,
        scratch=[pltpu.VMEM((1, 2 * hidden_size), F32), pltpu.SemaphoreType.DMA((2,))],
        vmem=8,
        hold=hold,
        far=(6, 8),
    )


def out_grad_kernel(meta, act_ref, grad_ref, x_ref, send_ref, keep_ref, again_ref):
    again_ref[...] = x_ref[...]
    quarter = send_ref.shape[0] // 2
    part = quarter // 2
    grad = grad_ref[...]
    for ref, bit in ((send_ref, 1 - meta[XBIT]), (keep_ref, meta[XBIT])):
        for z in range(2):
            there = pl.ds(pl.multiple_of((2 * z + bit) * quarter, quarter), quarter)
            found = mxu(act_ref[:, there], grad, TN).astype(BF16)
            for p in range(2):
                ref[(2 * p + z) * part : (2 * p + z + 1) * part, :] = found[p * part : (p + 1) * part]


def out_grad(meta, act, grad, x, hold):
    half = shape((act.shape[1] // 2, grad.shape[1]))
    return call(out_grad_kernel, "w_out_grad", meta, [act, grad, x], [half, half, shape(x.shape)], 3, hold=hold)


def in_grad_kernel(
    meta, act_ref, hid_ref, turned_ref, scaled_ref, gain, win_ref, wout_ref, branch_ref, term_ref, send_ref, keep_ref, small_ref
):
    width = win_ref.shape[0]
    fine = width // 16
    for ref, bit in ((send_ref, 1 - meta[ZLOW]), (keep_ref, meta[ZLOW])):
        pieces = []
        for xb in range(2):
            for p in range(2):
                for zh in range(2):
                    source = (4 * zh + 2 * bit + xb) * 2 * fine + p * fine
                    pieces.append(turned_ref[pl.ds(pl.multiple_of(source, fine), fine), :])
        ref[...] = mxu(jnp.concatenate(pieces, axis=0), hid_ref[...]).astype(BF16)
    rows = act_ref.shape[0] // 2
    small_ref[...] = jnp.zeros_like(small_ref)
    for block in range(2):
        at = slice(block * rows, (block + 1) * rows)
        branch_ref[at, :] = mxu(act_ref[at, :], wout_ref[...]).astype(BF16)
        normed_grad = mxu(hid_ref[at, :], win_ref[...], NT)
        term_ref[at, :] = (normed_grad * row_of(gain)).astype(BF16)
        small_ref[0:1, :] += jnp.sum(normed_grad * scaled_ref[at, :], axis=0, keepdims=True)
        small_ref[1:2, :] += jnp.sum(normed_grad, axis=0, keepdims=True)


def in_grad(meta, act, hid, turned, scaled, gain, w_in, w_out, hold):
    tokens, hidden_size = act.shape
    width = w_in.shape[0]
    outs = [
        shape((tokens, width)),
        shape((tokens, width)),
        shape((width // 2, hidden_size)),
        shape((width // 2, hidden_size)),
        shape((8, width), F32),
    ]
    return call(
        in_grad_kernel,
        "w_in_grad",
        meta,
        [act, hid, turned, scaled, gain, w_in, w_out],
        outs,
        9,
        hold=hold,
    )


def three(value):
    a = value.astype(BF16).astype(F32)
    rest = value - a
    b = rest.astype(BF16).astype(F32)
    return a, b, rest - b


def placer(meta, blocks):
    here, pair = meta[HERE], meta[PAIR]

    def placed(rows, b):
        low = here % 2 == b % 2
        near = jnp.where(low, blocks[0][rows, :], blocks[1][rows, :])
        far = jnp.where(low, blocks[2][rows, :], blocks[3][rows, :])
        return jnp.where(pair == b // 2, near, far)

    return placed


def beside(runs):
    current, first, second = runs[0]
    for _ in range(first):
        next(current)
    for n, (current, _, second) in enumerate(runs):
        following, total = (runs[n + 1][0], runs[n + 1][1]) if n + 1 < len(runs) else (None, 0)
        done = 0
        for i in range(second):
            next(current)
            while done < (i + 1) * total // second:
                next(following)
                done += 1
        for _ in current:
            raise ValueError("steps")


def tile_rows(v, tile):
    return tile * (v * (v + 1) // 2)


def forward_kernel(
    chosen, meta, b0, b1, b2, b3, do_near, do_far, near_ref, far_ref, p_first, p_last, do_ref, out_ref, ka_ref, vt_ref, s_ref
):
    tile = b0.shape[1]
    length = 4 * tile
    heads = do_near.shape[0] // HEAD
    step = tile // 2
    scale = HEAD ** (-0.5)
    pair = meta[PAIR]
    lows, highs = doc_bounds(meta, length)
    placed = placer(meta, (b0, b1, b2, b3))

    pos = lax.broadcasted_iota(jnp.int32, (EXTRA, length), 1)
    row = lax.broadcasted_iota(jnp.int32, (EXTRA, length), 0)
    inside = jnp.zeros(pos.shape, jnp.bool_)
    for d in range(DOCS):
        inside = inside | ((row == d) & (pos >= lows[d]) & (pos < highs[d]))
    key_rows = jnp.where(inside, 1.0, 0.0).astype(BF16)
    one_rows = jnp.where(row[:, :tile] < 3, 1.0, 0.0).astype(BF16)
    query_rows = jnp.where((row < DOCS) & jnp.logical_not(inside), MASKED, 0.0).astype(BF16)
    fill = jnp.zeros((HEAD - EXTRA, tile), BF16)
    for n, head in enumerate(chosen):
        for b in range(4):
            cols = slice(b * tile, (b + 1) * tile)
            kv = placed(slice(2 * HEAD * head, 2 * HEAD * (head + 1)), b)
            ka_ref[n, cols, :] = jnp.concatenate([kv[:HEAD], key_rows[:, cols], fill], axis=0).T
            vt_ref[n, :, cols] = jnp.concatenate([kv[HEAD:], one_rows], axis=0)
    extra_row = lax.broadcasted_iota(jnp.int32, (EXTRA, tile), 0)
    offset = lax.broadcasted_iota(jnp.int32, (step, tile), 0) - lax.broadcasted_iota(jnp.int32, (step, tile), 1)

    def run(n, v, buf):
        head = chosen[n]
        p_ref, m = (p_last, 0) if n == len(chosen) - 1 else (p_first, n)
        of_head = slice(head * HEAD, (head + 1) * HEAD)
        q_rows = slice(HEAD * (2 * heads + head), HEAD * (2 * heads + head + 1))
        chunks = (v + 1) * tile // step
        first_row = tile_rows(v, tile)
        cols = slice(v * tile, (v + 1) * tile)
        low = lambda k: max(0, k * step - v * tile)
        q_t = placed(q_rows, v) * jnp.asarray(scale, BF16)
        half = slice((v % 2) * tile, (v % 2 + 1) * tile)
        do_t = jnp.where(pair == v // 2, do_near[of_head, half], do_far[of_head, half])
        q_aug = jnp.concatenate([q_t, query_rows[:, cols], fill], axis=0)
        top = jnp.full((1, tile), MASKED, F32)
        for k in range(chunks):
            rows, l = slice(k * step, (k + 1) * step), low(k)
            scores = mxu(ka_ref[n, rows, :], q_aug[:, l:])
            if (k + 1) * step > v * tile:
                scores = jnp.where(offset[:, l:] <= v * tile - k * step, scores, MASKED)
            s_ref[buf, rows, l:] = scores
            peak = jnp.max(scores, axis=0, keepdims=True)
            if l:
                top = jnp.concatenate([top[:, :l], jnp.maximum(top[:, l:], peak)], axis=1)
            else:
                top = jnp.maximum(top, peak)
            yield
        for k in range(chunks):
            rows, l = slice(k * step, (k + 1) * step), low(k)
            to = slice(first_row + k * step, first_row + (k + 1) * step)
            p_ref[m, to, l:] = jnp.exp(s_ref[buf, rows, l:] - top[:, l:]).astype(BF16)
            yield
        lanes = [(g * step, v * tile + (g + 1) * step) for g in range(tile // step)]
        out_all = jnp.concatenate(
            [mxu(vt_ref[n, :, :w], p_ref[m, first_row : first_row + w, l : l + step]) for l, w in lanes], axis=1
        )
        inverse = 1.0 / out_all[HEAD : HEAD + 1]
        out_t = out_all[:HEAD] * inverse
        out_ref[(v // 2) ^ pair, n * HEAD : (n + 1) * HEAD, half] = out_t.astype(BF16)
        do_scaled = (do_t.astype(F32) * inverse).astype(BF16)
        delta = jnp.sum(do_scaled.astype(F32) * out_t, axis=0, keepdims=True)
        a, b, c = three(-delta)
        terms = jnp.where(extra_row == 0, a, jnp.where(extra_row == 1, b, jnp.where(extra_row == 2, c, 0.0)))
        do_ref[n, :, cols] = jnp.concatenate([do_scaled, terms.astype(BF16), fill], axis=0)
        yield

    tiles = length // tile
    beside(
        [
            (run(n, v, v % 2), (v + 1) * tile // step, (v + 1) * tile // step + 1)
            for n in range(len(chosen))
            for v in reversed(range(tiles))
        ]
    )
    near_ref[...] = out_ref[0]
    far_ref[...] = out_ref[1]


def attend_forward(meta, chosen, blocks, do_near, do_far, hold):
    rows = blocks[0].shape[1]
    length = 4 * rows
    count = len(chosen)
    return call(
        functools.partial(forward_kernel, chosen),
        "attend%d" % chosen[0],
        meta,
        [*blocks, do_near, do_far],
        [shape((count * HEAD, 2 * rows))] * 2
        + [shape((c, tile_rows(4, rows), rows)) for c in (count - 1, 1)]
        + [shape((count, 2 * HEAD, length))],
        4 * count,
        hold=hold,
        scratch=[
            pltpu.VMEM((2, count * HEAD, 2 * rows), BF16),
            pltpu.VMEM((count, length, 2 * HEAD), BF16),
            pltpu.VMEM((count, HEAD + EXTRA, length), BF16),
            pltpu.VMEM((2, length, rows), F32),
        ],
        vmem=12,
    )


def backward_kernel(
    chosen, meta, b0, b1, b2, b3, p_ref, do_ref, cos_ref, sin_ref, dq_ref, dkv_ref, kt_ref, va_ref, d_ref, acc_ref
):
    tile = b0.shape[1]
    length = 4 * tile
    heads = b0.shape[0] // (3 * HEAD)
    step = tile // 2
    scale = HEAD ** (-0.5)
    pair = meta[PAIR]
    placed = placer(meta, (b0, b1, b2, b3))
    row = lax.broadcasted_iota(jnp.int32, (EXTRA, tile), 0)
    one_rows = jnp.where(row < 3, 1.0, 0.0).astype(BF16)
    fill = jnp.zeros((HEAD - EXTRA, tile), BF16)
    for n, head in enumerate(chosen):
        for b in range(4):
            cols = slice(b * tile, (b + 1) * tile)
            kv = placed(slice(2 * HEAD * head, 2 * HEAD * (head + 1)), b)
            kt_ref[n, :, cols] = kv[:HEAD]
            va_ref[n, cols, :] = jnp.concatenate([kv[HEAD:], one_rows, fill], axis=0).T
    per_half = 2 * tile
    blank = jnp.zeros((HEAD, tile), F32)

    def run(n, v, buf, widest):
        head = chosen[n]
        q_rows = slice(HEAD * (2 * heads + head), HEAD * (2 * heads + head + 1))
        width = (v + 1) * tile
        chunks = width // step
        first_row = tile_rows(v, tile)
        cols = slice(v * tile, (v + 1) * tile)
        low = lambda k: max(0, k * step - v * tile)
        for k in range(chunks):
            rows, l = slice(k * step, (k + 1) * step), low(k)
            weights = p_ref[n, first_row + k * step : first_row + (k + 1) * step, l:]
            weight_grad = mxu(va_ref[n, rows, :], do_ref[head, :, v * tile + l : (v + 1) * tile])
            d_ref[buf, rows, l:] = (weights.astype(F32) * weight_grad).astype(BF16)
            yield
        q_t = placed(q_rows, v) * jnp.asarray(scale, BF16)
        groups = [(0, v * tile, 0)] if v else []
        groups += [(v * tile + g * step, v * tile + (g + 1) * step, g * step) for g in range(tile // step)]
        for r, s, l in groups:
            value = mxu(do_ref[head, :HEAD, v * tile + l : (v + 1) * tile], p_ref[n, first_row + r : first_row + s, l:], NT)
            key = mxu(q_t[:, l:], d_ref[buf, r:s, l:], NT)
            if widest:
                acc_ref[n, HEAD:, r:s] = value
                acc_ref[n, :HEAD, r:s] = key
            else:
                acc_ref[n, HEAD:, r:s] += value
                acc_ref[n, :HEAD, r:s] += key
            yield
        lanes = [(g * step, v * tile + (g + 1) * step) for g in range(tile // step)]
        dq_t = (
            jnp.concatenate([mxu(kt_ref[n, :, :w], d_ref[buf, :w, l : l + step]) for l, w in lanes], axis=1) * scale
        )
        cosine, sine = cos_ref[:, cols], sin_ref[:, cols]
        first, second = dq_t[:HALF], dq_t[HALF:ROT]
        joined = jnp.concatenate(
            [first * cosine + second * sine, second * cosine - first * sine, dq_t[ROT:], blank], axis=0
        )
        half = slice((v % 2) * tile, (v % 2 + 1) * tile)
        dq_ref[(v // 2) ^ pair, half, n * 2 * HEAD : (n + 1) * 2 * HEAD] = joined.T.astype(BF16)
        yield

    tiles = length // tile
    beside(
        [
            (run(n, v, v % 2, v == tiles - 1), (v + 1) * tile // step, (1 if v else 0) + tile // step + 1)
            for n in range(len(chosen))
            for v in reversed(range(tiles))
        ]
    )
    cosine, sine = cos_ref[...], sin_ref[...]
    for n in range(len(chosen)):
        grads = acc_ref[n]
        first, second = grads[:HALF], grads[HALF:ROT]
        grads = jnp.concatenate(
            [first * cosine + second * sine, second * cosine - first * sine, grads[ROT:]], axis=0
        )
        for h in range(2):
            lanes = slice(n * 2 * HEAD, (n + 1) * 2 * HEAD)
            dkv_ref[h ^ pair, :, lanes] = grads[:, h * per_half : (h + 1) * per_half].T.astype(BF16)


def attend_backward(meta, chosen, blocks, weights, do, cosine, sine, hold):
    rows = blocks[0].shape[1]
    length = 4 * rows
    count = len(chosen)
    return call(
        functools.partial(backward_kernel, chosen),
        "attend_back%d" % chosen[0],
        meta,
        [*blocks, weights, do, cosine, sine],
        [shape((2, 2 * rows, 2 * HEAD * count))] * 2,
        5 * count,
        hold=hold,
        scratch=[
            pltpu.VMEM((count, HEAD, length), BF16),
            pltpu.VMEM((count, length, 2 * HEAD), BF16),
            pltpu.VMEM((2, length, rows), BF16),
            pltpu.VMEM((count, 2 * HEAD, length), F32),
        ],
        vmem=10,
    )


def branch_kernel(meta, mine_ref, theirs_ref, w_ref, branch, own_ct, core_ct, own_ref, send_ref, goa_send, goa_keep):
    pair, core = meta[PAIR], meta[CORE]
    rows = own_ref.shape[0]
    mine, theirs = mine_ref[...], theirs_ref[...]
    six = jnp.concatenate([jnp.where(pair == 0, mine, theirs), jnp.where(pair == 0, theirs, mine)], axis=0)
    own_cols = jnp.where(core == 0, six[:, :rows], six[:, rows:])
    other_cols = jnp.where(core == 0, six[:, rows:], six[:, :rows])
    half = w_ref.shape[0]
    weight = w_ref[...]
    send_ref[...] = (mxu(other_cols, weight, TN) + branch[rows:, :].astype(F32)).astype(BF16)
    own_ref[...] = mxu(own_cols, weight, TN) + branch[:rows, :].astype(F32)
    grads = []
    for j, ct in enumerate((own_ct, core_ct)):
        place = (meta[HERE] ^ j) * rows
        grads.append((ct[...].astype(F32) * token_weight(meta, column(place, rows))).astype(BF16))
    total = mxu(own_cols, grads[0]) + mxu(other_cols, grads[1])
    first, second = total[: half // 2], total[half // 2 :]
    goa_keep[...] = jnp.where(meta[ZLOW] == 0, first, second).astype(BF16)
    goa_send[...] = jnp.where(meta[ZLOW] == 0, second, first).astype(BF16)


def branch_job(mine, arrived, w_rows, branch, own_ct, core_ct):
    rows, width = own_ct.shape
    outs = [shape((rows, width), F32), shape((rows, width))] + [shape((width // 4, width))] * 2
    return branch_kernel, [mine, arrived, w_rows, branch, own_ct, core_ct], outs


def with_queries(wt_ref):
    span = wt_ref.shape[0] // 3
    pieces = [wt_ref[: 2 * span, :]]
    for h in range(span // HEAD):
        head = wt_ref[2 * span + h * HEAD : 2 * span + (h + 1) * HEAD, :]
        pieces += [head, jnp.zeros_like(head)]
    return jnp.concatenate(pieces, axis=0)


def far_kernel(meta, *refs):
    kv, qo = refs[0:2], refs[2:4]
    wt_ref, gain, send_ref, keep_ref = refs[4:]
    core = meta[CORE]
    rows = send_ref.shape[0]
    right = with_queries(wt_ref)
    for out, b in ((send_ref, 1 - core), (keep_ref, core)):
        at = pl.ds(pl.multiple_of(b * rows, rows), rows)
        left = jnp.concatenate([r[1, at, :] for r in kv] + [r[1, at, :] for r in qo], axis=1)
        out[...] = (mxu(left, right) * row_of(gain)).astype(BF16)


PIECES = 24


def weight_kernel(meta, *refs):
    kv, qo = refs[0:2], refs[2:4]
    wt_ref, gain, shift, n0, n1, n2, n3, two_ref, branch_sum, bin_ref = refs[4:14]
    send_ref, keep_ref, vector_ref = refs[14:]
    core = meta[CORE]
    width, rows = n0.shape
    features = wt_ref.shape[0]
    span = features // 3
    devices = 2 * keep_ref.shape[0]
    gain_row, shift_row = row_of(gain), row_of(shift)

    def both(half, b):
        at = pl.ds(pl.multiple_of(b * rows, rows), rows)
        return jnp.concatenate([r[half, at, :] for r in kv] + [r[half, at, :] for r in qo], axis=1)

    near_own, near_core = both(0, core), both(0, 1 - core)
    far_own, far_core = both(1, core), both(1, 1 - core)
    grad = mxu(n0[...], near_own) + mxu(n1[...], near_core) + mxu(n2[...], far_own) + mxu(n3[...], far_core)
    sums = sum(
        jnp.sum(a.astype(F32), axis=0, keepdims=True) for a in (near_own, near_core, far_own, far_core)
    )

    def tight(value):
        queries = [value[:, 2 * span + 2 * HEAD * h : 2 * span + 2 * HEAD * h + HEAD] for h in range(3)]
        return jnp.concatenate([value[:, : 2 * span]] + queries, axis=1)

    grad, sums = tight(grad), tight(sums)
    weights = wt_ref[...].T.astype(F32)
    by_weight = jnp.sum(weights * grad, axis=1, keepdims=True)
    shift_grad = jnp.sum(weights * sums, axis=1, keepdims=True)
    lane = lax.broadcasted_iota(jnp.int32, (width, 128), 1)
    turned = jnp.where(lane == 0, by_weight, jnp.where(lane == 1, shift_grad, 0.0)).T
    shift_grad = turned[1:2, :]
    gain_grad = (turned[0:1, :] - shift_row * shift_grad) / gain_row

    offset = features % 128

    def spread(vectors, place_row, place_col, pieces):
        count = vectors.shape[0]
        index = lambda place: jnp.floor((place.astype(F32) + 0.5) * (1.0 / PIECES)).astype(jnp.int32)
        device = lax.broadcasted_iota(jnp.int32, (devices, vectors.shape[1]), 0)
        owner = index(place_row)
        parts = []
        for p in range(pieces):
            chosen = owner == device * pieces + p
            for c in range(count):
                value = vectors[c : c + 1, :]
                high = value.astype(BF16)
                low = (value - high.astype(F32)).astype(BF16)
                for part in (high, low):
                    parts.append(jnp.where(chosen, part.astype(F32), 0.0))
        within = place_col - PIECES * index(place_col) + offset
        lane = lax.broadcasted_iota(jnp.int32, (vectors.shape[1], 128), 1)
        table = jnp.where(within == lane, 1.0, 0.0).astype(BF16)
        return mxu(jnp.concatenate(parts, axis=0).astype(BF16), table)

    def counted(size):
        return (
            lax.broadcasted_iota(jnp.int32, (1, size), 1),
            lax.broadcasted_iota(jnp.int32, (size, 1), 0),
        )

    def qkv_place(index):
        rest = index - 2 * span
        keys = (1 + (index // HEAD) % 2) * width + (index // (2 * HEAD)) * HEAD
        return meta[GROUP] * span + index % HEAD + jnp.where(rest < 0, keys, (rest // HEAD) * HEAD)

    lanes, sub = counted(width)
    norms = jnp.concatenate(
        [gain_grad, shift_grad, two_ref[0:1, :], two_ref[1:2, :], branch_sum[0:1, :]], axis=0
    )
    lanes_kv, sub_kv = counted(features)
    hidden_size = bin_ref.shape[1]
    lanes_in, sub_in = counted(hidden_size)
    base = core * hidden_size
    row = 0
    for found in (
        spread(norms, lanes, sub, 1),
        spread(sums, qkv_place(lanes_kv), qkv_place(sub_kv), 3),
        spread(bin_ref[...], base + lanes_in, base + sub_in, 4),
    ):
        for k in range(found.shape[0] // devices):
            vector_ref[:, row, :] = found[k * devices : (k + 1) * devices]
            row += 1
    chunk = width // devices
    whole = (features // 128) * 128
    tail = jnp.concatenate([grad[:, whole:], jnp.zeros((width, 128 - offset), F32)], axis=1)
    def piece(d):
        at = slice(d * chunk, (d + 1) * chunk)
        return jnp.concatenate([grad[at, :whole], tail[at] + vector_ref[d]], axis=1)

    for e in range(devices // 2):
        d = (e // 4 % 2) * 16 + (e // 8) * 8 + e % 4
        first, second = piece(d), piece(d + 4)
        keep_ref[e] = jnp.where(meta[XBIT] == 0, first, second)
        send_ref[e] = jnp.where(meta[XBIT] == 0, second, first).astype(BF16)


def near_kernel(meta, *refs):
    kv, qo = refs[0:2], refs[2:4]
    wt_ref, gain, term_two, far_ref, send_ref, own_ref = refs[4:]
    core = meta[CORE]
    rows = own_ref.shape[0]
    right = with_queries(wt_ref)

    def part(b):
        at = pl.ds(pl.multiple_of(b * rows, rows), rows)
        return jnp.concatenate([r[0, at, :] for r in kv] + [r[0, at, :] for r in qo], axis=1)

    gain_row = row_of(gain)
    send_ref[:rows, :] = far_ref[...]
    send_ref[rows:, :] = (mxu(part(1 - core), right) * gain_row + term_two[rows:, :].astype(F32)).astype(BF16)
    own_ref[...] = mxu(part(core), right) * gain_row + term_two[:rows, :].astype(F32)


def last_head_kernel(
    chosen,
    meta,
    b0,
    b1,
    b2,
    b3,
    p_ref,
    do_ref,
    cos_ref,
    sin_ref,
    dq_a,
    dkv_a,
    wt_ref,
    gain,
    shift,
    n0,
    n1,
    n2,
    n3,
    two_ref,
    branch_sum,
    bin_ref,
    dq_ref,
    dkv_ref,
    far_send,
    far_keep,
    g_send,
    g_keep,
    kt_ref,
    va_ref,
    d_ref,
    acc_ref,
    vector_ref,
):
    backward_kernel(
        chosen, meta, b0, b1, b2, b3, p_ref, do_ref, cos_ref, sin_ref, dq_ref, dkv_ref, kt_ref, va_ref, d_ref, acc_ref
    )
    grads = (dkv_a, dkv_ref, dq_a, dq_ref)
    far_kernel(meta, *grads, wt_ref, gain, far_send, far_keep)
    weight_kernel(
        meta, *grads, wt_ref, gain, shift, n0, n1, n2, n3, two_ref, branch_sum, bin_ref, g_send, g_keep, vector_ref
    )


def last_head(meta, chosen, blocks, weights, do, cosine, sine, earlier, wt, gain, shift, normed, vectors, devices, hold):
    rows = blocks[0].shape[1]
    length = 4 * rows
    count = len(chosen)
    width = wt.shape[1]
    lanes = -(-wt.shape[0] // 128) * 128
    chunk = width // devices
    outs = [shape((2, 2 * rows, 2 * HEAD * count))] * 2 + [shape((rows, width))] * 2
    outs += [shape((devices // 2, chunk, lanes)), shape((devices // 2, chunk, lanes), F32)]
    return call(
        functools.partial(last_head_kernel, chosen),
        "last_head",
        meta,
        [*blocks, weights, do, cosine, sine, *earlier, wt, gain, shift, *normed, *vectors],
        outs,
        12,
        hold=hold,
        scratch=[
            pltpu.VMEM((count, HEAD, length), BF16),
            pltpu.VMEM((count, length, 2 * HEAD), BF16),
            pltpu.VMEM((2, length, rows), BF16),
            pltpu.VMEM((count, 2 * HEAD, length), F32),
            pltpu.VMEM((devices, chunk, 128), F32),
        ],
        vmem=14,
    )


def near_job(dkv, dqo, wt, gain, term_two, far):
    rows, width = far.shape
    operands = [*dkv, *dqo, wt, gain, term_two, far]
    return near_kernel, operands, [shape((2 * rows, width)), shape((rows, width), F32)]


def core_sums_kernel(meta, far_ref, near_ref, arrived_ref, far_sum_ref, near_sum_ref):
    rows = far_ref.shape[0]
    far_sum_ref[...] = (far_ref[...].astype(F32) + arrived_ref[:rows, :].astype(F32)).astype(BF16)
    near_sum_ref[...] = near_ref[...] + arrived_ref[rows:, :].astype(F32)


def core_sums_job(far, near, arrived):
    return core_sums_kernel, [far, near, arrived], [shape(far.shape), shape(near.shape, F32)]


def gather_kernel(meta, r0, r2, core_ref, out_ref, *vector_refs):
    heads = HEADS // 4
    span = heads * HEAD
    width = out_ref.shape[1] // 3
    whole = ((3 * span) // 128) * 128
    here = meta[HERE]
    found = [r0[...], core_ref[0].astype(F32), r2[...], core_ref[1].astype(F32)]
    vectors = sum(value[:, whole:] for value in found)
    for s in range(4):
        low = here % 2 == s % 2
        value = jnp.where(
            here // 2 == s // 2, jnp.where(low, found[0], found[1]), jnp.where(low, found[2], found[3])
        )
        group = 2 * (s % 2) + s // 2
        for h in range(heads):
            at = group * span + h * HEAD
            out_ref[:, at : at + HEAD] = value[:, 2 * span + h * HEAD : 2 * span + (h + 1) * HEAD]
            out_ref[:, width + at : width + at + HEAD] = value[:, 2 * HEAD * h : 2 * HEAD * h + HEAD]
            out_ref[:, 2 * width + at : 2 * width + at + HEAD] = value[:, 2 * HEAD * h + HEAD : 2 * HEAD * (h + 1)]
    vectors = pltpu.roll(vectors, 128 - (3 * span) % 128, 1)
    pieces = [
        vectors[2 * k : 2 * k + 1, :PIECES] + vectors[2 * k + 1 : 2 * k + 2, :PIECES]
        for k in range(vectors.shape[0] // 2)
    ]
    again_ref, vector_refs = vector_refs[-1], vector_refs[:-1]
    again_ref[...] = pieces[4].reshape(again_ref.shape)
    k = 0
    for ref in vector_refs:
        count = ref.shape[0] // PIECES
        ref[...] = jnp.concatenate(pieces[k : k + count], axis=1).reshape(ref.shape)
        k += count


def gather_qkv(meta, parts, after):
    rows = parts[0].shape[0]
    outs = [shape((rows, 3 * HEADS * HEAD), F32)]
    outs += [shape((count * PIECES,), F32) for count in (1, 1, 1, 1, 1, 3, 4, 1)]
    return call(gather_kernel, "gather", meta, parts, outs, 0, after=after)


def layer_out_kernel(meta, x_ref, own_ref, core_ref, first, second, out_ref):
    total = x_ref[...].astype(F32) + own_ref[...] + core_ref[...].astype(F32)
    out_ref[...] = (total + (row_of(first) + row_of(second))).astype(BF16)


def last_kernel(meta, x_ref, ct_ref, near_ref, pair_ref, tokens_ref, docs_ref):
    rows = x_ref.shape[0]
    scaled, rate = standard(x_ref[...].astype(F32))
    term = near_ref[...] + pair_ref[...].astype(F32)
    back = rate * (
        term
        - jnp.mean(term, axis=-1, keepdims=True)
        - scaled * jnp.mean(term * scaled, axis=-1, keepdims=True)
    )
    pos = column(meta[HERE] * rows, rows)
    grad = ct_ref[...].astype(F32) * token_weight(meta, pos) + back
    tokens_ref[...] = grad.astype(BF16)
    squares = jnp.sum(grad * grad, axis=1, keepdims=True)
    lows, highs = doc_bounds(meta, 4 * rows)
    lane = lax.broadcasted_iota(jnp.int32, (8, 128), 1)
    docs = jnp.zeros((8, 128), F32)
    for d in range(DOCS):
        total = jnp.sum(jnp.where((pos >= lows[d]) & (pos < highs[d]), squares, 0.0), axis=0, keepdims=True)
        docs = jnp.where(lane == d, total, docs)
    docs_ref[...] = docs


def last_job(*operands):
    return last_kernel, list(operands), [shape(operands[0].shape), shape((8, 128), F32)]


def flip(value, axis, bit):
    size = lax.axis_size(axis)
    return lax.ppermute(value, axis, [(i, i ^ (1 << bit)) for i in range(size)])


def relay_kernel(places, finals, meta, *refs):
    count = len(places)
    ins, outs = refs[: 2 * count], refs[2 * count :]
    for k, (place, final) in enumerate(zip(places, finals)):
        keep, arrived = ins[2 * k], ins[2 * k + 1]
        first, second = outs[2 * k], outs[2 * k + 1]
        if final:
            total = keep[...].astype(F32) + arrived[...].astype(F32)
            first[...] = total.astype(first.dtype)
            second[...] = total
        else:
            half = first.shape[0]
            for out, bit in ((first, 1 - meta[place]), (second, meta[place])):
                at = pl.ds(pl.multiple_of(bit * half, half), half)
                out[...] = (keep[at, :].astype(F32) + arrived[at, :].astype(F32)).astype(out.dtype)


def split_kernel(meta, *refs):
    kept_ref, given_ref = refs[-2:]
    total = sum(ref[...].astype(F32) for ref in refs[:-2])
    fine = kept_ref.shape[0]
    kept_ref[...] = jnp.where(meta[CORE] == 0, total[:fine], total[fine:])
    given_ref[...] = jnp.where(meta[CORE] == 0, total[fine:], total[:fine])


def together(meta, name, jobs, after=(), hold=(), vmem=8, through=()):
    counts = [(len(operands), len(outs)) for _, operands, outs in jobs]
    inputs = sum(count for count, _ in counts) + len(through)

    def kernel(meta, *refs):
        first, out = len(through), inputs + len(through)
        for (body, _, _), (ins, outs) in zip(jobs, counts):
            body(meta, *refs[first : first + ins], *refs[out : out + outs])
            first, out = first + ins, out + outs

    found = call(
        kernel,
        name,
        meta,
        list(through) + [x for _, operands, _ in jobs for x in operands],
        [shape(x.shape, x.dtype) for x in through] + [x for _, _, outs in jobs for x in outs],
        0,
        after=after,
        hold=hold,
        vmem=vmem,
        aliases={1 + k: k for k in range(len(through))},
    )
    passed, found = found[: len(through)], found[len(through) :]
    results = []
    for _, outs in counts:
        results.append(found[:outs])
        found = found[outs:]
    return results + [passed] if through else results


def relay_job(keep, arrived, place):
    rows = keep.shape[0] if place is None else keep.shape[0] // 2
    dims = (rows,) + keep.shape[1:]
    return (
        functools.partial(relay_kernel, [place], [place is None]),
        [keep, arrived],
        [shape(dims), shape(dims, F32)],
    )


def split_job(*terms):
    rows, width = terms[0].shape
    return split_kernel, list(terms), [shape((rows // 2, width), F32)] * 2


def row_steps_kernel(meta, keep_ref, arrived_ref, send_ref, own_ref, pair_ref):
    core = meta[CORE]
    own_ref[...] = keep_ref[core]
    pair_ref[...] = arrived_ref[core].astype(F32)
    send_ref[0] = keep_ref[1 - core].astype(BF16)
    send_ref[1] = arrived_ref[1 - core]


def row_steps_job(keep, arrived):
    dims = keep.shape[1:]
    return row_steps_kernel, [keep, arrived], [shape(keep.shape), shape(dims, F32), shape(dims, F32)]


def beside_kernel(meta, mine_ref, other_ref, out_ref):
    size = mine_ref.shape[1]
    mine, other = mine_ref[...], other_ref[...]
    out_ref[:, :size] = jnp.where(meta[CORE] == 0, mine, other)
    out_ref[:, size:] = jnp.where(meta[CORE] == 0, other, mine)


def beside_job(mine, other):
    return beside_kernel, [mine, other], [shape((mine.shape[0], 2 * mine.shape[1]), F32)]


def owned_kernel(meta, mine_ref, other_ref, out_ref):
    out_ref[...] = jnp.where(meta[ZHIGH] == meta[CORE], mine_ref[...], other_ref[...])


def owned_job(mine, other):
    return owned_kernel, [mine, other], [shape(mine.shape, F32)]


def sum_job(a, b):
    return add_kernel, [a, b], [shape(a.shape, a.dtype)]


def doc_norms_kernel(meta, a_ref, b_ref, out_ref):
    lane = lax.broadcasted_iota(jnp.int32, a_ref.shape, 1)
    count = jnp.zeros(a_ref.shape, F32)
    for d in range(DOCS):
        count = jnp.where(lane == d, meta[LENS + d].astype(F32), count)
    out_ref[...] = (a_ref[...] + b_ref[...]) * (count / TOK_DEV)


def add_kernel(meta, a_ref, b_ref, out_ref):
    out_ref[...] = (a_ref[...].astype(F32) + b_ref[...].astype(F32)).astype(out_ref.dtype)


def add(meta, name, a, b, after=()):
    return call(add_kernel, name, meta, [a, b], [shape(a.shape)], 0, after=after)[0]


def head_plan(
    tokens,
    cotangent,
    lengths,
    ln1_gain,
    ln1_bias,
    ln2_gain,
    ln2_bias,
    w_qkv,
    b_qkv,
    w_out_attn,
    b_out_attn,
    w_in,
    b_in,
    w_out,
    b_out,
):
    dp_size = lax.axis_size("dp")
    here = lax.axis_index("blk").astype(jnp.int32)
    row = lax.axis_index("dp").astype(jnp.int32)
    pair, core = here // 2, here % 2
    xbit, z_low, z_high = row & 1, (row >> 1) & 1, row >> 2
    meta = jnp.concatenate([jnp.stack([here, pair, core, 2 * core + pair, xbit, z_low, z_high]), lengths[0]])
    own_x, own_ct = tokens[0], cotangent[0]
    rows, width = own_x.shape
    length = 4 * rows
    heads = HEADS // 4
    assert width == PIECES * 4 * dp_size
    positions = np.arange(length, dtype=np.float32)
    frequency = (10000.0 ** (-(np.arange(HALF, dtype=np.float32) * 2.0) / ROT)).astype(np.float32)
    angle = frequency[:, None] * positions[None, :]
    cosine, sine = jnp.asarray(np.cos(angle)), jnp.asarray(np.sin(angle))

    core_x = flip(own_x, "blk", 0)
    core_ct = flip(own_ct, "blk", 0)
    pair_x = flip(own_x, "blk", 1)

    devices = 4 * dp_size
    axes = ("dp", "blk")
    wt, bias = prepare_weights(meta, w_qkv, b_qkv)
    projection = (ln1_gain, ln1_bias, wt, bias, cosine, sine)
    do_near, do_send, w_rows = attended_grad(meta, own_ct, core_ct, w_out_attn, (wt, bias))
    do_far = flip(do_send, "blk", 1)
    (
        act,
        hid,
        grad,
        turned,
        scaled,
        b_in_grad,
        branch_sum,
        qkv_own,
        qkv_core,
        normed_own,
        normed_core,
        win_half,
        wout_half,
    ) = hidden_part(
        meta, own_x, core_x, own_ct, core_ct, ln2_gain, ln2_bias, w_in, b_in, w_out, projection, (do_near, do_send)
    )
    early = (do_near, wt, bias, qkv_own, qkv_core, normed_own, normed_core, b_in_grad, branch_sum, w_rows)
    gout_send, gout_keep, pair_again = out_grad(
        meta, act, grad, pair_x, early + (hid, turned, scaled, win_half, wout_half)
    )
    gout_x = flip(gout_send, "dp", 0)
    far_x = flip(pair_again, "blk", 0)
    branch, term_two, gin_send, gin_keep, small_two = in_grad(
        meta, act, hid, turned, scaled, ln2_gain, win_half, wout_half, early + (gout_keep,)
    )
    gin_z = flip(gin_send, "dp", 1)
    keep = (normed_own, normed_core, b_in_grad, branch_sum, w_rows, branch, term_two, small_two)
    qkv_pair, qkv_far, normed_pair, normed_far = project(
        meta, pair_x, far_x, projection, keep + (do_near, qkv_own, qkv_core, gout_keep, gin_keep)
    )
    blocks = (qkv_own, qkv_core, qkv_pair, qkv_far)
    normed = (normed_own, normed_core, normed_pair, normed_far)
    keep = keep + (wt, normed_pair, normed_far)
    near, far, weights, last_weights, do_scaled = attend_forward(
        meta, tuple(range(heads)), blocks, do_near, do_far, keep + (gout_keep, gin_keep)
    )
    arrived = flip(far, "blk", 1)
    keep = keep + (near, gout_keep)
    dq_a, dkv_a = attend_backward(
        meta, tuple(range(heads - 1)), blocks, weights, do_scaled, cosine, sine, keep + (gin_keep, last_weights)
    )
    keep = tuple(k for k in keep if k is not near and k is not w_rows and k is not branch) + (dq_a, dkv_a)
    (gin_send, gin_keep), (gout_send, gout_keep), (own_part, send_part, goa_send, goa_keep) = together(
        meta,
        "steps_one",
        [
            relay_job(gin_keep, gin_z, XBIT),
            relay_job(gout_keep, gout_x, PAIR),
            branch_job(near, arrived, w_rows, branch, own_ct, core_ct),
        ],
        hold=keep + blocks + (last_weights, do_scaled),
    )
    gin_x = flip(gin_send, "dp", 0)
    gout_p = flip(gout_send, "blk", 1)
    goa_z = flip(goa_send, "dp", 1)
    core_part = flip(send_part, "blk", 0)
    dq_b, dkv_b, far_send, far_keep, g_send, g_keep = last_head(
        meta,
        (heads - 1,),
        blocks,
        last_weights,
        do_scaled,
        cosine,
        sine,
        (dq_a, dkv_a),
        wt,
        ln1_gain,
        ln1_bias,
        normed,
        (small_two, branch_sum, b_in_grad),
        devices,
        (term_two, goa_keep, gin_keep, gout_keep, goa_send, gin_send, gout_send),
    )
    dqo, dkv = (dq_a, dq_b), (dkv_a, dkv_b)
    top = devices // 2
    to_owner = [(i, i ^ top) for i in range(devices) if i // top != i % 2]
    owners = [i for i in range(devices) if i // top == i % 2]
    (
        (gin_send, gin_keep),
        (gout_send, gout_keep),
        (goa_send, goa_keep),
        (both_send, near_own),
        (layer_out,),
        (g_send,),
    ) = together(
        meta,
        "steps_two",
        [
            relay_job(gin_keep, gin_x, PAIR),
            relay_job(gout_keep, gout_p, ZLOW),
            relay_job(goa_keep, goa_z, XBIT),
            near_job(dkv, dqo, wt, ln1_gain, term_two, far_send),
            (layer_out_kernel, [own_x, own_part, core_part, b_out_attn, b_out], [shape(own_x.shape)]),
        ],
        hold=(far_keep, g_keep),
        through=(g_send,),
    )
    both = flip(both_send, "blk", 0)
    g_x = flip(g_send, "dp", 0)
    gin_p = flip(gin_send, "blk", 1)
    gout_z = flip(gout_send, "dp", 1)
    goa_x = flip(goa_send, "dp", 0)

    (far_sum, near_sum), (gin_send, gin_keep), (gout_send, gout_keep) = together(
        meta,
        "steps_three",
        [
            core_sums_job(far_keep, near_own, both),
            relay_job(gin_keep, gin_p, ZHIGH),
            relay_job(gout_keep, gout_z, None),
        ],
        hold=(g_keep, goa_keep),
    )
    from_pair = flip(far_sum, "blk", 1)
    gin_h = flip(gin_send, "dp", 2)
    gout_o = lax.ppermute(gout_send, axes, to_owner)

    (g_send, g_keep), (goa_send, goa_keep) = together(
        meta,
        "steps_four",
        [relay_job(g_keep, g_x, ZLOW), relay_job(goa_keep, goa_x, None)],
        (far_sum,),
    )
    g_z = flip(g_send, "dp", 1)
    goa_o = lax.ppermute(goa_send, axes, to_owner)

    (g_send, g_keep), (goa_send, goa_keep), (gin_mine, gin_other), (gout_mine, gout_other) = together(
        meta,
        "steps_five",
        [
            relay_job(g_keep, g_z, ZHIGH),
            relay_job(goa_keep, goa_o, PAIR),
            split_job(gin_keep, gin_h),
            split_job(gout_keep, gout_o),
        ],
    )
    g_h = flip(g_send, "dp", 2)
    goa_p = flip(goa_send, "blk", 1)
    gin_other = flip(gin_other, "blk", 0)
    gout_other = flip(gout_other, "blk", 0)

    ((tokens_grad, docs),) = together(
        meta, "input_grad", [last_job(own_x, own_ct, near_sum, from_pair)], (gin_mine,)
    )
    docs_core = flip(docs, "blk", 0)

    (g_send, g_keep), (docs,), (goa_mine, goa_other), (w_in_grad,), (w_out_grad,) = together(
        meta,
        "steps_six",
        [
            relay_job(g_keep, g_h, PAIR),
            sum_job(docs, docs_core),
            split_job(goa_keep, goa_p),
            beside_job(gin_mine, gin_other),
            owned_job(gout_mine, gout_other),
        ],
    )
    g_p = flip(g_send, "blk", 1)
    docs_pair = flip(docs, "blk", 1)
    goa_other = flip(goa_other, "blk", 0)

    (g_send, g_own, g_pair), (doc_norms,), (w_out_attn_grad,) = together(
        meta,
        "steps_seven",
        [
            row_steps_job(g_keep, g_p),
            (doc_norms_kernel, [docs, docs_pair], [shape(docs.shape, F32)]),
            owned_job(goa_mine, goa_other),
        ],
    )
    g_core = flip(g_send, "blk", 0)
    doc_norms = doc_norms[0, :DOCS]
    w_qkv_grad, gain_one, shift_one, gain_two, shift_two, b_attn_out, b_qkv_grad, b_in_out, b_ff_out = gather_qkv(
        meta, (g_own, g_pair, g_core), ()
    )
    return (
        layer_out[None],
        tokens_grad[None],
        gain_one,
        shift_one,
        gain_two,
        shift_two,
        w_qkv_grad,
        b_qkv_grad,
        w_out_attn_grad,
        b_attn_out,
        w_in_grad,
        b_in_out,
        w_out_grad,
        b_ff_out,
        doc_norms[None],
    )


def solution(mesh):
    in_specs = (
        P("dp", "blk", None),
        P("dp", "blk", None),
        P("dp", None),
        P(),
        P(),
        P(),
        P(),
        P(),
        P(),
        P(),
        P(),
        P(),
        P(),
        P(),
        P(),
    )
    out_specs = (
        P("dp", "blk", None),
        P("dp", "blk", None),
        P(("dp", "blk")),
        P(("dp", "blk")),
        P(("dp", "blk")),
        P(("dp", "blk")),
        P(("dp", "blk"), None),
        P(("dp", "blk")),
        P(("dp", "blk"), None),
        P(("dp", "blk")),
        P(("dp", "blk"), None),
        P(("dp", "blk")),
        P(("dp", "blk"), None),
        P(("dp", "blk")),
        P("dp", None),
    )
    suits = mesh.shape["blk"] == 4 and HEADS % 4 == 0 and mesh.shape["dp"] == 8
    plan = head_plan if suits else general_plan
    return jax.shard_map(
        plan, mesh=mesh, in_specs=in_specs, out_specs=out_specs, check_vma=False
    )
```

```python
import functools

import jax
import jax.numpy as jnp
import numpy as np
from jax import lax
from jax.experimental import pallas as pl
from jax.experimental.pallas import tpu as pltpu
from jax.sharding import PartitionSpec as P

HEADS = 12
HEAD = 64
ROT = 16
DOCS = 4
TOK_DEV = 512


epsilon = 1e-05


def layer_norm(value, gain, shift):
    mean = jnp.mean(value, axis=-1, keepdims=True)
    centered = value - mean
    variance = jnp.mean(centered * centered, axis=-1, keepdims=True)
    return centered * lax.rsqrt(variance + epsilon) * gain + shift


def rotate(value, cosine, sine):
    half = ROT // 2
    rotary_part = value[..., :ROT]
    first = rotary_part[..., :half]
    second = rotary_part[..., half:]
    turned = jnp.concatenate([-second, first], axis=-1)
    return jnp.concatenate([rotary_part * cosine + turned * sine, value[..., ROT:]], axis=-1)


def document_of(positions, ends):
    return jnp.sum((positions[:, None] >= ends[None, :]).astype(jnp.int32), axis=1)


def inner(left, right):
    return lax.dot_general(
        left, right, (((0,), (0,)), ((), ())), preferred_element_type=jnp.float32
    )


def back_through(grad, weight_matrix):
    return lax.dot_general(
        grad, weight_matrix, (((1,), (1,)), ((), ())), preferred_element_type=jnp.float32
    )


def general_plan(
    tokens,
    cotangent,
    lengths,
    ln1_gain,
    ln1_bias,
    ln2_gain,
    ln2_bias,
    w_qkv,
    b_qkv,
    w_out_attn,
    b_out_attn,
    w_in,
    b_in,
    w_out,
    b_out,
):
    blocks = lax.axis_size("blk")
    block_here = lax.axis_index("blk")
    inputs = tokens[0].astype(jnp.float32)
    rows_here = inputs.shape[0]
    width = inputs.shape[1]
    scale = HEAD ** (-0.5)
    query_positions = block_here * rows_here + jnp.arange(rows_here, dtype=jnp.int32)
    row_lengths = lengths[0]
    ends = jnp.cumsum(row_lengths)
    doc_starts = ends - row_lengths
    query_docs = document_of(query_positions, ends)
    doc_numbers = jnp.arange(DOCS, dtype=jnp.int32)
    member = (query_docs[:, None] == doc_numbers[None, :]).astype(jnp.float32)
    earliest = jnp.sum(jnp.where(doc_numbers == query_docs[0], doc_starts, 0))
    last_query = query_positions[rows_here - 1]
    token_length = jnp.sum(member * row_lengths.astype(jnp.float32)[None, :], axis=1)
    weight = jnp.sqrt(TOK_DEV / token_length)
    half = ROT // 2
    frequency = 10000.0 ** (-(jnp.arange(half, dtype=jnp.float32) * 2.0) / ROT)
    angle = query_positions.astype(jnp.float32)[:, None] * frequency[None, :]
    cosine = jnp.concatenate([jnp.cos(angle), jnp.cos(angle)], axis=-1)[:, None, :]
    sine = jnp.concatenate([jnp.sin(angle), jnp.sin(angle)], axis=-1)[:, None, :]
    gain_one = ln1_gain.astype(jnp.float32)
    shift_one = ln1_bias.astype(jnp.float32)
    gain_two = ln2_gain.astype(jnp.float32)
    shift_two = ln2_bias.astype(jnp.float32)
    normed_one = layer_norm(inputs, gain_one, shift_one).astype(jnp.bfloat16)
    projected = jnp.dot(normed_one, w_qkv, preferred_element_type=jnp.float32) + b_qkv.astype(
        jnp.float32
    )
    query_raw = projected[:, :width].reshape(rows_here, HEADS, HEAD)
    key_raw = projected[:, width : 2 * width].reshape(rows_here, HEADS, HEAD)
    queries = rotate(query_raw, cosine, sine).astype(jnp.bfloat16)
    keys_rotated = rotate(key_raw, cosine, sine).reshape(rows_here, width)
    keys_values = jnp.concatenate([keys_rotated, projected[:, 2 * width :]], axis=1).astype(
        jnp.bfloat16
    )

    def useful(first_row, count):
        return (first_row <= last_query) & (first_row + count > earliest)

    def masked_scores(kv_piece, first_row):
        count = kv_piece.shape[0]
        key_block = kv_piece[:, :width].reshape(count, HEADS, HEAD)
        value_block = kv_piece[:, width:].reshape(count, HEADS, HEAD)
        key_positions = first_row + jnp.arange(count, dtype=jnp.int32)
        key_docs = document_of(key_positions, ends)
        allowed = (query_docs[:, None] == key_docs[None, :]) & (
            key_positions[None, :] <= query_positions[:, None]
        )
        scores = (
            jnp.einsum("qhd,khd->qhk", queries, key_block, preferred_element_type=jnp.float32)
            * scale
        )
        return (jnp.where(allowed[:, None, :], scores, -jnp.inf), key_block, value_block)

    initial = (
        jnp.full((rows_here, HEADS), -1e30, jnp.float32),
        jnp.zeros((rows_here, HEADS), jnp.float32),
        jnp.zeros((rows_here, HEADS, HEAD), jnp.float32),
    )
    kv_piece = lax.all_gather(keys_values, "blk", axis=0, tiled=True)
    first_row = jnp.int32(0)

    def fold_work(state):
        row_max, denominator, accum = state
        scores, key_block, value_block = masked_scores(kv_piece, first_row)
        new_max = jnp.maximum(row_max, jnp.max(scores, axis=-1))
        expo = jnp.exp(scores - new_max[..., None])
        denominator = jnp.sum(expo, axis=-1)
        accum = jnp.einsum(
            "qhk,khd->qhd",
            expo.astype(jnp.bfloat16),
            value_block,
            preferred_element_type=jnp.float32,
        )
        return (new_max, denominator, accum)

    row_max, denominator, accum = lax.cond(
        useful(first_row, kv_piece.shape[0]), fold_work, lambda state: state, initial
    )
    log_total = row_max + jnp.log(denominator)
    attended_full = accum / denominator[..., None]
    attended = attended_full.reshape(rows_here, width).astype(jnp.bfloat16)
    attn_branch = jnp.dot(
        attended, w_out_attn, preferred_element_type=jnp.float32
    ) + b_out_attn.astype(jnp.float32)
    normed_two = layer_norm(inputs, gain_two, shift_two).astype(jnp.bfloat16)
    hidden = jnp.dot(normed_two, w_in, preferred_element_type=jnp.float32) + b_in.astype(
        jnp.float32
    )
    activated = jax.nn.gelu(hidden, approximate=False).astype(jnp.bfloat16)
    mlp_branch = jnp.dot(activated, w_out, preferred_element_type=jnp.float32) + b_out.astype(
        jnp.float32
    )
    layer_out = (inputs + attn_branch + mlp_branch).astype(jnp.bfloat16)
    out_grad = cotangent[0].astype(jnp.float32) * weight[:, None]
    branch_grad = out_grad.astype(jnp.bfloat16)
    branch_bias_grad = jnp.sum(branch_grad.astype(jnp.float32), axis=0)
    w_out_grad = inner(activated, branch_grad)
    activated_grad = back_through(branch_grad, w_out)
    unused, gelu_back = jax.vjp(lambda value: jax.nn.gelu(value, approximate=False), hidden)
    hidden_grad = gelu_back(activated_grad)[0].astype(jnp.bfloat16)
    w_in_grad = inner(normed_two, hidden_grad)
    b_in_grad = jnp.sum(hidden_grad.astype(jnp.float32), axis=0)
    normed_two_grad = back_through(hidden_grad, w_in)
    unused, norm_two_back = jax.vjp(layer_norm, inputs, gain_two, shift_two)
    input_two, gain_two_grad, shift_two_grad = norm_two_back(normed_two_grad)
    w_out_attn_grad = inner(attended, branch_grad)
    attended_grad = (
        back_through(branch_grad, w_out_attn).astype(jnp.bfloat16).reshape(rows_here, HEADS, HEAD)
    )
    delta = jnp.sum(attended_grad.astype(jnp.float32) * attended_full, axis=-1)
    gathered = lax.all_gather(keys_values, "blk", axis=0, tiled=True)

    def pair_terms_of(scores, value_block, grad_side, lse_side, delta_side):
        weights = jnp.exp(scores - lse_side[..., None])
        weight_grad = jnp.einsum(
            "qhd,khd->qhk", grad_side, value_block, preferred_element_type=jnp.float32
        )
        score_grad = (weights * (weight_grad - delta_side[..., None])).astype(jnp.bfloat16)
        return (weights, score_grad)

    def block_back(query_grad, block_index):
        first_row = block_index * rows_here
        kv_piece = lax.dynamic_slice_in_dim(gathered, first_row, rows_here, 0)

        def block_work(query_grad):
            scores, key_block, value_block = masked_scores(kv_piece, first_row)
            weights, score_grad = pair_terms_of(
                scores, value_block, attended_grad, log_total, delta
            )
            query_grad = (
                query_grad
                + jnp.einsum(
                    "qhk,khd->qhd", score_grad, key_block, preferred_element_type=jnp.float32
                )
                * scale
            )
            key_grad = (
                jnp.einsum("qhk,qhd->khd", score_grad, queries, preferred_element_type=jnp.float32)
                * scale
            )
            value_grad = jnp.einsum(
                "qhk,qhd->khd",
                weights.astype(jnp.bfloat16),
                attended_grad,
                preferred_element_type=jnp.float32,
            )
            pair_grad = jnp.concatenate(
                [key_grad.reshape(rows_here, width), value_grad.reshape(rows_here, width)], axis=1
            )
            return (query_grad, pair_grad)

        def skipped(query_grad):
            return (query_grad, jnp.zeros((rows_here, 2 * width), jnp.float32))

        return lax.cond(useful(first_row, rows_here), block_work, skipped, query_grad)

    query_grad, pair_terms = lax.scan(
        block_back,
        jnp.zeros((rows_here, HEADS, HEAD), jnp.float32),
        jnp.arange(blocks, dtype=jnp.int32),
    )
    pair_grads = lax.psum_scatter(
        pair_terms.reshape(blocks * rows_here, 2 * width).astype(jnp.bfloat16),
        "blk",
        scatter_dimension=0,
        tiled=True,
    ).astype(jnp.float32)
    unused, rotate_back = jax.vjp(lambda value: rotate(value, cosine, sine), query_raw)
    query_raw_grad = rotate_back(query_grad)[0].reshape(rows_here, width)
    key_raw_grad = rotate_back(pair_grads[:, :width].reshape(rows_here, HEADS, HEAD))[0].reshape(
        rows_here, width
    )
    projected_grad = jnp.concatenate(
        [query_raw_grad, key_raw_grad, pair_grads[:, width:]], axis=1
    ).astype(jnp.bfloat16)
    w_qkv_grad = inner(normed_one, projected_grad)
    b_qkv_grad = jnp.sum(projected_grad.astype(jnp.float32), axis=0)
    normed_one_grad = back_through(projected_grad, w_qkv)
    unused, norm_one_back = jax.vjp(layer_norm, inputs, gain_one, shift_one)
    input_one, gain_one_grad, shift_one_grad = norm_one_back(normed_one_grad)
    input_grad = out_grad + input_one + input_two
    squares = jnp.sum(input_grad * input_grad, axis=1)
    doc_local = jnp.sum(member * squares[:, None], axis=0)
    doc_norms = lax.psum(doc_local, "blk") * (row_lengths.astype(jnp.float32) / TOK_DEV)
    summed = (
        lax.psum_scatter(gain_one_grad, ("dp", "blk"), scatter_dimension=0, tiled=True),
        lax.psum_scatter(shift_one_grad, ("dp", "blk"), scatter_dimension=0, tiled=True),
        lax.psum_scatter(gain_two_grad, ("dp", "blk"), scatter_dimension=0, tiled=True),
        lax.psum_scatter(shift_two_grad, ("dp", "blk"), scatter_dimension=0, tiled=True),
        lax.psum_scatter(w_qkv_grad, ("dp", "blk"), scatter_dimension=0, tiled=True),
        lax.psum_scatter(b_qkv_grad, ("dp", "blk"), scatter_dimension=0, tiled=True),
        lax.psum_scatter(w_out_attn_grad, ("dp", "blk"), scatter_dimension=0, tiled=True),
        lax.psum_scatter(branch_bias_grad, ("dp", "blk"), scatter_dimension=0, tiled=True),
        lax.psum_scatter(w_in_grad, ("dp", "blk"), scatter_dimension=0, tiled=True),
        lax.psum_scatter(b_in_grad, ("dp", "blk"), scatter_dimension=0, tiled=True),
        lax.psum_scatter(w_out_grad, ("dp", "blk"), scatter_dimension=0, tiled=True),
        lax.psum_scatter(branch_bias_grad, ("dp", "blk"), scatter_dimension=0, tiled=True),
    )
    return (
        layer_out[None],
        input_grad.astype(jnp.bfloat16)[None],
        summed[0],
        summed[1],
        summed[2],
        summed[3],
        summed[4],
        summed[5],
        summed[6],
        summed[7],
        summed[8],
        summed[9],
        summed[10],
        summed[11],
        doc_norms[None],
    )


NT = (((1,), (1,)), ((), ()))
TN = (((0,), (0,)), ((), ()))
NN = (((1,), (0,)), ((), ()))
F32 = jnp.float32
BF16 = jnp.bfloat16
MASKED = -1e30
PEAK = 1.15e9
HALF = ROT // 2
EXTRA = 16
HERE, PAIR, CORE, GROUP, XBIT, ZLOW, ZHIGH, LENS = 0, 1, 2, 3, 4, 5, 6, 7


def mxu(left, right, dims=NN):
    return lax.dot_general(left, right, dims, preferred_element_type=F32)


def exact(left, right):
    return lax.dot_general(
        left, right, NN, precision=lax.Precision.HIGHEST, preferred_element_type=F32
    )


def row_of(ref):
    return ref[...].astype(F32).reshape(1, -1)


def token_weight(meta, pos):
    lens = [meta[LENS + d] for d in range(DOCS)]
    length = jnp.full(pos.shape, lens[DOCS - 1], jnp.int32)
    end = lens[0]
    ends = [end]
    for d in range(1, DOCS - 1):
        end = end + lens[d]
        ends.append(end)
    for d in reversed(range(DOCS - 1)):
        length = jnp.where(pos < ends[d], lens[d], length)
    return jnp.sqrt(TOK_DEV / length.astype(F32))


def doc_bounds(meta, length):
    ends = [meta[LENS]]
    for d in range(1, DOCS - 1):
        ends.append(ends[-1] + meta[LENS + d])
    return [0] + ends, ends + [length]


def column(first, count):
    return first + lax.broadcasted_iota(jnp.int32, (count, 1), 0)


def standard(x):
    mean = jnp.mean(x, axis=-1, keepdims=True)
    centered = x - mean
    variance = jnp.mean(centered * centered, axis=-1, keepdims=True)
    rate = lax.rsqrt(variance + epsilon)
    return centered * rate, rate


def call(kernel, name, meta, operands, outs, cost_us, scratch=(), vmem=6, after=(), hold=(), far=(), aliases={}):
    inside = pl.BlockSpec(memory_space=pltpu.VMEM)
    scalars = pl.BlockSpec(memory_space=pltpu.SMEM)
    used = 1 + len(operands)
    idle = len(after) + len(hold)

    def body(*refs):
        kernel(*refs[:used], *refs[used + idle :])

    return pl.pallas_call(
        body,
        in_specs=[scalars]
        + [pl.BlockSpec(memory_space=pltpu.HBM) if k in far else inside for k in range(len(operands))]
        + [inside] * len(hold)
        + [pl.BlockSpec(memory_space=pl.ANY)] * len(after),
        out_specs=[scalars if o.shape == (1,) else inside for o in outs],
        out_shape=outs,
        scratch_shapes=list(scratch),
        input_output_aliases=aliases,
        compiler_params=pltpu.CompilerParams(vmem_limit_bytes=vmem << 20),
        cost_estimate=cost(cost_us),
        name=name,
    )(meta, *operands, *hold, *after)


def cost(us):
    return pl.CostEstimate(flops=int(us * PEAK), bytes_accessed=0, transcendentals=0)


def shape(dims, dtype=BF16):
    return jax.ShapeDtypeStruct(tuple(dims), dtype)


def all_of(array):
    rank = array.ndim
    return pl.BlockSpec(array.shape, lambda *_: (0,) * rank)


def group_rows(meta, columns, width, part, span):
    first = meta[GROUP] * span
    both = columns(pl.ds(pl.multiple_of(part * width + (first // 128) * 128, 128), 256)).T
    return jnp.where(meta[GROUP] % 2 == 1, both[HEAD : HEAD + span], both[:span])


def by_head(queries, keys, values):
    pieces = []
    for h in range(keys.shape[0] // HEAD):
        head = slice(h * HEAD, (h + 1) * HEAD)
        pieces += [keys[head], values[head]]
    return jnp.concatenate(pieces + [queries], axis=0)


def weights_kernel(meta, w_ref, wt_ref, columns, sems):
    span = wt_ref.shape[0] // 3
    width = wt_ref.shape[1]
    copies = []
    for part in range(3):
        first = meta[GROUP] * span
        place = pl.ds(pl.multiple_of(part * width + (first // 128) * 128, 128), 256)
        copies.append(pltpu.make_async_copy(w_ref.at[:, place], columns.at[part], sems.at[part]))
    for copy in copies:
        copy.start()
    for copy in copies:
        copy.wait()
    wt_ref[...] = by_head(
        *(group_rows(meta, lambda place, part=part: columns[part], width, part, span) for part in range(3))
    )


def prepare_weights(meta, w_qkv):
    width, total = w_qkv.shape
    return call(
        weights_kernel,
        "weights",
        meta,
        [w_qkv],
        [shape((total // 4, width))],
        2,
        scratch=[pltpu.VMEM((3, width, 256), BF16), pltpu.SemaphoreType.DMA((3,))],
        far=(0,),
    )[0]


def queries_keys_values(place, cols, normed, wt_ref, bias, cos_ref, sin_ref, out_ref):
    count = normed.shape[0]
    out = mxu(wt_ref[...], normed, NT) + bias[...]
    at = pl.ds(pl.multiple_of(place, count), count)
    cosine, sine = cos_ref[:, at], sin_ref[:, at]
    heads = out_ref.shape[0] // (3 * HEAD)
    out_ref[:, cols] = out.astype(BF16)
    starts = [2 * HEAD * h for h in range(heads)] + [2 * HEAD * heads + HEAD * h for h in range(heads)]
    for row in starts:
        first, second = out[row : row + HALF], out[row + HALF : row + ROT]
        turned = jnp.concatenate([first * cosine - second * sine, second * cosine + first * sine], axis=0)
        out_ref[row : row + ROT, cols] = turned.astype(BF16)


def project_kernel(meta, pair_x, far_x, gain, shift, wt_ref, bias, cos_ref, sin_ref, qkv_pair, qkv_far, normed_pair, normed_far):
    rows = pair_x.shape[0]
    for j, (x_ref, qkv_ref, normed_ref) in enumerate(((pair_x, qkv_pair, normed_pair), (far_x, qkv_far, normed_far))):
        scaled, _ = standard(x_ref[...].astype(F32))
        normed = (scaled * row_of(gain) + row_of(shift)).astype(BF16)
        normed_ref[...] = normed.T
        place = (meta[HERE] ^ (2 + j)) * rows
        queries_keys_values(place, slice(None), normed, wt_ref, bias, cos_ref, sin_ref, qkv_ref)


def project(meta, pair_x, far_x, projection, hold):
    rows, width = pair_x.shape
    features = projection[2].shape[0]
    return call(
        project_kernel,
        "project",
        meta,
        [pair_x, far_x, *projection],
        [shape((features, rows))] * 2 + [shape((width, rows))] * 2,
        4,
        hold=hold,
    )


def attended_grad_kernel(meta, own_ct, core_ct, w_ref, b_ref, mine_ref, send_ref, rows_ref, bias_ref, row_ref, sem):
    rows = own_ct.shape[0]
    span = mine_ref.shape[0]
    core, pair = meta[CORE], meta[PAIR]
    half = pl.ds(pl.multiple_of(core * 2 * span, 2 * span), 2 * span)
    copy = pltpu.make_async_copy(w_ref.at[half, :], rows_ref, sem)
    copy.start()
    row_ref[...] = row_of(b_ref)
    wide = lambda place: jnp.broadcast_to(row_ref[:, place], (8, 256))
    width = own_ct.shape[1]
    bias_ref[...] = by_head(*(group_rows(meta, wide, width, part, span) for part in range(3)))[:, 0:1]
    copy.wait()
    for b in range(2):
        ct = jnp.where(core == b, own_ct[...], core_ct[...]).astype(F32)
        grad = (ct * token_weight(meta, column((2 * pair + b) * rows, rows))).astype(BF16)
        both = mxu(rows_ref[...], grad, NT).astype(BF16)
        cols = slice(b * rows, (b + 1) * rows)
        mine_ref[:, cols] = jnp.where(pair == 0, both[:span], both[span:])
        send_ref[:, cols] = jnp.where(pair == 0, both[span:], both[:span])


def attended_grad(meta, own_ct, core_ct, w_out_attn, b_qkv, hold):
    rows, width = own_ct.shape
    span = width // 4
    return call(
        attended_grad_kernel,
        "attended_grad",
        meta,
        [own_ct, core_ct, w_out_attn, b_qkv],
        [shape((span, 2 * rows)), shape((span, 2 * rows)), shape((2 * span, width)), shape((3 * span, 1), F32)],
        2,
        scratch=[pltpu.VMEM((1, 3 * width), F32), pltpu.SemaphoreType.DMA],
        hold=hold,
        far=(2,),
    )


def hidden_kernel(
    meta,
    own_x,
    core_x,
    own_ct,
    core_ct,
    gain,
    shift,
    win_ref,
    bin_ref,
    wout_ref,
    gain_one,
    shift_one,
    wt_ref,
    bias,
    cos_ref,
    sin_ref,
    act_ref,
    hid_ref,
    grad_ref,
    turned_ref,
    scaled_ref,
    bin_grad_ref,
    branch_sum_ref,
    qkv_own,
    qkv_core,
    normed_own,
    normed_core,
    win_half,
    wout_half,
    bin_row,
    sems,
):
    rows, width = own_x.shape
    hidden_size = win_ref.shape[1] // 2
    chunk = 256
    base = pl.multiple_of(meta[CORE] * hidden_size, hidden_size)
    copies = [
        pltpu.make_async_copy(win_ref.at[:, pl.ds(base, hidden_size)], win_half, sems.at[0]),
        pltpu.make_async_copy(wout_ref.at[pl.ds(base, hidden_size), :], wout_half, sems.at[1]),
    ]
    for copy in copies:
        copy.start()
    bin_row[...] = row_of(bin_ref)
    branch_sum_ref[...] = jnp.zeros_like(branch_sum_ref)
    inputs = ((own_x, own_ct, qkv_own, normed_own), (core_x, core_ct, qkv_core, normed_core))
    totals = []
    for block, (x_ref, ct_ref, qkv_ref, normed_ref) in enumerate(inputs):
        at = slice(block * rows, (block + 1) * rows)
        place = (meta[HERE] ^ block) * rows
        scaled, _ = standard(x_ref[...].astype(F32))
        scaled_ref[at, :] = scaled
        normed = (scaled * row_of(gain_one) + row_of(shift_one)).astype(BF16)
        normed_ref[...] = normed.T
        queries_keys_values(place, slice(None), normed, wt_ref, bias, cos_ref, sin_ref, qkv_ref)
        normed = (scaled * row_of(gain) + row_of(shift)).astype(BF16)
        turned_ref[:, at] = normed.T
        grad = (ct_ref[...].astype(F32) * token_weight(meta, column(place, rows))).astype(BF16)
        grad_ref[at, :] = grad
        if block == 0:
            branch_sum_ref[0:1, :] = jnp.sum(grad.astype(F32), axis=0, keepdims=True)
        if block == 0:
            for copy in copies:
                copy.wait()
        sums = []
        for j in range(0, hidden_size, chunk):
            cols = slice(j, j + chunk)
            there = pl.ds(pl.multiple_of(base + j, 128), chunk)
            hidden = mxu(normed, win_half[:, cols]) + bin_row[:, there]
            back = mxu(grad, wout_half[cols, :], NT)
            below = 0.5 + 0.5 * lax.erf(hidden * (0.5**0.5))
            bell = jnp.exp(hidden * hidden * -0.5) * 0.3989422804014327
            act_ref[at, cols] = (hidden * below).astype(BF16)
            rounded = (back * (below + hidden * bell)).astype(BF16)
            hid_ref[at, cols] = rounded
            sums.append(jnp.sum(rounded.astype(F32), axis=0, keepdims=True))
        totals.append(jnp.concatenate(sums, axis=1))
    bin_grad_ref[...] = totals[0] + totals[1]


def hidden_part(meta, own_x, core_x, own_ct, core_ct, gain, shift, w_in, b_in, w_out, projection, hold):
    rows, width = own_x.shape
    hidden_size = w_in.shape[1] // 2
    features = projection[2].shape[0]
    outs = [
        shape((2 * rows, hidden_size)),
        shape((2 * rows, hidden_size)),
        shape((2 * rows, width)),
        shape((width, 2 * rows)),
        shape((2 * rows, width), F32),
        shape((1, hidden_size), F32),
        shape((8, width), F32),
        shape((features, rows)),
        shape((features, rows)),
        shape((width, rows)),
        shape((width, rows)),
        shape((width, hidden_size)),
        shape((hidden_size, width)),
    ]
    operands = [own_x, core_x, own_ct, core_ct, gain, shift, w_in, b_in, w_out, *projection]
    return call(
        hidden_kernel,
        "hidden",
        meta,
        operands,
        outs,
        13,
        scratch=[pltpu.VMEM((1, 2 * hidden_size), F32), pltpu.SemaphoreType.DMA((2,))],
        vmem=8,
        hold=hold,
        far=(6, 8),
    )


def out_grad_kernel(meta, act_ref, grad_ref, x_ref, send_ref, keep_ref, again_ref):
    again_ref[...] = x_ref[...]
    quarter = send_ref.shape[0] // 2
    part = quarter // 2
    grad = grad_ref[...]
    for ref, bit in ((send_ref, 1 - meta[XBIT]), (keep_ref, meta[XBIT])):
        for z in range(2):
            there = pl.ds(pl.multiple_of((2 * z + bit) * quarter, quarter), quarter)
            found = mxu(act_ref[:, there], grad, TN).astype(BF16)
            for p in range(2):
                ref[(2 * p + z) * part : (2 * p + z + 1) * part, :] = found[p * part : (p + 1) * part]


def out_grad(meta, act, grad, x, hold):
    half = shape((act.shape[1] // 2, grad.shape[1]))
    return call(out_grad_kernel, "w_out_grad", meta, [act, grad, x], [half, half, shape(x.shape)], 3, hold=hold)


def in_grad_kernel(
    meta, act_ref, hid_ref, turned_ref, scaled_ref, gain, win_ref, wout_ref, branch_ref, term_ref, send_ref, keep_ref, small_ref
):
    width = win_ref.shape[0]
    fine = width // 16
    for ref, bit in ((send_ref, 1 - meta[ZLOW]), (keep_ref, meta[ZLOW])):
        pieces = []
        for xb in range(2):
            for p in range(2):
                for zh in range(2):
                    source = (4 * zh + 2 * bit + xb) * 2 * fine + p * fine
                    pieces.append(turned_ref[pl.ds(pl.multiple_of(source, fine), fine), :])
        ref[...] = mxu(jnp.concatenate(pieces, axis=0), hid_ref[...]).astype(BF16)
    rows = act_ref.shape[0] // 2
    small_ref[...] = jnp.zeros_like(small_ref)
    for block in range(2):
        at = slice(block * rows, (block + 1) * rows)
        branch_ref[at, :] = mxu(act_ref[at, :], wout_ref[...]).astype(BF16)
        normed_grad = mxu(hid_ref[at, :], win_ref[...], NT)
        term_ref[at, :] = (normed_grad * row_of(gain)).astype(BF16)
        small_ref[0:1, :] += jnp.sum(normed_grad * scaled_ref[at, :], axis=0, keepdims=True)
        small_ref[1:2, :] += jnp.sum(normed_grad, axis=0, keepdims=True)


def in_grad(meta, act, hid, turned, scaled, gain, w_in, w_out, hold):
    tokens, hidden_size = act.shape
    width = w_in.shape[0]
    outs = [
        shape((tokens, width)),
        shape((tokens, width)),
        shape((width // 2, hidden_size)),
        shape((width // 2, hidden_size)),
        shape((8, width), F32),
    ]
    return call(
        in_grad_kernel,
        "w_in_grad",
        meta,
        [act, hid, turned, scaled, gain, w_in, w_out],
        outs,
        9,
        hold=hold,
    )


def three(value):
    a = value.astype(BF16).astype(F32)
    rest = value - a
    b = rest.astype(BF16).astype(F32)
    return a, b, rest - b


def placer(meta, blocks):
    here, pair = meta[HERE], meta[PAIR]

    def placed(rows, b):
        low = here % 2 == b % 2
        near = jnp.where(low, blocks[0][rows, :], blocks[1][rows, :])
        far = jnp.where(low, blocks[2][rows, :], blocks[3][rows, :])
        return jnp.where(pair == b // 2, near, far)

    return placed


def beside(runs):
    current, first, second = runs[0]
    for _ in range(first):
        next(current)
    for n, (current, _, second) in enumerate(runs):
        following, total = (runs[n + 1][0], runs[n + 1][1]) if n + 1 < len(runs) else (None, 0)
        done = 0
        for i in range(second):
            next(current)
            while done < (i + 1) * total // second:
                next(following)
                done += 1
        for _ in current:
            raise ValueError("steps")


def tile_rows(v, tile):
    return tile * (v * (v + 1) // 2)


def forward_kernel(
    chosen, meta, b0, b1, b2, b3, do_near, do_far, near_ref, far_ref, p_first, p_last, do_ref, out_ref, ka_ref, vt_ref, s_ref
):
    tile = b0.shape[1]
    length = 4 * tile
    heads = do_near.shape[0] // HEAD
    step = tile // 2
    scale = HEAD ** (-0.5)
    pair = meta[PAIR]
    lows, highs = doc_bounds(meta, length)
    placed = placer(meta, (b0, b1, b2, b3))

    pos = lax.broadcasted_iota(jnp.int32, (EXTRA, length), 1)
    row = lax.broadcasted_iota(jnp.int32, (EXTRA, length), 0)
    inside = jnp.zeros(pos.shape, jnp.bool_)
    for d in range(DOCS):
        inside = inside | ((row == d) & (pos >= lows[d]) & (pos < highs[d]))
    key_rows = jnp.where(inside, 1.0, 0.0).astype(BF16)
    one_rows = jnp.where(row[:, :tile] < 3, 1.0, 0.0).astype(BF16)
    query_rows = jnp.where((row < DOCS) & jnp.logical_not(inside), MASKED, 0.0).astype(BF16)
    fill = jnp.zeros((HEAD - EXTRA, tile), BF16)
    for n, head in enumerate(chosen):
        for b in range(4):
            cols = slice(b * tile, (b + 1) * tile)
            kv = placed(slice(2 * HEAD * head, 2 * HEAD * (head + 1)), b)
            ka_ref[n, cols, :] = jnp.concatenate([kv[:HEAD], key_rows[:, cols], fill], axis=0).T
            vt_ref[n, :, cols] = jnp.concatenate([kv[HEAD:], one_rows], axis=0)
    extra_row = lax.broadcasted_iota(jnp.int32, (EXTRA, tile), 0)
    offset = lax.broadcasted_iota(jnp.int32, (step, tile), 0) - lax.broadcasted_iota(jnp.int32, (step, tile), 1)

    def run(n, v, buf):
        head = chosen[n]
        p_ref, m = (p_last, 0) if n == len(chosen) - 1 else (p_first, n)
        of_head = slice(head * HEAD, (head + 1) * HEAD)
        q_rows = slice(HEAD * (2 * heads + head), HEAD * (2 * heads + head + 1))
        chunks = (v + 1) * tile // step
        first_row = tile_rows(v, tile)
        cols = slice(v * tile, (v + 1) * tile)
        low = lambda k: max(0, k * step - v * tile)
        q_t = placed(q_rows, v) * jnp.asarray(scale, BF16)
        half = slice((v % 2) * tile, (v % 2 + 1) * tile)
        do_t = jnp.where(pair == v // 2, do_near[of_head, half], do_far[of_head, half])
        q_aug = jnp.concatenate([q_t, query_rows[:, cols], fill], axis=0)
        top = jnp.full((1, tile), MASKED, F32)
        for k in range(chunks):
            rows, l = slice(k * step, (k + 1) * step), low(k)
            scores = mxu(ka_ref[n, rows, :], q_aug[:, l:])
            if (k + 1) * step > v * tile:
                scores = jnp.where(offset[:, l:] <= v * tile - k * step, scores, MASKED)
            s_ref[buf, rows, l:] = scores
            peak = jnp.max(scores, axis=0, keepdims=True)
            if l:
                top = jnp.concatenate([top[:, :l], jnp.maximum(top[:, l:], peak)], axis=1)
            else:
                top = jnp.maximum(top, peak)
            yield
        for k in range(chunks):
            rows, l = slice(k * step, (k + 1) * step), low(k)
            to = slice(first_row + k * step, first_row + (k + 1) * step)
            p_ref[m, to, l:] = jnp.exp(s_ref[buf, rows, l:] - top[:, l:]).astype(BF16)
            yield
        lanes = [(g * step, v * tile + (g + 1) * step) for g in range(tile // step)]
        out_all = jnp.concatenate(
            [mxu(vt_ref[n, :, :w], p_ref[m, first_row : first_row + w, l : l + step]) for l, w in lanes], axis=1
        )
        inverse = 1.0 / out_all[HEAD : HEAD + 1]
        out_t = out_all[:HEAD] * inverse
        out_ref[(v // 2) ^ pair, n * HEAD : (n + 1) * HEAD, half] = out_t.astype(BF16)
        do_scaled = (do_t.astype(F32) * inverse).astype(BF16)
        delta = jnp.sum(do_scaled.astype(F32) * out_t, axis=0, keepdims=True)
        a, b, c = three(-delta)
        terms = jnp.where(extra_row == 0, a, jnp.where(extra_row == 1, b, jnp.where(extra_row == 2, c, 0.0)))
        do_ref[n, :, cols] = jnp.concatenate([do_scaled, terms.astype(BF16), fill], axis=0)
        yield

    tiles = length // tile
    beside(
        [
            (run(n, v, v % 2), (v + 1) * tile // step, (v + 1) * tile // step + 1)
            for n in range(len(chosen))
            for v in reversed(range(tiles))
        ]
    )
    near_ref[...] = out_ref[0]
    far_ref[...] = out_ref[1]


def attend_forward(meta, chosen, blocks, do_near, do_far, hold):
    rows = blocks[0].shape[1]
    length = 4 * rows
    count = len(chosen)
    return call(
        functools.partial(forward_kernel, chosen),
        "attend%d" % chosen[0],
        meta,
        [*blocks, do_near, do_far],
        [shape((count * HEAD, 2 * rows))] * 2
        + [shape((c, tile_rows(4, rows), rows)) for c in (count - 1, 1)]
        + [shape((count, 2 * HEAD, length))],
        4 * count,
        hold=hold,
        scratch=[
            pltpu.VMEM((2, count * HEAD, 2 * rows), BF16),
            pltpu.VMEM((count, length, 2 * HEAD), BF16),
            pltpu.VMEM((count, HEAD + EXTRA, length), BF16),
            pltpu.VMEM((2, length, rows), F32),
        ],
        vmem=12,
    )


def backward_kernel(
    chosen, meta, b0, b1, b2, b3, p_ref, do_ref, cos_ref, sin_ref, dq_ref, dkv_ref, kt_ref, va_ref, d_ref, acc_ref
):
    tile = b0.shape[1]
    length = 4 * tile
    heads = b0.shape[0] // (3 * HEAD)
    step = tile // 2
    scale = HEAD ** (-0.5)
    pair = meta[PAIR]
    placed = placer(meta, (b0, b1, b2, b3))
    row = lax.broadcasted_iota(jnp.int32, (EXTRA, tile), 0)
    one_rows = jnp.where(row < 3, 1.0, 0.0).astype(BF16)
    fill = jnp.zeros((HEAD - EXTRA, tile), BF16)
    for n, head in enumerate(chosen):
        for b in range(4):
            cols = slice(b * tile, (b + 1) * tile)
            kv = placed(slice(2 * HEAD * head, 2 * HEAD * (head + 1)), b)
            kt_ref[n, :, cols] = kv[:HEAD]
            va_ref[n, cols, :] = jnp.concatenate([kv[HEAD:], one_rows, fill], axis=0).T
    per_half = 2 * tile
    blank = jnp.zeros((HEAD, tile), F32)

    def run(n, v, buf, widest):
        head = chosen[n]
        q_rows = slice(HEAD * (2 * heads + head), HEAD * (2 * heads + head + 1))
        width = (v + 1) * tile
        chunks = width // step
        first_row = tile_rows(v, tile)
        cols = slice(v * tile, (v + 1) * tile)
        low = lambda k: max(0, k * step - v * tile)
        for k in range(chunks):
            rows, l = slice(k * step, (k + 1) * step), low(k)
            weights = p_ref[n, first_row + k * step : first_row + (k + 1) * step, l:]
            weight_grad = mxu(va_ref[n, rows, :], do_ref[head, :, v * tile + l : (v + 1) * tile])
            d_ref[buf, rows, l:] = (weights.astype(F32) * weight_grad).astype(BF16)
            yield
        q_t = placed(q_rows, v) * jnp.asarray(scale, BF16)
        groups = [(0, v * tile, 0)] if v else []
        groups += [(v * tile + g * step, v * tile + (g + 1) * step, g * step) for g in range(tile // step)]
        for r, s, l in groups:
            value = mxu(do_ref[head, :HEAD, v * tile + l : (v + 1) * tile], p_ref[n, first_row + r : first_row + s, l:], NT)
            key = mxu(q_t[:, l:], d_ref[buf, r:s, l:], NT)
            if widest:
                acc_ref[n, HEAD:, r:s] = value
                acc_ref[n, :HEAD, r:s] = key
            else:
                acc_ref[n, HEAD:, r:s] += value
                acc_ref[n, :HEAD, r:s] += key
            yield
        lanes = [(g * step, v * tile + (g + 1) * step) for g in range(tile // step)]
        dq_t = (
            jnp.concatenate([mxu(kt_ref[n, :, :w], d_ref[buf, :w, l : l + step]) for l, w in lanes], axis=1) * scale
        )
        cosine, sine = cos_ref[:, cols], sin_ref[:, cols]
        first, second = dq_t[:HALF], dq_t[HALF:ROT]
        joined = jnp.concatenate(
            [first * cosine + second * sine, second * cosine - first * sine, dq_t[ROT:], blank], axis=0
        )
        half = slice((v % 2) * tile, (v % 2 + 1) * tile)
        dq_ref[(v // 2) ^ pair, half, n * 2 * HEAD : (n + 1) * 2 * HEAD] = joined.T.astype(BF16)
        yield

    tiles = length // tile
    beside(
        [
            (run(n, v, v % 2, v == tiles - 1), (v + 1) * tile // step, (1 if v else 0) + tile // step + 1)
            for n in range(len(chosen))
            for v in reversed(range(tiles))
        ]
    )
    cosine, sine = cos_ref[...], sin_ref[...]
    for n in range(len(chosen)):
        grads = acc_ref[n]
        first, second = grads[:HALF], grads[HALF:ROT]
        grads = jnp.concatenate(
            [first * cosine + second * sine, second * cosine - first * sine, grads[ROT:]], axis=0
        )
        for h in range(2):
            lanes = slice(n * 2 * HEAD, (n + 1) * 2 * HEAD)
            dkv_ref[h ^ pair, :, lanes] = grads[:, h * per_half : (h + 1) * per_half].T.astype(BF16)


def attend_backward(meta, chosen, blocks, weights, do, cosine, sine, hold):
    rows = blocks[0].shape[1]
    length = 4 * rows
    count = len(chosen)
    return call(
        functools.partial(backward_kernel, chosen),
        "attend_back%d" % chosen[0],
        meta,
        [*blocks, weights, do, cosine, sine],
        [shape((2, 2 * rows, 2 * HEAD * count))] * 2,
        5 * count,
        hold=hold,
        scratch=[
            pltpu.VMEM((count, HEAD, length), BF16),
            pltpu.VMEM((count, length, 2 * HEAD), BF16),
            pltpu.VMEM((2, length, rows), BF16),
            pltpu.VMEM((count, 2 * HEAD, length), F32),
        ],
        vmem=10,
    )


def branch_kernel(meta, mine_ref, theirs_ref, w_ref, branch, own_ct, core_ct, own_ref, send_ref, goa_send, goa_keep):
    pair, core = meta[PAIR], meta[CORE]
    rows = own_ref.shape[0]
    mine, theirs = mine_ref[...], theirs_ref[...]
    six = jnp.concatenate([jnp.where(pair == 0, mine, theirs), jnp.where(pair == 0, theirs, mine)], axis=0)
    own_cols = jnp.where(core == 0, six[:, :rows], six[:, rows:])
    other_cols = jnp.where(core == 0, six[:, rows:], six[:, :rows])
    half = w_ref.shape[0]
    weight = w_ref[...]
    send_ref[...] = (mxu(other_cols, weight, TN) + branch[rows:, :].astype(F32)).astype(BF16)
    own_ref[...] = mxu(own_cols, weight, TN) + branch[:rows, :].astype(F32)
    grads = []
    for j, ct in enumerate((own_ct, core_ct)):
        place = (meta[HERE] ^ j) * rows
        grads.append((ct[...].astype(F32) * token_weight(meta, column(place, rows))).astype(BF16))
    total = mxu(own_cols, grads[0]) + mxu(other_cols, grads[1])
    first, second = total[: half // 2], total[half // 2 :]
    goa_keep[...] = jnp.where(meta[ZLOW] == 0, first, second).astype(BF16)
    goa_send[...] = jnp.where(meta[ZLOW] == 0, second, first).astype(BF16)


def branch_job(mine, arrived, w_rows, branch, own_ct, core_ct):
    rows, width = own_ct.shape
    outs = [shape((rows, width), F32), shape((rows, width))] + [shape((width // 4, width))] * 2
    return branch_kernel, [mine, arrived, w_rows, branch, own_ct, core_ct], outs


def with_queries(wt_ref):
    span = wt_ref.shape[0] // 3
    pieces = [wt_ref[: 2 * span, :]]
    for h in range(span // HEAD):
        head = wt_ref[2 * span + h * HEAD : 2 * span + (h + 1) * HEAD, :]
        pieces += [head, jnp.zeros_like(head)]
    return jnp.concatenate(pieces, axis=0)


def far_kernel(meta, *refs):
    kv, qo = refs[0:2], refs[2:4]
    wt_ref, gain, send_ref, keep_ref = refs[4:]
    core = meta[CORE]
    rows = send_ref.shape[0]
    right = with_queries(wt_ref)
    for out, b in ((send_ref, 1 - core), (keep_ref, core)):
        at = pl.ds(pl.multiple_of(b * rows, rows), rows)
        left = jnp.concatenate([r[1, at, :] for r in kv] + [r[1, at, :] for r in qo], axis=1)
        out[...] = (mxu(left, right) * row_of(gain)).astype(BF16)


PIECES = 24


def weight_kernel(meta, *refs):
    kv, qo = refs[0:2], refs[2:4]
    wt_ref, gain, shift, n0, n1, n2, n3, two_ref, branch_sum, bin_ref = refs[4:14]
    send_ref, keep_ref, vector_ref = refs[14:]
    core = meta[CORE]
    width, rows = n0.shape
    features = wt_ref.shape[0]
    span = features // 3
    devices = 2 * keep_ref.shape[0]
    gain_row, shift_row = row_of(gain), row_of(shift)

    def both(half, b):
        at = pl.ds(pl.multiple_of(b * rows, rows), rows)
        return jnp.concatenate([r[half, at, :] for r in kv] + [r[half, at, :] for r in qo], axis=1)

    near_own, near_core = both(0, core), both(0, 1 - core)
    far_own, far_core = both(1, core), both(1, 1 - core)
    grad = mxu(n0[...], near_own) + mxu(n1[...], near_core) + mxu(n2[...], far_own) + mxu(n3[...], far_core)
    sums = sum(
        jnp.sum(a.astype(F32), axis=0, keepdims=True) for a in (near_own, near_core, far_own, far_core)
    )

    def tight(value):
        queries = [value[:, 2 * span + 2 * HEAD * h : 2 * span + 2 * HEAD * h + HEAD] for h in range(3)]
        return jnp.concatenate([value[:, : 2 * span]] + queries, axis=1)

    grad, sums = tight(grad), tight(sums)
    weights = wt_ref[...].T.astype(F32)
    by_weight = jnp.sum(weights * grad, axis=1, keepdims=True)
    shift_grad = jnp.sum(weights * sums, axis=1, keepdims=True)
    lane = lax.broadcasted_iota(jnp.int32, (width, 128), 1)
    turned = jnp.where(lane == 0, by_weight, jnp.where(lane == 1, shift_grad, 0.0)).T
    shift_grad = turned[1:2, :]
    gain_grad = (turned[0:1, :] - shift_row * shift_grad) / gain_row

    offset = features % 128

    def spread(vectors, place_row, place_col, pieces):
        count = vectors.shape[0]
        index = lambda place: jnp.floor((place.astype(F32) + 0.5) * (1.0 / PIECES)).astype(jnp.int32)
        device = lax.broadcasted_iota(jnp.int32, (devices, vectors.shape[1]), 0)
        owner = index(place_row)
        parts = []
        for p in range(pieces):
            chosen = owner == device * pieces + p
            for c in range(count):
                value = vectors[c : c + 1, :]
                high = value.astype(BF16)
                low = (value - high.astype(F32)).astype(BF16)
                for part in (high, low):
                    parts.append(jnp.where(chosen, part.astype(F32), 0.0))
        within = place_col - PIECES * index(place_col) + offset
        lane = lax.broadcasted_iota(jnp.int32, (vectors.shape[1], 128), 1)
        table = jnp.where(within == lane, 1.0, 0.0).astype(BF16)
        return mxu(jnp.concatenate(parts, axis=0).astype(BF16), table)

    def counted(size):
        return (
            lax.broadcasted_iota(jnp.int32, (1, size), 1),
            lax.broadcasted_iota(jnp.int32, (size, 1), 0),
        )

    def qkv_place(index):
        rest = index - 2 * span
        keys = (1 + (index // HEAD) % 2) * width + (index // (2 * HEAD)) * HEAD
        return meta[GROUP] * span + index % HEAD + jnp.where(rest < 0, keys, (rest // HEAD) * HEAD)

    lanes, sub = counted(width)
    norms = jnp.concatenate(
        [gain_grad, shift_grad, two_ref[0:1, :], two_ref[1:2, :], branch_sum[0:1, :]], axis=0
    )
    lanes_kv, sub_kv = counted(features)
    hidden_size = bin_ref.shape[1]
    lanes_in, sub_in = counted(hidden_size)
    base = core * hidden_size
    row = 0
    for found in (
        spread(norms, lanes, sub, 1),
        spread(sums, qkv_place(lanes_kv), qkv_place(sub_kv), 3),
        spread(bin_ref[...], base + lanes_in, base + sub_in, 4),
    ):
        for k in range(found.shape[0] // devices):
            vector_ref[:, row, :] = found[k * devices : (k + 1) * devices]
            row += 1
    chunk = width // devices
    whole = (features // 128) * 128
    tail = jnp.concatenate([grad[:, whole:], jnp.zeros((width, 128 - offset), F32)], axis=1)
    def piece(d):
        at = slice(d * chunk, (d + 1) * chunk)
        return jnp.concatenate([grad[at, :whole], tail[at] + vector_ref[d]], axis=1)

    for e in range(devices // 2):
        d = (e // 4 % 2) * 16 + (e // 8) * 8 + e % 4
        first, second = piece(d), piece(d + 4)
        keep_ref[e] = jnp.where(meta[XBIT] == 0, first, second)
        send_ref[e] = jnp.where(meta[XBIT] == 0, second, first).astype(BF16)


def near_kernel(meta, *refs):
    kv, qo = refs[0:2], refs[2:4]
    wt_ref, gain, term_two, far_ref, send_ref, own_ref = refs[4:]
    core = meta[CORE]
    rows = own_ref.shape[0]
    right = with_queries(wt_ref)

    def part(b):
        at = pl.ds(pl.multiple_of(b * rows, rows), rows)
        return jnp.concatenate([r[0, at, :] for r in kv] + [r[0, at, :] for r in qo], axis=1)

    gain_row = row_of(gain)
    send_ref[:rows, :] = far_ref[...]
    send_ref[rows:, :] = (mxu(part(1 - core), right) * gain_row + term_two[rows:, :].astype(F32)).astype(BF16)
    own_ref[...] = mxu(part(core), right) * gain_row + term_two[:rows, :].astype(F32)


def last_head_kernel(
    chosen,
    meta,
    b0,
    b1,
    b2,
    b3,
    p_ref,
    do_ref,
    cos_ref,
    sin_ref,
    dq_a,
    dkv_a,
    wt_ref,
    gain,
    shift,
    n0,
    n1,
    n2,
    n3,
    two_ref,
    branch_sum,
    bin_ref,
    dq_ref,
    dkv_ref,
    far_send,
    far_keep,
    g_send,
    g_keep,
    kt_ref,
    va_ref,
    d_ref,
    acc_ref,
    vector_ref,
):
    backward_kernel(
        chosen, meta, b0, b1, b2, b3, p_ref, do_ref, cos_ref, sin_ref, dq_ref, dkv_ref, kt_ref, va_ref, d_ref, acc_ref
    )
    grads = (dkv_a, dkv_ref, dq_a, dq_ref)
    far_kernel(meta, *grads, wt_ref, gain, far_send, far_keep)
    weight_kernel(
        meta, *grads, wt_ref, gain, shift, n0, n1, n2, n3, two_ref, branch_sum, bin_ref, g_send, g_keep, vector_ref
    )


def last_head(meta, chosen, blocks, weights, do, cosine, sine, earlier, wt, gain, shift, normed, vectors, devices, hold):
    rows = blocks[0].shape[1]
    length = 4 * rows
    count = len(chosen)
    width = wt.shape[1]
    lanes = -(-wt.shape[0] // 128) * 128
    chunk = width // devices
    outs = [shape((2, 2 * rows, 2 * HEAD * count))] * 2 + [shape((rows, width))] * 2
    outs += [shape((devices // 2, chunk, lanes)), shape((devices // 2, chunk, lanes), F32)]
    return call(
        functools.partial(last_head_kernel, chosen),
        "last_head",
        meta,
        [*blocks, weights, do, cosine, sine, *earlier, wt, gain, shift, *normed, *vectors],
        outs,
        12,
        hold=hold,
        scratch=[
            pltpu.VMEM((count, HEAD, length), BF16),
            pltpu.VMEM((count, length, 2 * HEAD), BF16),
            pltpu.VMEM((2, length, rows), BF16),
            pltpu.VMEM((count, 2 * HEAD, length), F32),
            pltpu.VMEM((devices, chunk, 128), F32),
        ],
        vmem=14,
    )


def near_job(dkv, dqo, wt, gain, term_two, far):
    rows, width = far.shape
    operands = [*dkv, *dqo, wt, gain, term_two, far]
    return near_kernel, operands, [shape((2 * rows, width)), shape((rows, width), F32)]


def core_sums_kernel(meta, far_ref, near_ref, arrived_ref, far_sum_ref, near_sum_ref):
    rows = far_ref.shape[0]
    far_sum_ref[...] = (far_ref[...].astype(F32) + arrived_ref[:rows, :].astype(F32)).astype(BF16)
    near_sum_ref[...] = near_ref[...] + arrived_ref[rows:, :].astype(F32)


def core_sums_job(far, near, arrived):
    return core_sums_kernel, [far, near, arrived], [shape(far.shape), shape(near.shape, F32)]


def gather_kernel(meta, r0, r2, core_ref, out_ref, *vector_refs):
    heads = HEADS // 4
    span = heads * HEAD
    width = out_ref.shape[1] // 3
    whole = ((3 * span) // 128) * 128
    here = meta[HERE]
    found = [r0[...], core_ref[0].astype(F32), r2[...], core_ref[1].astype(F32)]
    vectors = sum(value[:, whole:] for value in found)
    for s in range(4):
        low = here % 2 == s % 2
        value = jnp.where(
            here // 2 == s // 2, jnp.where(low, found[0], found[1]), jnp.where(low, found[2], found[3])
        )
        group = 2 * (s % 2) + s // 2
        for h in range(heads):
            at = group * span + h * HEAD
            out_ref[:, at : at + HEAD] = value[:, 2 * span + h * HEAD : 2 * span + (h + 1) * HEAD]
            out_ref[:, width + at : width + at + HEAD] = value[:, 2 * HEAD * h : 2 * HEAD * h + HEAD]
            out_ref[:, 2 * width + at : 2 * width + at + HEAD] = value[:, 2 * HEAD * h + HEAD : 2 * HEAD * (h + 1)]
    vectors = pltpu.roll(vectors, 128 - (3 * span) % 128, 1)
    pieces = [
        vectors[2 * k : 2 * k + 1, :PIECES] + vectors[2 * k + 1 : 2 * k + 2, :PIECES]
        for k in range(vectors.shape[0] // 2)
    ]
    again_ref, vector_refs = vector_refs[-1], vector_refs[:-1]
    again_ref[...] = pieces[4].reshape(again_ref.shape)
    k = 0
    for ref in vector_refs:
        count = ref.shape[0] // PIECES
        ref[...] = jnp.concatenate(pieces[k : k + count], axis=1).reshape(ref.shape)
        k += count


def gather_qkv(meta, parts, after):
    rows = parts[0].shape[0]
    outs = [shape((rows, 3 * HEADS * HEAD), F32)]
    outs += [shape((count * PIECES,), F32) for count in (1, 1, 1, 1, 1, 3, 4, 1)]
    return call(gather_kernel, "gather", meta, parts, outs, 0, after=after)


def layer_out_kernel(meta, x_ref, own_ref, core_ref, first, second, out_ref):
    total = x_ref[...].astype(F32) + own_ref[...] + core_ref[...].astype(F32)
    out_ref[...] = (total + (row_of(first) + row_of(second))).astype(BF16)


def last_kernel(meta, x_ref, ct_ref, near_ref, pair_ref, tokens_ref, docs_ref):
    rows = x_ref.shape[0]
    scaled, rate = standard(x_ref[...].astype(F32))
    term = near_ref[...] + pair_ref[...].astype(F32)
    back = rate * (
        term
        - jnp.mean(term, axis=-1, keepdims=True)
        - scaled * jnp.mean(term * scaled, axis=-1, keepdims=True)
    )
    pos = column(meta[HERE] * rows, rows)
    grad = ct_ref[...].astype(F32) * token_weight(meta, pos) + back
    tokens_ref[...] = grad.astype(BF16)
    squares = jnp.sum(grad * grad, axis=1, keepdims=True)
    lows, highs = doc_bounds(meta, 4 * rows)
    lane = lax.broadcasted_iota(jnp.int32, (8, 128), 1)
    docs = jnp.zeros((8, 128), F32)
    for d in range(DOCS):
        total = jnp.sum(jnp.where((pos >= lows[d]) & (pos < highs[d]), squares, 0.0), axis=0, keepdims=True)
        docs = jnp.where(lane == d, total, docs)
    docs_ref[...] = docs


def last_job(*operands):
    return last_kernel, list(operands), [shape(operands[0].shape), shape((8, 128), F32)]


def flip(value, axis, bit):
    size = lax.axis_size(axis)
    return lax.ppermute(value, axis, [(i, i ^ (1 << bit)) for i in range(size)])


def relay_kernel(places, finals, meta, *refs):
    count = len(places)
    ins, outs = refs[: 2 * count], refs[2 * count :]
    for k, (place, final) in enumerate(zip(places, finals)):
        keep, arrived = ins[2 * k], ins[2 * k + 1]
        first, second = outs[2 * k], outs[2 * k + 1]
        if final:
            total = keep[...].astype(F32) + arrived[...].astype(F32)
            first[...] = total.astype(first.dtype)
            second[...] = total
        else:
            half = first.shape[0]
            for out, bit in ((first, 1 - meta[place]), (second, meta[place])):
                at = pl.ds(pl.multiple_of(bit * half, half), half)
                out[...] = (keep[at, :].astype(F32) + arrived[at, :].astype(F32)).astype(out.dtype)


def split_kernel(meta, *refs):
    kept_ref, given_ref = refs[-2:]
    total = sum(ref[...].astype(F32) for ref in refs[:-2])
    fine = kept_ref.shape[0]
    kept_ref[...] = jnp.where(meta[CORE] == 0, total[:fine], total[fine:])
    given_ref[...] = jnp.where(meta[CORE] == 0, total[fine:], total[:fine])


def together(meta, name, jobs, after=(), hold=(), vmem=8, through=()):
    counts = [(len(operands), len(outs)) for _, operands, outs in jobs]
    inputs = sum(count for count, _ in counts) + len(through)

    def kernel(meta, *refs):
        first, out = len(through), inputs + len(through)
        for (body, _, _), (ins, outs) in zip(jobs, counts):
            body(meta, *refs[first : first + ins], *refs[out : out + outs])
            first, out = first + ins, out + outs

    found = call(
        kernel,
        name,
        meta,
        list(through) + [x for _, operands, _ in jobs for x in operands],
        [shape(x.shape, x.dtype) for x in through] + [x for _, _, outs in jobs for x in outs],
        0,
        after=after,
        hold=hold,
        vmem=vmem,
        aliases={1 + k: k for k in range(len(through))},
    )
    passed, found = found[: len(through)], found[len(through) :]
    results = []
    for _, outs in counts:
        results.append(found[:outs])
        found = found[outs:]
    return results + [passed] if through else results


def relay_job(keep, arrived, place):
    rows = keep.shape[0] if place is None else keep.shape[0] // 2
    dims = (rows,) + keep.shape[1:]
    return (
        functools.partial(relay_kernel, [place], [place is None]),
        [keep, arrived],
        [shape(dims), shape(dims, F32)],
    )


def split_job(*terms):
    rows, width = terms[0].shape
    return split_kernel, list(terms), [shape((rows // 2, width), F32)] * 2


def owners_cut_kernel(meta, keep_ref, arrived_ref, mine_ref, high_ref, pair_ref, both_ref):
    size = mine_ref.shape[0]
    mine = 2 * meta[ZHIGH] + meta[PAIR]
    for out, mask in ((mine_ref, 0), (high_ref, 2), (pair_ref, 1), (both_ref, 3)):
        at = pl.ds((mine ^ mask) * size, size)
        out[...] = (keep_ref[at] + arrived_ref[at].astype(F32)).astype(out.dtype)


def owners_cut_job(keep, arrived):
    dims = (keep.shape[0] // 4,) + keep.shape[1:]
    return owners_cut_kernel, [keep, arrived], [shape(dims, F32)] + [shape(dims)] * 3


def row_steps_kernel(meta, mine_ref, high_ref, pair_ref, both_ref, send_ref, own_out, pair_out):
    core = meta[CORE]
    for k, (first, second, out) in enumerate(((mine_ref, high_ref, own_out), (pair_ref, both_ref, pair_out))):
        out[...] = first[core].astype(F32) + second[core].astype(F32)
        send_ref[k] = (first[1 - core].astype(F32) + second[1 - core].astype(F32)).astype(BF16)


def row_steps_job(mine, high, pair, both):
    dims = mine.shape[1:]
    return row_steps_kernel, [mine, high, pair, both], [shape(mine.shape), shape(dims, F32), shape(dims, F32)]


def beside_kernel(meta, mine_ref, other_ref, out_ref):
    size = mine_ref.shape[1]
    mine, other = mine_ref[...], other_ref[...]
    out_ref[:, :size] = jnp.where(meta[CORE] == 0, mine, other)
    out_ref[:, size:] = jnp.where(meta[CORE] == 0, other, mine)


def beside_job(mine, other):
    return beside_kernel, [mine, other], [shape((mine.shape[0], 2 * mine.shape[1]), F32)]


def owned_kernel(meta, mine_ref, other_ref, out_ref):
    out_ref[...] = jnp.where(meta[ZHIGH] == meta[CORE], mine_ref[...], other_ref[...])


def owned_job(mine, other):
    return owned_kernel, [mine, other], [shape(mine.shape, F32)]


def sum_job(a, b):
    return add_kernel, [a, b], [shape(a.shape, a.dtype)]


def doc_norms_kernel(meta, a_ref, b_ref, out_ref):
    lane = lax.broadcasted_iota(jnp.int32, a_ref.shape, 1)
    count = jnp.zeros(a_ref.shape, F32)
    for d in range(DOCS):
        count = jnp.where(lane == d, meta[LENS + d].astype(F32), count)
    norms = (a_ref[...] + b_ref[...]) * (count / TOK_DEV)
    out_ref[...] = norms[0:1, :DOCS].reshape(DOCS)


def add_kernel(meta, a_ref, b_ref, out_ref):
    out_ref[...] = (a_ref[...].astype(F32) + b_ref[...].astype(F32)).astype(out_ref.dtype)


def add(meta, name, a, b, after=()):
    return call(add_kernel, name, meta, [a, b], [shape(a.shape)], 0, after=after)[0]


def head_plan(
    tokens,
    cotangent,
    lengths,
    ln1_gain,
    ln1_bias,
    ln2_gain,
    ln2_bias,
    w_qkv,
    b_qkv,
    w_out_attn,
    b_out_attn,
    w_in,
    b_in,
    w_out,
    b_out,
):
    dp_size = lax.axis_size("dp")
    here = lax.axis_index("blk").astype(jnp.int32)
    row = lax.axis_index("dp").astype(jnp.int32)
    pair, core = here // 2, here % 2
    xbit, z_low, z_high = row & 1, (row >> 1) & 1, row >> 2
    meta = jnp.concatenate([jnp.stack([here, pair, core, 2 * core + pair, xbit, z_low, z_high]), lengths[0]])
    own_x, own_ct = tokens[0], cotangent[0]
    rows, width = own_x.shape
    length = 4 * rows
    heads = HEADS // 4
    assert width == PIECES * 4 * dp_size
    positions = np.arange(length, dtype=np.float32)
    frequency = (10000.0 ** (-(np.arange(HALF, dtype=np.float32) * 2.0) / ROT)).astype(np.float32)
    angle = frequency[:, None] * positions[None, :]
    cosine, sine = jnp.asarray(np.cos(angle)), jnp.asarray(np.sin(angle))

    core_x = flip(own_x, "blk", 0)
    core_ct = flip(own_ct, "blk", 0)
    pair_x = flip(own_x, "blk", 1)

    devices = 4 * dp_size
    axes = ("dp", "blk")
    wt = prepare_weights(meta, w_qkv)
    do_near, do_send, w_rows, bias = attended_grad(meta, own_ct, core_ct, w_out_attn, b_qkv, (wt,))
    projection = (ln1_gain, ln1_bias, wt, bias, cosine, sine)
    do_far = flip(do_send, "blk", 1)
    (
        act,
        hid,
        grad,
        turned,
        scaled,
        b_in_grad,
        branch_sum,
        qkv_own,
        qkv_core,
        normed_own,
        normed_core,
        win_half,
        wout_half,
    ) = hidden_part(
        meta, own_x, core_x, own_ct, core_ct, ln2_gain, ln2_bias, w_in, b_in, w_out, projection, (do_near, do_send)
    )
    early = (do_near, wt, bias, qkv_own, qkv_core, normed_own, normed_core, b_in_grad, branch_sum, w_rows)
    gout_send, gout_keep, pair_again = out_grad(
        meta, act, grad, pair_x, early + (hid, turned, scaled, win_half, wout_half)
    )
    gout_x = flip(gout_send, "dp", 0)
    far_x = flip(pair_again, "blk", 0)
    branch, term_two, gin_send, gin_keep, small_two = in_grad(
        meta, act, hid, turned, scaled, ln2_gain, win_half, wout_half, early + (gout_keep,)
    )
    gin_z = flip(gin_send, "dp", 1)
    keep = (normed_own, normed_core, b_in_grad, branch_sum, w_rows, branch, term_two, small_two)
    qkv_pair, qkv_far, normed_pair, normed_far = project(
        meta, pair_x, far_x, projection, keep + (do_near, qkv_own, qkv_core, gout_keep, gin_keep)
    )
    blocks = (qkv_own, qkv_core, qkv_pair, qkv_far)
    normed = (normed_own, normed_core, normed_pair, normed_far)
    keep = keep + (wt, normed_pair, normed_far)
    near, far, weights, last_weights, do_scaled = attend_forward(
        meta, tuple(range(heads)), blocks, do_near, do_far, keep + (gout_keep, gin_keep)
    )
    arrived = flip(far, "blk", 1)
    keep = keep + (near, gout_keep)
    dq_a, dkv_a = attend_backward(
        meta, tuple(range(heads - 1)), blocks, weights, do_scaled, cosine, sine, keep + (gin_keep, last_weights)
    )
    keep = tuple(k for k in keep if k is not near and k is not w_rows and k is not branch) + (dq_a, dkv_a)
    (gin_send, gin_keep), (gout_send, gout_keep), (own_part, send_part, goa_send, goa_keep) = together(
        meta,
        "steps_one",
        [
            relay_job(gin_keep, gin_z, XBIT),
            relay_job(gout_keep, gout_x, PAIR),
            branch_job(near, arrived, w_rows, branch, own_ct, core_ct),
        ],
        hold=keep + blocks + (last_weights, do_scaled),
    )
    gin_x = flip(gin_send, "dp", 0)
    gout_p = flip(gout_send, "blk", 1)
    goa_z = flip(goa_send, "dp", 1)
    core_part = flip(send_part, "blk", 0)
    dq_b, dkv_b, far_send, far_keep, g_send, g_keep = last_head(
        meta,
        (heads - 1,),
        blocks,
        last_weights,
        do_scaled,
        cosine,
        sine,
        (dq_a, dkv_a),
        wt,
        ln1_gain,
        ln1_bias,
        normed,
        (small_two, branch_sum, b_in_grad),
        devices,
        (term_two, goa_keep, gin_keep, gout_keep, goa_send, gin_send, gout_send),
    )
    dqo, dkv = (dq_a, dq_b), (dkv_a, dkv_b)
    top = devices // 2
    to_owner = [(i, i ^ top) for i in range(devices) if i // top != i % 2]
    owners = [i for i in range(devices) if i // top == i % 2]
    (
        (gin_send, gin_keep),
        (gout_send, gout_keep),
        (goa_send, goa_keep),
        (both_send, near_own),
        (g_send,),
    ) = together(
        meta,
        "steps_two",
        [
            relay_job(gin_keep, gin_x, PAIR),
            relay_job(gout_keep, gout_p, ZLOW),
            relay_job(goa_keep, goa_z, XBIT),
            near_job(dkv, dqo, wt, ln1_gain, term_two, far_send),
        ],
        hold=(far_keep, g_keep),
        through=(g_send,),
    )
    both = flip(both_send, "blk", 0)
    g_x = flip(g_send, "dp", 0)
    gin_p = flip(gin_send, "blk", 1)
    gout_z = flip(gout_send, "dp", 1)
    goa_x = flip(goa_send, "dp", 0)

    (far_sum, near_sum), (gin_send, gin_keep), (gout_send, gout_keep) = together(
        meta,
        "steps_three",
        [
            core_sums_job(far_keep, near_own, both),
            relay_job(gin_keep, gin_p, ZHIGH),
            relay_job(gout_keep, gout_z, None),
        ],
        hold=(g_keep, goa_keep),
    )
    from_pair = flip(far_sum, "blk", 1)
    gin_h = flip(gin_send, "dp", 2)
    gout_o = lax.ppermute(gout_send, axes, to_owner)

    ((layer_out,),) = together(
        meta,
        "layer_out",
        [(layer_out_kernel, [own_x, own_part, core_part, b_out_attn, b_out], [shape(own_x.shape)])],
        (far_sum,),
        (g_keep, goa_keep),
    )
    (g_send, g_keep), (goa_send, goa_keep) = together(
        meta,
        "steps_four",
        [relay_job(g_keep, g_x, ZLOW), relay_job(goa_keep, goa_x, None)],
        (layer_out,),
    )
    g_z = flip(g_send, "dp", 1)
    goa_o = lax.ppermute(goa_send, axes, to_owner)

    (g_mine, *g_sends), (goa_send, goa_keep), (gin_mine, gin_other), (gout_mine, gout_other) = together(
        meta,
        "steps_five",
        [
            owners_cut_job(g_keep, g_z),
            relay_job(goa_keep, goa_o, PAIR),
            split_job(gin_keep, gin_h),
            split_job(gout_keep, gout_o),
        ],
    )
    g_parts = [
        lax.ppermute(g, axes, [(i, i ^ mask) for i in range(devices)])
        for g, mask in zip(g_sends, (top, 2, top + 2))
    ]
    goa_p = flip(goa_send, "blk", 1)

    ((tokens_grad, docs),) = together(
        meta, "input_grad", [last_job(own_x, own_ct, near_sum, from_pair)], (gout_mine,)
    )
    docs_core = flip(docs, "blk", 0)

    (g_send, g_own, g_pair), (docs,), (goa_mine, goa_other), (gin_other, gout_other) = together(
        meta,
        "steps_six",
        [row_steps_job(g_mine, *g_parts), sum_job(docs, docs_core), split_job(goa_keep, goa_p)],
        through=(gin_other, gout_other),
    )
    g_core = flip(g_send, "blk", 0)
    docs_pair = flip(docs, "blk", 1)
    goa_other = flip(goa_other, "blk", 0)
    gin_other = flip(gin_other, "blk", 0)
    gout_other = flip(gout_other, "blk", 0)

    (doc_norms,), (w_out_attn_grad,), (w_in_grad,), (w_out_grad,) = together(
        meta,
        "steps_seven",
        [
            (doc_norms_kernel, [docs, docs_pair], [shape((DOCS,), F32)]),
            owned_job(goa_mine, goa_other),
            beside_job(gin_mine, gin_other),
            owned_job(gout_mine, gout_other),
        ],
    )
    w_qkv_grad, gain_one, shift_one, gain_two, shift_two, b_attn_out, b_qkv_grad, b_in_out, b_ff_out = gather_qkv(
        meta, (g_own, g_pair, g_core), ()
    )
    return (
        layer_out[None],
        tokens_grad[None],
        gain_one,
        shift_one,
        gain_two,
        shift_two,
        w_qkv_grad,
        b_qkv_grad,
        w_out_attn_grad,
        b_attn_out,
        w_in_grad,
        b_in_out,
        w_out_grad,
        b_ff_out,
        doc_norms[None],
    )


def solution(mesh):
    in_specs = (
        P("dp", "blk", None),
        P("dp", "blk", None),
        P("dp", None),
        P(),
        P(),
        P(),
        P(),
        P(),
        P(),
        P(),
        P(),
        P(),
        P(),
        P(),
        P(),
    )
    out_specs = (
        P("dp", "blk", None),
        P("dp", "blk", None),
        P(("dp", "blk")),
        P(("dp", "blk")),
        P(("dp", "blk")),
        P(("dp", "blk")),
        P(("dp", "blk"), None),
        P(("dp", "blk")),
        P(("dp", "blk"), None),
        P(("dp", "blk")),
        P(("dp", "blk"), None),
        P(("dp", "blk")),
        P(("dp", "blk"), None),
        P(("dp", "blk")),
        P("dp", None),
    )
    suits = mesh.shape["blk"] == 4 and HEADS % 4 == 0 and mesh.shape["dp"] == 8
    plan = head_plan if suits else general_plan
    return jax.shard_map(
        plan, mesh=mesh, in_specs=in_specs, out_specs=out_specs, check_vma=False
    )
```

```python
import functools

import jax
import jax.numpy as jnp
import numpy as np
from jax import lax
from jax.experimental import pallas as pl
from jax.experimental.pallas import tpu as pltpu
from jax.sharding import PartitionSpec as P

HEADS = 12
HEAD = 64
ROT = 16
DOCS = 4
TOK_DEV = 512


epsilon = 1e-05


def layer_norm(value, gain, shift):
    mean = jnp.mean(value, axis=-1, keepdims=True)
    centered = value - mean
    variance = jnp.mean(centered * centered, axis=-1, keepdims=True)
    return centered * lax.rsqrt(variance + epsilon) * gain + shift


def rotate(value, cosine, sine):
    half = ROT // 2
    rotary_part = value[..., :ROT]
    first = rotary_part[..., :half]
    second = rotary_part[..., half:]
    turned = jnp.concatenate([-second, first], axis=-1)
    return jnp.concatenate([rotary_part * cosine + turned * sine, value[..., ROT:]], axis=-1)


def document_of(positions, ends):
    return jnp.sum((positions[:, None] >= ends[None, :]).astype(jnp.int32), axis=1)


def inner(left, right):
    return lax.dot_general(
        left, right, (((0,), (0,)), ((), ())), preferred_element_type=jnp.float32
    )


def back_through(grad, weight_matrix):
    return lax.dot_general(
        grad, weight_matrix, (((1,), (1,)), ((), ())), preferred_element_type=jnp.float32
    )


def general_plan(
    tokens,
    cotangent,
    lengths,
    ln1_gain,
    ln1_bias,
    ln2_gain,
    ln2_bias,
    w_qkv,
    b_qkv,
    w_out_attn,
    b_out_attn,
    w_in,
    b_in,
    w_out,
    b_out,
):
    blocks = lax.axis_size("blk")
    block_here = lax.axis_index("blk")
    inputs = tokens[0].astype(jnp.float32)
    rows_here = inputs.shape[0]
    width = inputs.shape[1]
    scale = HEAD ** (-0.5)
    query_positions = block_here * rows_here + jnp.arange(rows_here, dtype=jnp.int32)
    row_lengths = lengths[0]
    ends = jnp.cumsum(row_lengths)
    doc_starts = ends - row_lengths
    query_docs = document_of(query_positions, ends)
    doc_numbers = jnp.arange(DOCS, dtype=jnp.int32)
    member = (query_docs[:, None] == doc_numbers[None, :]).astype(jnp.float32)
    earliest = jnp.sum(jnp.where(doc_numbers == query_docs[0], doc_starts, 0))
    last_query = query_positions[rows_here - 1]
    token_length = jnp.sum(member * row_lengths.astype(jnp.float32)[None, :], axis=1)
    weight = jnp.sqrt(TOK_DEV / token_length)
    half = ROT // 2
    frequency = 10000.0 ** (-(jnp.arange(half, dtype=jnp.float32) * 2.0) / ROT)
    angle = query_positions.astype(jnp.float32)[:, None] * frequency[None, :]
    cosine = jnp.concatenate([jnp.cos(angle), jnp.cos(angle)], axis=-1)[:, None, :]
    sine = jnp.concatenate([jnp.sin(angle), jnp.sin(angle)], axis=-1)[:, None, :]
    gain_one = ln1_gain.astype(jnp.float32)
    shift_one = ln1_bias.astype(jnp.float32)
    gain_two = ln2_gain.astype(jnp.float32)
    shift_two = ln2_bias.astype(jnp.float32)
    normed_one = layer_norm(inputs, gain_one, shift_one).astype(jnp.bfloat16)
    projected = jnp.dot(normed_one, w_qkv, preferred_element_type=jnp.float32) + b_qkv.astype(
        jnp.float32
    )
    query_raw = projected[:, :width].reshape(rows_here, HEADS, HEAD)
    key_raw = projected[:, width : 2 * width].reshape(rows_here, HEADS, HEAD)
    queries = rotate(query_raw, cosine, sine).astype(jnp.bfloat16)
    keys_rotated = rotate(key_raw, cosine, sine).reshape(rows_here, width)
    keys_values = jnp.concatenate([keys_rotated, projected[:, 2 * width :]], axis=1).astype(
        jnp.bfloat16
    )

    def useful(first_row, count):
        return (first_row <= last_query) & (first_row + count > earliest)

    def masked_scores(kv_piece, first_row):
        count = kv_piece.shape[0]
        key_block = kv_piece[:, :width].reshape(count, HEADS, HEAD)
        value_block = kv_piece[:, width:].reshape(count, HEADS, HEAD)
        key_positions = first_row + jnp.arange(count, dtype=jnp.int32)
        key_docs = document_of(key_positions, ends)
        allowed = (query_docs[:, None] == key_docs[None, :]) & (
            key_positions[None, :] <= query_positions[:, None]
        )
        scores = (
            jnp.einsum("qhd,khd->qhk", queries, key_block, preferred_element_type=jnp.float32)
            * scale
        )
        return (jnp.where(allowed[:, None, :], scores, -jnp.inf), key_block, value_block)

    initial = (
        jnp.full((rows_here, HEADS), -1e30, jnp.float32),
        jnp.zeros((rows_here, HEADS), jnp.float32),
        jnp.zeros((rows_here, HEADS, HEAD), jnp.float32),
    )
    kv_piece = lax.all_gather(keys_values, "blk", axis=0, tiled=True)
    first_row = jnp.int32(0)

    def fold_work(state):
        row_max, denominator, accum = state
        scores, key_block, value_block = masked_scores(kv_piece, first_row)
        new_max = jnp.maximum(row_max, jnp.max(scores, axis=-1))
        expo = jnp.exp(scores - new_max[..., None])
        denominator = jnp.sum(expo, axis=-1)
        accum = jnp.einsum(
            "qhk,khd->qhd",
            expo.astype(jnp.bfloat16),
            value_block,
            preferred_element_type=jnp.float32,
        )
        return (new_max, denominator, accum)

    row_max, denominator, accum = lax.cond(
        useful(first_row, kv_piece.shape[0]), fold_work, lambda state: state, initial
    )
    log_total = row_max + jnp.log(denominator)
    attended_full = accum / denominator[..., None]
    attended = attended_full.reshape(rows_here, width).astype(jnp.bfloat16)
    attn_branch = jnp.dot(
        attended, w_out_attn, preferred_element_type=jnp.float32
    ) + b_out_attn.astype(jnp.float32)
    normed_two = layer_norm(inputs, gain_two, shift_two).astype(jnp.bfloat16)
    hidden = jnp.dot(normed_two, w_in, preferred_element_type=jnp.float32) + b_in.astype(
        jnp.float32
    )
    activated = jax.nn.gelu(hidden, approximate=False).astype(jnp.bfloat16)
    mlp_branch = jnp.dot(activated, w_out, preferred_element_type=jnp.float32) + b_out.astype(
        jnp.float32
    )
    layer_out = (inputs + attn_branch + mlp_branch).astype(jnp.bfloat16)
    out_grad = cotangent[0].astype(jnp.float32) * weight[:, None]
    branch_grad = out_grad.astype(jnp.bfloat16)
    branch_bias_grad = jnp.sum(branch_grad.astype(jnp.float32), axis=0)
    w_out_grad = inner(activated, branch_grad)
    activated_grad = back_through(branch_grad, w_out)
    unused, gelu_back = jax.vjp(lambda value: jax.nn.gelu(value, approximate=False), hidden)
    hidden_grad = gelu_back(activated_grad)[0].astype(jnp.bfloat16)
    w_in_grad = inner(normed_two, hidden_grad)
    b_in_grad = jnp.sum(hidden_grad.astype(jnp.float32), axis=0)
    normed_two_grad = back_through(hidden_grad, w_in)
    unused, norm_two_back = jax.vjp(layer_norm, inputs, gain_two, shift_two)
    input_two, gain_two_grad, shift_two_grad = norm_two_back(normed_two_grad)
    w_out_attn_grad = inner(attended, branch_grad)
    attended_grad = (
        back_through(branch_grad, w_out_attn).astype(jnp.bfloat16).reshape(rows_here, HEADS, HEAD)
    )
    delta = jnp.sum(attended_grad.astype(jnp.float32) * attended_full, axis=-1)
    gathered = lax.all_gather(keys_values, "blk", axis=0, tiled=True)

    def pair_terms_of(scores, value_block, grad_side, lse_side, delta_side):
        weights = jnp.exp(scores - lse_side[..., None])
        weight_grad = jnp.einsum(
            "qhd,khd->qhk", grad_side, value_block, preferred_element_type=jnp.float32
        )
        score_grad = (weights * (weight_grad - delta_side[..., None])).astype(jnp.bfloat16)
        return (weights, score_grad)

    def block_back(query_grad, block_index):
        first_row = block_index * rows_here
        kv_piece = lax.dynamic_slice_in_dim(gathered, first_row, rows_here, 0)

        def block_work(query_grad):
            scores, key_block, value_block = masked_scores(kv_piece, first_row)
            weights, score_grad = pair_terms_of(
                scores, value_block, attended_grad, log_total, delta
            )
            query_grad = (
                query_grad
                + jnp.einsum(
                    "qhk,khd->qhd", score_grad, key_block, preferred_element_type=jnp.float32
                )
                * scale
            )
            key_grad = (
                jnp.einsum("qhk,qhd->khd", score_grad, queries, preferred_element_type=jnp.float32)
                * scale
            )
            value_grad = jnp.einsum(
                "qhk,qhd->khd",
                weights.astype(jnp.bfloat16),
                attended_grad,
                preferred_element_type=jnp.float32,
            )
            pair_grad = jnp.concatenate(
                [key_grad.reshape(rows_here, width), value_grad.reshape(rows_here, width)], axis=1
            )
            return (query_grad, pair_grad)

        def skipped(query_grad):
            return (query_grad, jnp.zeros((rows_here, 2 * width), jnp.float32))

        return lax.cond(useful(first_row, rows_here), block_work, skipped, query_grad)

    query_grad, pair_terms = lax.scan(
        block_back,
        jnp.zeros((rows_here, HEADS, HEAD), jnp.float32),
        jnp.arange(blocks, dtype=jnp.int32),
    )
    pair_grads = lax.psum_scatter(
        pair_terms.reshape(blocks * rows_here, 2 * width).astype(jnp.bfloat16),
        "blk",
        scatter_dimension=0,
        tiled=True,
    ).astype(jnp.float32)
    unused, rotate_back = jax.vjp(lambda value: rotate(value, cosine, sine), query_raw)
    query_raw_grad = rotate_back(query_grad)[0].reshape(rows_here, width)
    key_raw_grad = rotate_back(pair_grads[:, :width].reshape(rows_here, HEADS, HEAD))[0].reshape(
        rows_here, width
    )
    projected_grad = jnp.concatenate(
        [query_raw_grad, key_raw_grad, pair_grads[:, width:]], axis=1
    ).astype(jnp.bfloat16)
    w_qkv_grad = inner(normed_one, projected_grad)
    b_qkv_grad = jnp.sum(projected_grad.astype(jnp.float32), axis=0)
    normed_one_grad = back_through(projected_grad, w_qkv)
    unused, norm_one_back = jax.vjp(layer_norm, inputs, gain_one, shift_one)
    input_one, gain_one_grad, shift_one_grad = norm_one_back(normed_one_grad)
    input_grad = out_grad + input_one + input_two
    squares = jnp.sum(input_grad * input_grad, axis=1)
    doc_local = jnp.sum(member * squares[:, None], axis=0)
    doc_norms = lax.psum(doc_local, "blk") * (row_lengths.astype(jnp.float32) / TOK_DEV)
    summed = (
        lax.psum_scatter(gain_one_grad, ("dp", "blk"), scatter_dimension=0, tiled=True),
        lax.psum_scatter(shift_one_grad, ("dp", "blk"), scatter_dimension=0, tiled=True),
        lax.psum_scatter(gain_two_grad, ("dp", "blk"), scatter_dimension=0, tiled=True),
        lax.psum_scatter(shift_two_grad, ("dp", "blk"), scatter_dimension=0, tiled=True),
        lax.psum_scatter(w_qkv_grad, ("dp", "blk"), scatter_dimension=0, tiled=True),
        lax.psum_scatter(b_qkv_grad, ("dp", "blk"), scatter_dimension=0, tiled=True),
        lax.psum_scatter(w_out_attn_grad, ("dp", "blk"), scatter_dimension=0, tiled=True),
        lax.psum_scatter(branch_bias_grad, ("dp", "blk"), scatter_dimension=0, tiled=True),
        lax.psum_scatter(w_in_grad, ("dp", "blk"), scatter_dimension=0, tiled=True),
        lax.psum_scatter(b_in_grad, ("dp", "blk"), scatter_dimension=0, tiled=True),
        lax.psum_scatter(w_out_grad, ("dp", "blk"), scatter_dimension=0, tiled=True),
        lax.psum_scatter(branch_bias_grad, ("dp", "blk"), scatter_dimension=0, tiled=True),
    )
    return (
        layer_out[None],
        input_grad.astype(jnp.bfloat16)[None],
        summed[0],
        summed[1],
        summed[2],
        summed[3],
        summed[4],
        summed[5],
        summed[6],
        summed[7],
        summed[8],
        summed[9],
        summed[10],
        summed[11],
        doc_norms[None],
    )


NT = (((1,), (1,)), ((), ()))
TN = (((0,), (0,)), ((), ()))
NN = (((1,), (0,)), ((), ()))
F32 = jnp.float32
BF16 = jnp.bfloat16
MASKED = -1e30
PEAK = 1.15e9
HALF = ROT // 2
EXTRA = 16
HERE, PAIR, CORE, GROUP, XBIT, ZLOW, ZHIGH, LENS = 0, 1, 2, 3, 4, 5, 6, 7


def mxu(left, right, dims=NN):
    return lax.dot_general(left, right, dims, preferred_element_type=F32)


def exact(left, right):
    return lax.dot_general(
        left, right, NN, precision=lax.Precision.HIGHEST, preferred_element_type=F32
    )


def row_of(ref):
    return ref[...].astype(F32).reshape(1, -1)


def token_weight(meta, pos):
    lens = [meta[LENS + d] for d in range(DOCS)]
    length = jnp.full(pos.shape, lens[DOCS - 1], jnp.int32)
    end = lens[0]
    ends = [end]
    for d in range(1, DOCS - 1):
        end = end + lens[d]
        ends.append(end)
    for d in reversed(range(DOCS - 1)):
        length = jnp.where(pos < ends[d], lens[d], length)
    return jnp.sqrt(TOK_DEV / length.astype(F32))


def doc_bounds(meta, length):
    ends = [meta[LENS]]
    for d in range(1, DOCS - 1):
        ends.append(ends[-1] + meta[LENS + d])
    return [0] + ends, ends + [length]


def column(first, count):
    return first + lax.broadcasted_iota(jnp.int32, (count, 1), 0)


def standard(x):
    mean = jnp.mean(x, axis=-1, keepdims=True)
    centered = x - mean
    variance = jnp.mean(centered * centered, axis=-1, keepdims=True)
    rate = lax.rsqrt(variance + epsilon)
    return centered * rate, rate


def call(kernel, name, meta, operands, outs, cost_us, scratch=(), vmem=6, after=(), hold=(), far=(), aliases={}):
    inside = pl.BlockSpec(memory_space=pltpu.VMEM)
    scalars = pl.BlockSpec(memory_space=pltpu.SMEM)
    used = 1 + len(operands)
    idle = len(after) + len(hold)

    def body(*refs):
        kernel(*refs[:used], *refs[used + idle :])

    return pl.pallas_call(
        body,
        in_specs=[scalars]
        + [pl.BlockSpec(memory_space=pltpu.HBM) if k in far else inside for k in range(len(operands))]
        + [inside] * len(hold)
        + [pl.BlockSpec(memory_space=pl.ANY)] * len(after),
        out_specs=[scalars if o.shape == (1,) else inside for o in outs],
        out_shape=outs,
        scratch_shapes=list(scratch),
        input_output_aliases=aliases,
        compiler_params=pltpu.CompilerParams(vmem_limit_bytes=vmem << 20),
        cost_estimate=cost(cost_us),
        name=name,
    )(meta, *operands, *hold, *after)


def cost(us):
    return pl.CostEstimate(flops=int(us * PEAK), bytes_accessed=0, transcendentals=0)


def shape(dims, dtype=BF16):
    return jax.ShapeDtypeStruct(tuple(dims), dtype)


def all_of(array):
    rank = array.ndim
    return pl.BlockSpec(array.shape, lambda *_: (0,) * rank)


def group_rows(meta, columns, width, part, span):
    first = meta[GROUP] * span
    both = columns(pl.ds(pl.multiple_of(part * width + (first // 128) * 128, 128), 256)).T
    return jnp.where(meta[GROUP] % 2 == 1, both[HEAD : HEAD + span], both[:span])


def by_head(queries, keys, values):
    pieces = []
    for h in range(keys.shape[0] // HEAD):
        head = slice(h * HEAD, (h + 1) * HEAD)
        pieces += [keys[head], values[head]]
    return jnp.concatenate(pieces + [queries], axis=0)


def weights_kernel(meta, w_ref, wt_ref, columns, sems):
    span = wt_ref.shape[0] // 3
    width = wt_ref.shape[1]
    copies = []
    for part in range(3):
        first = meta[GROUP] * span
        place = pl.ds(pl.multiple_of(part * width + (first // 128) * 128, 128), 256)
        copies.append(pltpu.make_async_copy(w_ref.at[:, place], columns.at[part], sems.at[part]))
    for copy in copies:
        copy.start()
    for copy in copies:
        copy.wait()
    wt_ref[...] = by_head(
        *(group_rows(meta, lambda place, part=part: columns[part], width, part, span) for part in range(3))
    )


def prepare_weights(meta, w_qkv):
    width, total = w_qkv.shape
    return call(
        weights_kernel,
        "weights",
        meta,
        [w_qkv],
        [shape((total // 4, width))],
        2,
        scratch=[pltpu.VMEM((3, width, 256), BF16), pltpu.SemaphoreType.DMA((3,))],
        far=(0,),
    )[0]


def queries_keys_values(place, cols, normed, wt_ref, bias, cos_ref, sin_ref, out_ref):
    count = normed.shape[0]
    out = mxu(wt_ref[...], normed, NT) + bias[...]
    at = pl.ds(pl.multiple_of(place, count), count)
    cosine, sine = cos_ref[:, at], sin_ref[:, at]
    heads = out_ref.shape[0] // (3 * HEAD)
    out_ref[:, cols] = out.astype(BF16)
    starts = [2 * HEAD * h for h in range(heads)] + [2 * HEAD * heads + HEAD * h for h in range(heads)]
    for row in starts:
        first, second = out[row : row + HALF], out[row + HALF : row + ROT]
        turned = jnp.concatenate([first * cosine - second * sine, second * cosine + first * sine], axis=0)
        out_ref[row : row + ROT, cols] = turned.astype(BF16)


def project_kernel(meta, pair_x, far_x, gain, shift, wt_ref, bias, cos_ref, sin_ref, qkv_pair, qkv_far, normed_pair, normed_far):
    rows = pair_x.shape[0]
    for j, (x_ref, qkv_ref, normed_ref) in enumerate(((pair_x, qkv_pair, normed_pair), (far_x, qkv_far, normed_far))):
        scaled, _ = standard(x_ref[...].astype(F32))
        normed = (scaled * row_of(gain) + row_of(shift)).astype(BF16)
        normed_ref[...] = normed.T
        place = (meta[HERE] ^ (2 + j)) * rows
        queries_keys_values(place, slice(None), normed, wt_ref, bias, cos_ref, sin_ref, qkv_ref)


def project(meta, pair_x, far_x, projection, hold):
    rows, width = pair_x.shape
    features = projection[2].shape[0]
    return call(
        project_kernel,
        "project",
        meta,
        [pair_x, far_x, *projection],
        [shape((features, rows))] * 2 + [shape((width, rows))] * 2,
        4,
        hold=hold,
    )


def attended_grad_kernel(meta, own_ct, core_ct, w_ref, b_ref, mine_ref, send_ref, rows_ref, bias_ref, row_ref, sem):
    rows = own_ct.shape[0]
    span = mine_ref.shape[0]
    core, pair = meta[CORE], meta[PAIR]
    half = pl.ds(pl.multiple_of(core * 2 * span, 2 * span), 2 * span)
    copy = pltpu.make_async_copy(w_ref.at[half, :], rows_ref, sem)
    copy.start()
    row_ref[...] = row_of(b_ref)
    wide = lambda place: jnp.broadcast_to(row_ref[:, place], (8, 256))
    width = own_ct.shape[1]
    bias_ref[...] = by_head(*(group_rows(meta, wide, width, part, span) for part in range(3)))[:, 0:1]
    copy.wait()
    for b in range(2):
        ct = jnp.where(core == b, own_ct[...], core_ct[...]).astype(F32)
        grad = (ct * token_weight(meta, column((2 * pair + b) * rows, rows))).astype(BF16)
        both = mxu(rows_ref[...], grad, NT).astype(BF16)
        cols = slice(b * rows, (b + 1) * rows)
        mine_ref[:, cols] = jnp.where(pair == 0, both[:span], both[span:])
        send_ref[:, cols] = jnp.where(pair == 0, both[span:], both[:span])


def attended_grad(meta, own_ct, core_ct, w_out_attn, b_qkv, hold):
    rows, width = own_ct.shape
    span = width // 4
    return call(
        attended_grad_kernel,
        "attended_grad",
        meta,
        [own_ct, core_ct, w_out_attn, b_qkv],
        [shape((span, 2 * rows)), shape((span, 2 * rows)), shape((2 * span, width)), shape((3 * span, 1), F32)],
        2,
        scratch=[pltpu.VMEM((1, 3 * width), F32), pltpu.SemaphoreType.DMA],
        hold=hold,
        far=(2,),
    )


def hidden_kernel(
    meta,
    own_x,
    core_x,
    own_ct,
    core_ct,
    gain,
    shift,
    win_ref,
    bin_ref,
    wout_ref,
    gain_one,
    shift_one,
    wt_ref,
    bias,
    cos_ref,
    sin_ref,
    act_ref,
    hid_ref,
    grad_ref,
    turned_ref,
    scaled_ref,
    bin_grad_ref,
    branch_sum_ref,
    qkv_own,
    qkv_core,
    normed_own,
    normed_core,
    win_half,
    wout_half,
    bin_row,
    sems,
):
    rows, width = own_x.shape
    hidden_size = win_ref.shape[1] // 2
    chunk = 256
    base = pl.multiple_of(meta[CORE] * hidden_size, hidden_size)
    copies = [
        pltpu.make_async_copy(win_ref.at[:, pl.ds(base, hidden_size)], win_half, sems.at[0]),
        pltpu.make_async_copy(wout_ref.at[pl.ds(base, hidden_size), :], wout_half, sems.at[1]),
    ]
    for copy in copies:
        copy.start()
    bin_row[...] = row_of(bin_ref)
    branch_sum_ref[...] = jnp.zeros_like(branch_sum_ref)
    inputs = ((own_x, own_ct, qkv_own, normed_own), (core_x, core_ct, qkv_core, normed_core))
    totals = []
    for block, (x_ref, ct_ref, qkv_ref, normed_ref) in enumerate(inputs):
        at = slice(block * rows, (block + 1) * rows)
        place = (meta[HERE] ^ block) * rows
        scaled, _ = standard(x_ref[...].astype(F32))
        scaled_ref[at, :] = scaled
        normed = (scaled * row_of(gain_one) + row_of(shift_one)).astype(BF16)
        normed_ref[...] = normed.T
        queries_keys_values(place, slice(None), normed, wt_ref, bias, cos_ref, sin_ref, qkv_ref)
        normed = (scaled * row_of(gain) + row_of(shift)).astype(BF16)
        turned_ref[:, at] = normed.T
        grad = (ct_ref[...].astype(F32) * token_weight(meta, column(place, rows))).astype(BF16)
        grad_ref[at, :] = grad
        if block == 0:
            branch_sum_ref[0:1, :] = jnp.sum(grad.astype(F32), axis=0, keepdims=True)
        if block == 0:
            for copy in copies:
                copy.wait()
        sums = []
        for j in range(0, hidden_size, chunk):
            cols = slice(j, j + chunk)
            there = pl.ds(pl.multiple_of(base + j, 128), chunk)
            hidden = mxu(normed, win_half[:, cols]) + bin_row[:, there]
            back = mxu(grad, wout_half[cols, :], NT)
            below = 0.5 + 0.5 * lax.erf(hidden * (0.5**0.5))
            bell = jnp.exp(hidden * hidden * -0.5) * 0.3989422804014327
            act_ref[at, cols] = (hidden * below).astype(BF16)
            rounded = (back * (below + hidden * bell)).astype(BF16)
            hid_ref[at, cols] = rounded
            sums.append(jnp.sum(rounded.astype(F32), axis=0, keepdims=True))
        totals.append(jnp.concatenate(sums, axis=1))
    bin_grad_ref[...] = totals[0] + totals[1]


def hidden_part(meta, own_x, core_x, own_ct, core_ct, gain, shift, w_in, b_in, w_out, projection, hold):
    rows, width = own_x.shape
    hidden_size = w_in.shape[1] // 2
    features = projection[2].shape[0]
    outs = [
        shape((2 * rows, hidden_size)),
        shape((2 * rows, hidden_size)),
        shape((2 * rows, width)),
        shape((width, 2 * rows)),
        shape((2 * rows, width), F32),
        shape((1, hidden_size), F32),
        shape((8, width), F32),
        shape((features, rows)),
        shape((features, rows)),
        shape((width, rows)),
        shape((width, rows)),
        shape((width, hidden_size)),
        shape((hidden_size, width)),
    ]
    operands = [own_x, core_x, own_ct, core_ct, gain, shift, w_in, b_in, w_out, *projection]
    return call(
        hidden_kernel,
        "hidden",
        meta,
        operands,
        outs,
        13,
        scratch=[pltpu.VMEM((1, 2 * hidden_size), F32), pltpu.SemaphoreType.DMA((2,))],
        vmem=8,
        hold=hold,
        far=(6, 8),
    )


def out_grad_kernel(meta, act_ref, grad_ref, x_ref, send_ref, keep_ref, again_ref):
    again_ref[...] = x_ref[...]
    quarter = send_ref.shape[0] // 2
    part = quarter // 2
    grad = grad_ref[...]
    for ref, bit in ((send_ref, 1 - meta[XBIT]), (keep_ref, meta[XBIT])):
        for z in range(2):
            there = pl.ds(pl.multiple_of((2 * z + bit) * quarter, quarter), quarter)
            found = mxu(act_ref[:, there], grad, TN).astype(BF16)
            for p in range(2):
                ref[(2 * p + z) * part : (2 * p + z + 1) * part, :] = found[p * part : (p + 1) * part]


def out_grad(meta, act, grad, x, hold):
    half = shape((act.shape[1] // 2, grad.shape[1]))
    return call(out_grad_kernel, "w_out_grad", meta, [act, grad, x], [half, half, shape(x.shape)], 3, hold=hold)


def in_grad_kernel(
    meta, act_ref, hid_ref, turned_ref, scaled_ref, gain, win_ref, wout_ref, branch_ref, term_ref, send_ref, keep_ref, small_ref
):
    width = win_ref.shape[0]
    fine = width // 16
    for ref, bit in ((send_ref, 1 - meta[ZLOW]), (keep_ref, meta[ZLOW])):
        pieces = []
        for xb in range(2):
            for p in range(2):
                for zh in range(2):
                    source = (4 * zh + 2 * bit + xb) * 2 * fine + p * fine
                    pieces.append(turned_ref[pl.ds(pl.multiple_of(source, fine), fine), :])
        ref[...] = mxu(jnp.concatenate(pieces, axis=0), hid_ref[...]).astype(BF16)
    rows = act_ref.shape[0] // 2
    small_ref[...] = jnp.zeros_like(small_ref)
    for block in range(2):
        at = slice(block * rows, (block + 1) * rows)
        branch_ref[at, :] = mxu(act_ref[at, :], wout_ref[...]).astype(BF16)
        normed_grad = mxu(hid_ref[at, :], win_ref[...], NT)
        term_ref[at, :] = (normed_grad * row_of(gain)).astype(BF16)
        small_ref[0:1, :] += jnp.sum(normed_grad * scaled_ref[at, :], axis=0, keepdims=True)
        small_ref[1:2, :] += jnp.sum(normed_grad, axis=0, keepdims=True)


def in_grad(meta, act, hid, turned, scaled, gain, w_in, w_out, hold):
    tokens, hidden_size = act.shape
    width = w_in.shape[0]
    outs = [
        shape((tokens, width)),
        shape((tokens, width)),
        shape((width // 2, hidden_size)),
        shape((width // 2, hidden_size)),
        shape((8, width), F32),
    ]
    return call(
        in_grad_kernel,
        "w_in_grad",
        meta,
        [act, hid, turned, scaled, gain, w_in, w_out],
        outs,
        9,
        hold=hold,
    )


def three(value):
    a = value.astype(BF16).astype(F32)
    rest = value - a
    b = rest.astype(BF16).astype(F32)
    return a, b, rest - b


def placer(meta, blocks):
    here, pair = meta[HERE], meta[PAIR]

    def placed(rows, b):
        low = here % 2 == b % 2
        near = jnp.where(low, blocks[0][rows, :], blocks[1][rows, :])
        far = jnp.where(low, blocks[2][rows, :], blocks[3][rows, :])
        return jnp.where(pair == b // 2, near, far)

    return placed


def beside(runs):
    current, first, second = runs[0]
    for _ in range(first):
        next(current)
    for n, (current, _, second) in enumerate(runs):
        following, total = (runs[n + 1][0], runs[n + 1][1]) if n + 1 < len(runs) else (None, 0)
        done = 0
        for i in range(second):
            next(current)
            while done < (i + 1) * total // second:
                next(following)
                done += 1
        for _ in current:
            raise ValueError("steps")


def tile_rows(v, tile):
    return tile * (v * (v + 1) // 2)


def forward_kernel(
    chosen, meta, b0, b1, b2, b3, do_near, do_far, near_ref, far_ref, p_first, p_last, do_ref, out_ref, ka_ref, vt_ref, s_ref
):
    tile = b0.shape[1]
    length = 4 * tile
    heads = do_near.shape[0] // HEAD
    step = tile // 2
    scale = HEAD ** (-0.5)
    pair = meta[PAIR]
    lows, highs = doc_bounds(meta, length)
    placed = placer(meta, (b0, b1, b2, b3))

    pos = lax.broadcasted_iota(jnp.int32, (EXTRA, length), 1)
    row = lax.broadcasted_iota(jnp.int32, (EXTRA, length), 0)
    inside = jnp.zeros(pos.shape, jnp.bool_)
    for d in range(DOCS):
        inside = inside | ((row == d) & (pos >= lows[d]) & (pos < highs[d]))
    key_rows = jnp.where(inside, 1.0, 0.0).astype(BF16)
    one_rows = jnp.where(row[:, :tile] < 3, 1.0, 0.0).astype(BF16)
    query_rows = jnp.where((row < DOCS) & jnp.logical_not(inside), MASKED, 0.0).astype(BF16)
    fill = jnp.zeros((HEAD - EXTRA, tile), BF16)
    for n, head in enumerate(chosen):
        for b in range(4):
            cols = slice(b * tile, (b + 1) * tile)
            kv = placed(slice(2 * HEAD * head, 2 * HEAD * (head + 1)), b)
            ka_ref[n, cols, :] = jnp.concatenate([kv[:HEAD], key_rows[:, cols], fill], axis=0).T
            vt_ref[n, :, cols] = jnp.concatenate([kv[HEAD:], one_rows], axis=0)
    extra_row = lax.broadcasted_iota(jnp.int32, (EXTRA, tile), 0)
    offset = lax.broadcasted_iota(jnp.int32, (step, tile), 0) - lax.broadcasted_iota(jnp.int32, (step, tile), 1)

    def run(n, v, buf):
        head = chosen[n]
        p_ref, m = (p_last, 0) if n == len(chosen) - 1 else (p_first, n)
        of_head = slice(head * HEAD, (head + 1) * HEAD)
        q_rows = slice(HEAD * (2 * heads + head), HEAD * (2 * heads + head + 1))
        chunks = (v + 1) * tile // step
        first_row = tile_rows(v, tile)
        cols = slice(v * tile, (v + 1) * tile)
        low = lambda k: max(0, k * step - v * tile)
        q_t = placed(q_rows, v) * jnp.asarray(scale, BF16)
        half = slice((v % 2) * tile, (v % 2 + 1) * tile)
        do_t = jnp.where(pair == v // 2, do_near[of_head, half], do_far[of_head, half])
        q_aug = jnp.concatenate([q_t, query_rows[:, cols], fill], axis=0)
        top = jnp.full((1, tile), MASKED, F32)
        for k in range(chunks):
            rows, l = slice(k * step, (k + 1) * step), low(k)
            scores = mxu(ka_ref[n, rows, :], q_aug[:, l:])
            if (k + 1) * step > v * tile:
                scores = jnp.where(offset[:, l:] <= v * tile - k * step, scores, MASKED)
            s_ref[buf, rows, l:] = scores
            peak = jnp.max(scores, axis=0, keepdims=True)
            if l:
                top = jnp.concatenate([top[:, :l], jnp.maximum(top[:, l:], peak)], axis=1)
            else:
                top = jnp.maximum(top, peak)
            yield
        for k in range(chunks):
            rows, l = slice(k * step, (k + 1) * step), low(k)
            to = slice(first_row + k * step, first_row + (k + 1) * step)
            p_ref[m, to, l:] = jnp.exp(s_ref[buf, rows, l:] - top[:, l:]).astype(BF16)
            yield
        lanes = [(g * step, v * tile + (g + 1) * step) for g in range(tile // step)]
        out_all = jnp.concatenate(
            [mxu(vt_ref[n, :, :w], p_ref[m, first_row : first_row + w, l : l + step]) for l, w in lanes], axis=1
        )
        inverse = 1.0 / out_all[HEAD : HEAD + 1]
        out_t = out_all[:HEAD] * inverse
        out_ref[(v // 2) ^ pair, n * HEAD : (n + 1) * HEAD, half] = out_t.astype(BF16)
        do_scaled = (do_t.astype(F32) * inverse).astype(BF16)
        delta = jnp.sum(do_scaled.astype(F32) * out_t, axis=0, keepdims=True)
        a, b, c = three(-delta)
        terms = jnp.where(extra_row == 0, a, jnp.where(extra_row == 1, b, jnp.where(extra_row == 2, c, 0.0)))
        do_ref[n, :, cols] = jnp.concatenate([do_scaled, terms.astype(BF16), fill], axis=0)
        yield

    tiles = length // tile
    beside(
        [
            (run(n, v, v % 2), (v + 1) * tile // step, (v + 1) * tile // step + 1)
            for n in range(len(chosen))
            for v in reversed(range(tiles))
        ]
    )
    near_ref[...] = out_ref[0]
    far_ref[...] = out_ref[1]


def attend_forward(meta, chosen, blocks, do_near, do_far, hold):
    rows = blocks[0].shape[1]
    length = 4 * rows
    count = len(chosen)
    return call(
        functools.partial(forward_kernel, chosen),
        "attend%d" % chosen[0],
        meta,
        [*blocks, do_near, do_far],
        [shape((count * HEAD, 2 * rows))] * 2
        + [shape((c, tile_rows(4, rows), rows)) for c in (count - 1, 1)]
        + [shape((count, 2 * HEAD, length))],
        4 * count,
        hold=hold,
        scratch=[
            pltpu.VMEM((2, count * HEAD, 2 * rows), BF16),
            pltpu.VMEM((count, length, 2 * HEAD), BF16),
            pltpu.VMEM((count, HEAD + EXTRA, length), BF16),
            pltpu.VMEM((2, length, rows), F32),
        ],
        vmem=12,
    )


def backward_kernel(
    chosen, meta, b0, b1, b2, b3, p_ref, do_ref, cos_ref, sin_ref, dq_ref, dkv_ref, kt_ref, va_ref, d_ref, acc_ref
):
    tile = b0.shape[1]
    length = 4 * tile
    heads = b0.shape[0] // (3 * HEAD)
    step = tile // 2
    scale = HEAD ** (-0.5)
    pair = meta[PAIR]
    placed = placer(meta, (b0, b1, b2, b3))
    row = lax.broadcasted_iota(jnp.int32, (EXTRA, tile), 0)
    one_rows = jnp.where(row < 3, 1.0, 0.0).astype(BF16)
    fill = jnp.zeros((HEAD - EXTRA, tile), BF16)
    for n, head in enumerate(chosen):
        for b in range(4):
            cols = slice(b * tile, (b + 1) * tile)
            kv = placed(slice(2 * HEAD * head, 2 * HEAD * (head + 1)), b)
            kt_ref[n, :, cols] = kv[:HEAD]
            va_ref[n, cols, :] = jnp.concatenate([kv[HEAD:], one_rows, fill], axis=0).T
    per_half = 2 * tile
    blank = jnp.zeros((HEAD, tile), F32)

    def run(n, v, buf, widest):
        head = chosen[n]
        q_rows = slice(HEAD * (2 * heads + head), HEAD * (2 * heads + head + 1))
        width = (v + 1) * tile
        chunks = width // step
        first_row = tile_rows(v, tile)
        cols = slice(v * tile, (v + 1) * tile)
        low = lambda k: max(0, k * step - v * tile)
        for k in range(chunks):
            rows, l = slice(k * step, (k + 1) * step), low(k)
            weights = p_ref[n, first_row + k * step : first_row + (k + 1) * step, l:]
            weight_grad = mxu(va_ref[n, rows, :], do_ref[head, :, v * tile + l : (v + 1) * tile])
            d_ref[buf, rows, l:] = (weights.astype(F32) * weight_grad).astype(BF16)
            yield
        q_t = placed(q_rows, v) * jnp.asarray(scale, BF16)
        groups = [(0, v * tile, 0)] if v else []
        groups += [(v * tile + g * step, v * tile + (g + 1) * step, g * step) for g in range(tile // step)]
        for r, s, l in groups:
            value = mxu(do_ref[head, :HEAD, v * tile + l : (v + 1) * tile], p_ref[n, first_row + r : first_row + s, l:], NT)
            key = mxu(q_t[:, l:], d_ref[buf, r:s, l:], NT)
            if widest:
                acc_ref[n, HEAD:, r:s] = value
                acc_ref[n, :HEAD, r:s] = key
            else:
                acc_ref[n, HEAD:, r:s] += value
                acc_ref[n, :HEAD, r:s] += key
            yield
        lanes = [(g * step, v * tile + (g + 1) * step) for g in range(tile // step)]
        dq_t = (
            jnp.concatenate([mxu(kt_ref[n, :, :w], d_ref[buf, :w, l : l + step]) for l, w in lanes], axis=1) * scale
        )
        cosine, sine = cos_ref[:, cols], sin_ref[:, cols]
        first, second = dq_t[:HALF], dq_t[HALF:ROT]
        joined = jnp.concatenate(
            [first * cosine + second * sine, second * cosine - first * sine, dq_t[ROT:], blank], axis=0
        )
        half = slice((v % 2) * tile, (v % 2 + 1) * tile)
        dq_ref[(v // 2) ^ pair, half, n * 2 * HEAD : (n + 1) * 2 * HEAD] = joined.T.astype(BF16)
        yield

    tiles = length // tile
    beside(
        [
            (run(n, v, v % 2, v == tiles - 1), (v + 1) * tile // step, (1 if v else 0) + tile // step + 1)
            for n in range(len(chosen))
            for v in reversed(range(tiles))
        ]
    )
    cosine, sine = cos_ref[...], sin_ref[...]
    for n in range(len(chosen)):
        grads = acc_ref[n]
        first, second = grads[:HALF], grads[HALF:ROT]
        grads = jnp.concatenate(
            [first * cosine + second * sine, second * cosine - first * sine, grads[ROT:]], axis=0
        )
        for h in range(2):
            lanes = slice(n * 2 * HEAD, (n + 1) * 2 * HEAD)
            dkv_ref[h ^ pair, :, lanes] = grads[:, h * per_half : (h + 1) * per_half].T.astype(BF16)


def attend_backward(meta, chosen, blocks, weights, do, cosine, sine, hold):
    rows = blocks[0].shape[1]
    length = 4 * rows
    count = len(chosen)
    return call(
        functools.partial(backward_kernel, chosen),
        "attend_back%d" % chosen[0],
        meta,
        [*blocks, weights, do, cosine, sine],
        [shape((2, 2 * rows, 2 * HEAD * count))] * 2,
        5 * count,
        hold=hold,
        scratch=[
            pltpu.VMEM((count, HEAD, length), BF16),
            pltpu.VMEM((count, length, 2 * HEAD), BF16),
            pltpu.VMEM((2, length, rows), BF16),
            pltpu.VMEM((count, 2 * HEAD, length), F32),
        ],
        vmem=10,
    )


def branch_kernel(meta, mine_ref, theirs_ref, w_ref, branch, own_ct, core_ct, own_ref, send_ref, goa_send, goa_keep):
    pair, core = meta[PAIR], meta[CORE]
    rows = own_ref.shape[0]
    mine, theirs = mine_ref[...], theirs_ref[...]
    six = jnp.concatenate([jnp.where(pair == 0, mine, theirs), jnp.where(pair == 0, theirs, mine)], axis=0)
    own_cols = jnp.where(core == 0, six[:, :rows], six[:, rows:])
    other_cols = jnp.where(core == 0, six[:, rows:], six[:, :rows])
    half = w_ref.shape[0]
    weight = w_ref[...]
    send_ref[...] = (mxu(other_cols, weight, TN) + branch[rows:, :].astype(F32)).astype(BF16)
    own_ref[...] = mxu(own_cols, weight, TN) + branch[:rows, :].astype(F32)
    grads = []
    for j, ct in enumerate((own_ct, core_ct)):
        place = (meta[HERE] ^ j) * rows
        grads.append((ct[...].astype(F32) * token_weight(meta, column(place, rows))).astype(BF16))
    total = mxu(own_cols, grads[0]) + mxu(other_cols, grads[1])
    first, second = total[: half // 2], total[half // 2 :]
    goa_keep[...] = jnp.where(meta[ZLOW] == 0, first, second).astype(BF16)
    goa_send[...] = jnp.where(meta[ZLOW] == 0, second, first).astype(BF16)


def branch_job(mine, arrived, w_rows, branch, own_ct, core_ct):
    rows, width = own_ct.shape
    outs = [shape((rows, width), F32), shape((rows, width))] + [shape((width // 4, width))] * 2
    return branch_kernel, [mine, arrived, w_rows, branch, own_ct, core_ct], outs


def with_queries(wt_ref):
    span = wt_ref.shape[0] // 3
    pieces = [wt_ref[: 2 * span, :]]
    for h in range(span // HEAD):
        head = wt_ref[2 * span + h * HEAD : 2 * span + (h + 1) * HEAD, :]
        pieces += [head, jnp.zeros_like(head)]
    return jnp.concatenate(pieces, axis=0)


def far_kernel(meta, *refs):
    kv, qo = refs[0:2], refs[2:4]
    wt_ref, gain, send_ref, keep_ref = refs[4:]
    core = meta[CORE]
    rows = send_ref.shape[0]
    right = with_queries(wt_ref)
    for out, b in ((send_ref, 1 - core), (keep_ref, core)):
        at = pl.ds(pl.multiple_of(b * rows, rows), rows)
        left = jnp.concatenate([r[1, at, :] for r in kv] + [r[1, at, :] for r in qo], axis=1)
        out[...] = (mxu(left, right) * row_of(gain)).astype(BF16)


PIECES = 24


def weight_kernel(meta, *refs):
    kv, qo = refs[0:2], refs[2:4]
    wt_ref, gain, shift, n0, n1, n2, n3, two_ref, branch_sum, bin_ref = refs[4:14]
    send_ref, keep_ref, vector_ref = refs[14:]
    core = meta[CORE]
    width, rows = n0.shape
    features = wt_ref.shape[0]
    span = features // 3
    devices = 2 * keep_ref.shape[0]
    gain_row, shift_row = row_of(gain), row_of(shift)

    def both(half, b):
        at = pl.ds(pl.multiple_of(b * rows, rows), rows)
        return jnp.concatenate([r[half, at, :] for r in kv] + [r[half, at, :] for r in qo], axis=1)

    near_own, near_core = both(0, core), both(0, 1 - core)
    far_own, far_core = both(1, core), both(1, 1 - core)
    grad = mxu(n0[...], near_own) + mxu(n1[...], near_core) + mxu(n2[...], far_own) + mxu(n3[...], far_core)
    sums = sum(
        jnp.sum(a.astype(F32), axis=0, keepdims=True) for a in (near_own, near_core, far_own, far_core)
    )

    def tight(value):
        queries = [value[:, 2 * span + 2 * HEAD * h : 2 * span + 2 * HEAD * h + HEAD] for h in range(3)]
        return jnp.concatenate([value[:, : 2 * span]] + queries, axis=1)

    grad, sums = tight(grad), tight(sums)
    weights = wt_ref[...].T.astype(F32)
    by_weight = jnp.sum(weights * grad, axis=1, keepdims=True)
    shift_grad = jnp.sum(weights * sums, axis=1, keepdims=True)
    lane = lax.broadcasted_iota(jnp.int32, (width, 128), 1)
    turned = jnp.where(lane == 0, by_weight, jnp.where(lane == 1, shift_grad, 0.0)).T
    shift_grad = turned[1:2, :]
    gain_grad = (turned[0:1, :] - shift_row * shift_grad) / gain_row

    offset = features % 128

    def spread(vectors, place_row, place_col, pieces):
        count = vectors.shape[0]
        index = lambda place: jnp.floor((place.astype(F32) + 0.5) * (1.0 / PIECES)).astype(jnp.int32)
        device = lax.broadcasted_iota(jnp.int32, (devices, vectors.shape[1]), 0)
        owner = index(place_row)
        parts = []
        for p in range(pieces):
            chosen = owner == device * pieces + p
            for c in range(count):
                value = vectors[c : c + 1, :]
                high = value.astype(BF16)
                low = (value - high.astype(F32)).astype(BF16)
                for part in (high, low):
                    parts.append(jnp.where(chosen, part.astype(F32), 0.0))
        within = place_col - PIECES * index(place_col) + offset
        lane = lax.broadcasted_iota(jnp.int32, (vectors.shape[1], 128), 1)
        table = jnp.where(within == lane, 1.0, 0.0).astype(BF16)
        return mxu(jnp.concatenate(parts, axis=0).astype(BF16), table)

    def counted(size):
        return (
            lax.broadcasted_iota(jnp.int32, (1, size), 1),
            lax.broadcasted_iota(jnp.int32, (size, 1), 0),
        )

    def qkv_place(index):
        rest = index - 2 * span
        keys = (1 + (index // HEAD) % 2) * width + (index // (2 * HEAD)) * HEAD
        return meta[GROUP] * span + index % HEAD + jnp.where(rest < 0, keys, (rest // HEAD) * HEAD)

    lanes, sub = counted(width)
    norms = jnp.concatenate(
        [gain_grad, shift_grad, two_ref[0:1, :], two_ref[1:2, :], branch_sum[0:1, :]], axis=0
    )
    lanes_kv, sub_kv = counted(features)
    hidden_size = bin_ref.shape[1]
    lanes_in, sub_in = counted(hidden_size)
    base = core * hidden_size
    row = 0
    for found in (
        spread(norms, lanes, sub, 1),
        spread(sums, qkv_place(lanes_kv), qkv_place(sub_kv), 3),
        spread(bin_ref[...], base + lanes_in, base + sub_in, 4),
    ):
        for k in range(found.shape[0] // devices):
            vector_ref[:, row, :] = found[k * devices : (k + 1) * devices]
            row += 1
    chunk = width // devices
    whole = (features // 128) * 128
    tail = jnp.concatenate([grad[:, whole:], jnp.zeros((width, 128 - offset), F32)], axis=1)
    def piece(d):
        at = slice(d * chunk, (d + 1) * chunk)
        return jnp.concatenate([grad[at, :whole], tail[at] + vector_ref[d]], axis=1)

    for e in range(devices // 2):
        d = (e // 4 % 2) * 16 + (e // 8) * 8 + e % 4
        first, second = piece(d), piece(d + 4)
        keep_ref[e] = jnp.where(meta[XBIT] == 0, first, second)
        send_ref[e] = jnp.where(meta[XBIT] == 0, second, first).astype(BF16)


def near_kernel(meta, *refs):
    kv, qo = refs[0:2], refs[2:4]
    wt_ref, gain, term_two, far_ref, send_ref, own_ref = refs[4:]
    core = meta[CORE]
    rows = own_ref.shape[0]
    right = with_queries(wt_ref)

    def part(b):
        at = pl.ds(pl.multiple_of(b * rows, rows), rows)
        return jnp.concatenate([r[0, at, :] for r in kv] + [r[0, at, :] for r in qo], axis=1)

    gain_row = row_of(gain)
    send_ref[:rows, :] = far_ref[...]
    send_ref[rows:, :] = (mxu(part(1 - core), right) * gain_row + term_two[rows:, :].astype(F32)).astype(BF16)
    own_ref[...] = mxu(part(core), right) * gain_row + term_two[:rows, :].astype(F32)


def last_head_kernel(
    chosen,
    meta,
    b0,
    b1,
    b2,
    b3,
    p_ref,
    do_ref,
    cos_ref,
    sin_ref,
    dq_a,
    dkv_a,
    wt_ref,
    gain,
    shift,
    n0,
    n1,
    n2,
    n3,
    two_ref,
    branch_sum,
    bin_ref,
    dq_ref,
    dkv_ref,
    far_send,
    far_keep,
    g_send,
    g_keep,
    kt_ref,
    va_ref,
    d_ref,
    acc_ref,
    vector_ref,
):
    backward_kernel(
        chosen, meta, b0, b1, b2, b3, p_ref, do_ref, cos_ref, sin_ref, dq_ref, dkv_ref, kt_ref, va_ref, d_ref, acc_ref
    )
    grads = (dkv_a, dkv_ref, dq_a, dq_ref)
    far_kernel(meta, *grads, wt_ref, gain, far_send, far_keep)
    weight_kernel(
        meta, *grads, wt_ref, gain, shift, n0, n1, n2, n3, two_ref, branch_sum, bin_ref, g_send, g_keep, vector_ref
    )


def last_head(meta, chosen, blocks, weights, do, cosine, sine, earlier, wt, gain, shift, normed, vectors, devices, hold):
    rows = blocks[0].shape[1]
    length = 4 * rows
    count = len(chosen)
    width = wt.shape[1]
    lanes = -(-wt.shape[0] // 128) * 128
    chunk = width // devices
    outs = [shape((2, 2 * rows, 2 * HEAD * count))] * 2 + [shape((rows, width))] * 2
    outs += [shape((devices // 2, chunk, lanes)), shape((devices // 2, chunk, lanes), F32)]
    return call(
        functools.partial(last_head_kernel, chosen),
        "last_head",
        meta,
        [*blocks, weights, do, cosine, sine, *earlier, wt, gain, shift, *normed, *vectors],
        outs,
        12,
        hold=hold,
        scratch=[
            pltpu.VMEM((count, HEAD, length), BF16),
            pltpu.VMEM((count, length, 2 * HEAD), BF16),
            pltpu.VMEM((2, length, rows), BF16),
            pltpu.VMEM((count, 2 * HEAD, length), F32),
            pltpu.VMEM((devices, chunk, 128), F32),
        ],
        vmem=14,
    )


def near_job(dkv, dqo, wt, gain, term_two, far):
    rows, width = far.shape
    operands = [*dkv, *dqo, wt, gain, term_two, far]
    return near_kernel, operands, [shape((2 * rows, width)), shape((rows, width), F32)]


def core_sums_kernel(meta, far_ref, near_ref, arrived_ref, far_sum_ref, near_sum_ref):
    rows = far_ref.shape[0]
    far_sum_ref[...] = (far_ref[...].astype(F32) + arrived_ref[:rows, :].astype(F32)).astype(BF16)
    near_sum_ref[...] = near_ref[...] + arrived_ref[rows:, :].astype(F32)


def core_sums_job(far, near, arrived):
    return core_sums_kernel, [far, near, arrived], [shape(far.shape), shape(near.shape, F32)]


def gather_kernel(meta, r0, r2, core_ref, out_ref, *vector_refs):
    heads = HEADS // 4
    span = heads * HEAD
    width = out_ref.shape[1] // 3
    whole = ((3 * span) // 128) * 128
    here = meta[HERE]
    found = [r0[...], core_ref[0].astype(F32), r2[...], core_ref[1].astype(F32)]
    vectors = sum(value[:, whole:] for value in found)
    for s in range(4):
        low = here % 2 == s % 2
        value = jnp.where(
            here // 2 == s // 2, jnp.where(low, found[0], found[1]), jnp.where(low, found[2], found[3])
        )
        group = 2 * (s % 2) + s // 2
        for h in range(heads):
            at = group * span + h * HEAD
            out_ref[:, at : at + HEAD] = value[:, 2 * span + h * HEAD : 2 * span + (h + 1) * HEAD]
            out_ref[:, width + at : width + at + HEAD] = value[:, 2 * HEAD * h : 2 * HEAD * h + HEAD]
            out_ref[:, 2 * width + at : 2 * width + at + HEAD] = value[:, 2 * HEAD * h + HEAD : 2 * HEAD * (h + 1)]
    vectors = pltpu.roll(vectors, 128 - (3 * span) % 128, 1)
    pieces = [
        vectors[2 * k : 2 * k + 1, :PIECES] + vectors[2 * k + 1 : 2 * k + 2, :PIECES]
        for k in range(vectors.shape[0] // 2)
    ]
    again_ref, vector_refs = vector_refs[-1], vector_refs[:-1]
    again_ref[...] = pieces[4].reshape(again_ref.shape)
    k = 0
    for ref in vector_refs:
        count = ref.shape[0] // PIECES
        ref[...] = jnp.concatenate(pieces[k : k + count], axis=1).reshape(ref.shape)
        k += count


def gather_qkv(meta, parts, after):
    rows = parts[0].shape[0]
    outs = [shape((rows, 3 * HEADS * HEAD), F32)]
    outs += [shape((count * PIECES,), F32) for count in (1, 1, 1, 1, 1, 3, 4, 1)]
    return call(gather_kernel, "gather", meta, parts, outs, 0, after=after)


def layer_out_kernel(
    meta, x_ref, ct_ref, own_ref, core_ref, first, second, out_ref, scaled_ref, rate_ref, grad_ref, stamp_ref
):
    stamp_ref[...] = jnp.zeros_like(stamp_ref)
    rows = x_ref.shape[0]
    x = x_ref[...].astype(F32)
    scaled_ref[...], rate_ref[...] = standard(x)
    grad_ref[...] = ct_ref[...].astype(F32) * token_weight(meta, column(meta[HERE] * rows, rows))
    total = x + own_ref[...] + core_ref[...].astype(F32)
    out_ref[...] = (total + (row_of(first) + row_of(second))).astype(BF16)


def last_kernel(meta, scaled_ref, rate_ref, grad_ref, near_ref, pair_ref, tokens_ref, docs_ref):
    rows = scaled_ref.shape[0]
    scaled, rate = scaled_ref[...], rate_ref[...]
    term = near_ref[...] + pair_ref[...].astype(F32)
    back = rate * (
        term
        - jnp.mean(term, axis=-1, keepdims=True)
        - scaled * jnp.mean(term * scaled, axis=-1, keepdims=True)
    )
    pos = column(meta[HERE] * rows, rows)
    grad = grad_ref[...] + back
    tokens_ref[...] = grad.astype(BF16)
    squares = jnp.sum(grad * grad, axis=1, keepdims=True)
    lows, highs = doc_bounds(meta, 4 * rows)
    lane = lax.broadcasted_iota(jnp.int32, (8, 128), 1)
    docs = jnp.zeros((8, 128), F32)
    for d in range(DOCS):
        total = jnp.sum(jnp.where((pos >= lows[d]) & (pos < highs[d]), squares, 0.0), axis=0, keepdims=True)
        docs = jnp.where(lane == d, total, docs)
    docs_ref[...] = docs


def last_job(*operands):
    return last_kernel, list(operands), [shape(operands[0].shape), shape((8, 128), F32)]


def flip(value, axis, bit):
    size = lax.axis_size(axis)
    return lax.ppermute(value, axis, [(i, i ^ (1 << bit)) for i in range(size)])


def relay_kernel(places, finals, meta, *refs):
    count = len(places)
    ins, outs = refs[: 2 * count], refs[2 * count :]
    for k, (place, final) in enumerate(zip(places, finals)):
        keep, arrived = ins[2 * k], ins[2 * k + 1]
        first, second = outs[2 * k], outs[2 * k + 1]
        if final:
            total = keep[...].astype(F32) + arrived[...].astype(F32)
            first[...] = total.astype(first.dtype)
            second[...] = total
        else:
            half = first.shape[0]
            for out, bit in ((first, 1 - meta[place]), (second, meta[place])):
                at = pl.ds(pl.multiple_of(bit * half, half), half)
                out[...] = (keep[at, :].astype(F32) + arrived[at, :].astype(F32)).astype(out.dtype)


def split_kernel(meta, *refs):
    kept_ref, given_ref = refs[-2:]
    total = sum(ref[...].astype(F32) for ref in refs[:-2])
    fine = kept_ref.shape[0]
    kept_ref[...] = jnp.where(meta[CORE] == 0, total[:fine], total[fine:])
    given_ref[...] = jnp.where(meta[CORE] == 0, total[fine:], total[:fine])


def together(meta, name, jobs, after=(), hold=(), vmem=8, through=()):
    counts = [(len(operands), len(outs)) for _, operands, outs in jobs]
    inputs = sum(count for count, _ in counts) + len(through)

    def kernel(meta, *refs):
        first, out = len(through), inputs + len(through)
        for (body, _, _), (ins, outs) in zip(jobs, counts):
            body(meta, *refs[first : first + ins], *refs[out : out + outs])
            first, out = first + ins, out + outs

    found = call(
        kernel,
        name,
        meta,
        list(through) + [x for _, operands, _ in jobs for x in operands],
        [shape(x.shape, x.dtype) for x in through] + [x for _, _, outs in jobs for x in outs],
        0,
        after=after,
        hold=hold,
        vmem=vmem,
        aliases={1 + k: k for k in range(len(through))},
    )
    passed, found = found[: len(through)], found[len(through) :]
    results = []
    for _, outs in counts:
        results.append(found[:outs])
        found = found[outs:]
    return results + [passed] if through else results


def relay_job(keep, arrived, place):
    rows = keep.shape[0] if place is None else keep.shape[0] // 2
    dims = (rows,) + keep.shape[1:]
    return (
        functools.partial(relay_kernel, [place], [place is None]),
        [keep, arrived],
        [shape(dims), shape(dims, F32)],
    )


def split_job(*terms):
    rows, width = terms[0].shape
    return split_kernel, list(terms), [shape((rows // 2, width), F32)] * 2


def owners_cut_kernel(meta, keep_ref, arrived_ref, mine_ref, high_ref, pair_ref, both_ref):
    size = mine_ref.shape[0]
    mine = 2 * meta[ZHIGH] + meta[PAIR]
    for out, mask in ((mine_ref, 0), (high_ref, 2), (pair_ref, 1), (both_ref, 3)):
        at = pl.ds((mine ^ mask) * size, size)
        out[...] = (keep_ref[at] + arrived_ref[at].astype(F32)).astype(out.dtype)


def owners_cut_job(keep, arrived):
    dims = (keep.shape[0] // 4,) + keep.shape[1:]
    return owners_cut_kernel, [keep, arrived], [shape(dims, F32)] + [shape(dims)] * 3


def row_steps_kernel(meta, mine_ref, high_ref, pair_ref, both_ref, send_ref, own_out, pair_out):
    core = meta[CORE]
    for k, (first, second, out) in enumerate(((mine_ref, high_ref, own_out), (pair_ref, both_ref, pair_out))):
        out[...] = first[core].astype(F32) + second[core].astype(F32)
        send_ref[k] = (first[1 - core].astype(F32) + second[1 - core].astype(F32)).astype(BF16)


def row_steps_job(mine, high, pair, both):
    dims = mine.shape[1:]
    return row_steps_kernel, [mine, high, pair, both], [shape(mine.shape), shape(dims, F32), shape(dims, F32)]


def beside_kernel(meta, mine_ref, other_ref, out_ref):
    size = mine_ref.shape[1]
    mine, other = mine_ref[...], other_ref[...]
    out_ref[:, :size] = jnp.where(meta[CORE] == 0, mine, other)
    out_ref[:, size:] = jnp.where(meta[CORE] == 0, other, mine)


def beside_job(mine, other):
    return beside_kernel, [mine, other], [shape((mine.shape[0], 2 * mine.shape[1]), F32)]


def owned_kernel(meta, mine_ref, other_ref, out_ref):
    out_ref[...] = jnp.where(meta[ZHIGH] == meta[CORE], mine_ref[...], other_ref[...])


def owned_job(mine, other):
    return owned_kernel, [mine, other], [shape(mine.shape, F32)]


def sum_job(a, b):
    return add_kernel, [a, b], [shape(a.shape, a.dtype)]


def doc_norms_kernel(meta, a_ref, b_ref, out_ref):
    lane = lax.broadcasted_iota(jnp.int32, a_ref.shape, 1)
    count = jnp.zeros(a_ref.shape, F32)
    for d in range(DOCS):
        count = jnp.where(lane == d, meta[LENS + d].astype(F32), count)
    norms = (a_ref[...] + b_ref[...]) * (count / TOK_DEV)
    out_ref[...] = norms[0:1, :DOCS].reshape(DOCS)


def add_kernel(meta, a_ref, b_ref, out_ref):
    out_ref[...] = (a_ref[...].astype(F32) + b_ref[...].astype(F32)).astype(out_ref.dtype)


def add(meta, name, a, b, after=()):
    return call(add_kernel, name, meta, [a, b], [shape(a.shape)], 0, after=after)[0]


def head_plan(
    tokens,
    cotangent,
    lengths,
    ln1_gain,
    ln1_bias,
    ln2_gain,
    ln2_bias,
    w_qkv,
    b_qkv,
    w_out_attn,
    b_out_attn,
    w_in,
    b_in,
    w_out,
    b_out,
):
    dp_size = lax.axis_size("dp")
    here = lax.axis_index("blk").astype(jnp.int32)
    row = lax.axis_index("dp").astype(jnp.int32)
    pair, core = here // 2, here % 2
    xbit, z_low, z_high = row & 1, (row >> 1) & 1, row >> 2
    meta = jnp.concatenate([jnp.stack([here, pair, core, 2 * core + pair, xbit, z_low, z_high]), lengths[0]])
    own_x, own_ct = tokens[0], cotangent[0]
    rows, width = own_x.shape
    length = 4 * rows
    heads = HEADS // 4
    assert width == PIECES * 4 * dp_size
    positions = np.arange(length, dtype=np.float32)
    frequency = (10000.0 ** (-(np.arange(HALF, dtype=np.float32) * 2.0) / ROT)).astype(np.float32)
    angle = frequency[:, None] * positions[None, :]
    cosine, sine = jnp.asarray(np.cos(angle)), jnp.asarray(np.sin(angle))

    core_x = flip(own_x, "blk", 0)
    core_ct = flip(own_ct, "blk", 0)
    pair_x = flip(own_x, "blk", 1)

    devices = 4 * dp_size
    axes = ("dp", "blk")
    wt = prepare_weights(meta, w_qkv)
    do_near, do_send, w_rows, bias = attended_grad(meta, own_ct, core_ct, w_out_attn, b_qkv, (wt,))
    projection = (ln1_gain, ln1_bias, wt, bias, cosine, sine)
    do_far = flip(do_send, "blk", 1)
    (
        act,
        hid,
        grad,
        turned,
        scaled,
        b_in_grad,
        branch_sum,
        qkv_own,
        qkv_core,
        normed_own,
        normed_core,
        win_half,
        wout_half,
    ) = hidden_part(
        meta, own_x, core_x, own_ct, core_ct, ln2_gain, ln2_bias, w_in, b_in, w_out, projection, (do_near, do_send)
    )
    early = (do_near, wt, bias, qkv_own, qkv_core, normed_own, normed_core, b_in_grad, branch_sum, w_rows)
    gout_send, gout_keep, pair_again = out_grad(
        meta, act, grad, pair_x, early + (hid, turned, scaled, win_half, wout_half)
    )
    gout_x = flip(gout_send, "dp", 0)
    far_x = flip(pair_again, "blk", 0)
    branch, term_two, gin_send, gin_keep, small_two = in_grad(
        meta, act, hid, turned, scaled, ln2_gain, win_half, wout_half, early + (gout_keep,)
    )
    gin_z = flip(gin_send, "dp", 1)
    keep = (normed_own, normed_core, b_in_grad, branch_sum, w_rows, branch, term_two, small_two)
    qkv_pair, qkv_far, normed_pair, normed_far = project(
        meta, pair_x, far_x, projection, keep + (do_near, qkv_own, qkv_core, gout_keep, gin_keep)
    )
    blocks = (qkv_own, qkv_core, qkv_pair, qkv_far)
    normed = (normed_own, normed_core, normed_pair, normed_far)
    keep = keep + (wt, normed_pair, normed_far)
    near, far, weights, last_weights, do_scaled = attend_forward(
        meta, tuple(range(heads)), blocks, do_near, do_far, keep + (gout_keep, gin_keep)
    )
    arrived = flip(far, "blk", 1)
    keep = keep + (near, gout_keep)
    dq_a, dkv_a = attend_backward(
        meta, tuple(range(heads - 1)), blocks, weights, do_scaled, cosine, sine, keep + (gin_keep, last_weights)
    )
    keep = tuple(k for k in keep if k is not near and k is not w_rows and k is not branch) + (dq_a, dkv_a)
    (gin_send, gin_keep), (gout_send, gout_keep), (own_part, send_part, goa_send, goa_keep) = together(
        meta,
        "steps_one",
        [
            relay_job(gin_keep, gin_z, XBIT),
            relay_job(gout_keep, gout_x, PAIR),
            branch_job(near, arrived, w_rows, branch, own_ct, core_ct),
        ],
        hold=keep + blocks + (last_weights, do_scaled),
    )
    gin_x = flip(gin_send, "dp", 0)
    gout_p = flip(gout_send, "blk", 1)
    goa_z = flip(goa_send, "dp", 1)
    core_part = flip(send_part, "blk", 0)
    dq_b, dkv_b, far_send, far_keep, g_send, g_keep = last_head(
        meta,
        (heads - 1,),
        blocks,
        last_weights,
        do_scaled,
        cosine,
        sine,
        (dq_a, dkv_a),
        wt,
        ln1_gain,
        ln1_bias,
        normed,
        (small_two, branch_sum, b_in_grad),
        devices,
        (term_two, goa_keep, gin_keep, gout_keep, goa_send, gin_send, gout_send),
    )
    dqo, dkv = (dq_a, dq_b), (dkv_a, dkv_b)
    top = devices // 2
    to_owner = [(i, i ^ top) for i in range(devices) if i // top != i % 2]
    owners = [i for i in range(devices) if i // top == i % 2]
    (
        (gin_send, gin_keep),
        (gout_send, gout_keep),
        (goa_send, goa_keep),
        (both_send, near_own),
        (g_send,),
    ) = together(
        meta,
        "steps_two",
        [
            relay_job(gin_keep, gin_x, PAIR),
            relay_job(gout_keep, gout_p, ZLOW),
            relay_job(goa_keep, goa_z, XBIT),
            near_job(dkv, dqo, wt, ln1_gain, term_two, far_send),
        ],
        hold=(far_keep, g_keep),
        through=(g_send,),
    )
    both = flip(both_send, "blk", 0)
    g_x = flip(g_send, "dp", 0)
    gin_p = flip(gin_send, "blk", 1)
    gout_z = flip(gout_send, "dp", 1)
    goa_x = flip(goa_send, "dp", 0)

    (far_sum, near_sum), (gin_send, gin_keep), (gout_send, gout_keep) = together(
        meta,
        "steps_three",
        [
            core_sums_job(far_keep, near_own, both),
            relay_job(gin_keep, gin_p, ZHIGH),
            relay_job(gout_keep, gout_z, None),
        ],
        hold=(g_keep, goa_keep),
    )
    from_pair = flip(far_sum, "blk", 1)
    gin_h = flip(gin_send, "dp", 2)
    gout_o = lax.ppermute(gout_send, axes, to_owner)

    ((layer_out, *of_input, stamp),) = together(
        meta,
        "layer_out",
        [
            (
                layer_out_kernel,
                [own_x, own_ct, own_part, core_part, b_out_attn, b_out],
                [shape(own_x.shape)]
                + [shape(d, F32) for d in (own_x.shape, (rows, 1), own_x.shape, (8, 128))],
            )
        ],
        (far_sum,),
        (g_keep, goa_keep),
    )
    (g_send, g_keep), (goa_send, goa_keep) = together(
        meta,
        "steps_four",
        [relay_job(g_keep, g_x, ZLOW), relay_job(goa_keep, goa_x, None)],
        (stamp,),
        tuple(of_input),
    )
    g_z = flip(g_send, "dp", 1)
    goa_o = lax.ppermute(goa_send, axes, to_owner)

    (g_mine, *g_sends), (goa_send, goa_keep), (gin_mine, gin_other), (gout_mine, gout_other) = together(
        meta,
        "steps_five",
        [
            owners_cut_job(g_keep, g_z),
            relay_job(goa_keep, goa_o, PAIR),
            split_job(gin_keep, gin_h),
            split_job(gout_keep, gout_o),
        ],
        hold=tuple(of_input) + (near_sum,),
    )
    g_parts = [
        lax.ppermute(g, axes, [(i, i ^ mask) for i in range(devices)])
        for g, mask in zip(g_sends, (top, 2, top + 2))
    ]
    goa_p = flip(goa_send, "blk", 1)

    ((tokens_grad, docs),) = together(
        meta, "input_grad", [last_job(*of_input, near_sum, from_pair)], (gout_mine,)
    )
    docs_core = flip(docs, "blk", 0)

    (g_send, g_own, g_pair), (docs,), (goa_mine, goa_other), (gin_other, gout_other) = together(
        meta,
        "steps_six",
        [row_steps_job(g_mine, *g_parts), sum_job(docs, docs_core), split_job(goa_keep, goa_p)],
        through=(gin_other, gout_other),
    )
    g_core = flip(g_send, "blk", 0)
    docs_pair = flip(docs, "blk", 1)
    goa_other = flip(goa_other, "blk", 0)
    gin_other = flip(gin_other, "blk", 0)
    gout_other = flip(gout_other, "blk", 0)

    (doc_norms,), (w_out_attn_grad,), (w_in_grad,), (w_out_grad,) = together(
        meta,
        "steps_seven",
        [
            (doc_norms_kernel, [docs, docs_pair], [shape((DOCS,), F32)]),
            owned_job(goa_mine, goa_other),
            beside_job(gin_mine, gin_other),
            owned_job(gout_mine, gout_other),
        ],
    )
    w_qkv_grad, gain_one, shift_one, gain_two, shift_two, b_attn_out, b_qkv_grad, b_in_out, b_ff_out = gather_qkv(
        meta, (g_own, g_pair, g_core), ()
    )
    return (
        layer_out[None],
        tokens_grad[None],
        gain_one,
        shift_one,
        gain_two,
        shift_two,
        w_qkv_grad,
        b_qkv_grad,
        w_out_attn_grad,
        b_attn_out,
        w_in_grad,
        b_in_out,
        w_out_grad,
        b_ff_out,
        doc_norms[None],
    )


def solution(mesh):
    in_specs = (
        P("dp", "blk", None),
        P("dp", "blk", None),
        P("dp", None),
        P(),
        P(),
        P(),
        P(),
        P(),
        P(),
        P(),
        P(),
        P(),
        P(),
        P(),
        P(),
    )
    out_specs = (
        P("dp", "blk", None),
        P("dp", "blk", None),
        P(("dp", "blk")),
        P(("dp", "blk")),
        P(("dp", "blk")),
        P(("dp", "blk")),
        P(("dp", "blk"), None),
        P(("dp", "blk")),
        P(("dp", "blk"), None),
        P(("dp", "blk")),
        P(("dp", "blk"), None),
        P(("dp", "blk")),
        P(("dp", "blk"), None),
        P(("dp", "blk")),
        P("dp", None),
    )
    suits = mesh.shape["blk"] == 4 and HEADS % 4 == 0 and mesh.shape["dp"] == 8
    plan = head_plan if suits else general_plan
    return jax.shard_map(
        plan, mesh=mesh, in_specs=in_specs, out_specs=out_specs, check_vma=False
    )
```
